32 devices in a mesh: rows: 4 (over y, x), seq: 8 (over z, core).
Axes of the slice: x: 2, y: 2, z: 4, core: 2. Of those that a mesh axis runs over, the one named last changes fastest.
Arguments:
- hidden_in: bfloat16 [4, 1024, 1024], P('rows', 'seq'), may hold values from -6 to 6
- clip_lengths: int32 [4, 4], P('rows'), may hold values from 1 to 1021, as said below
- text_lengths: int32 [4, 4], P('rows'), may hold values from 1 to 1021, as said below
- text_states: bfloat16 [4, 1024, 768], P('rows'), may hold values from -6 to 6
- norm_gain: bfloat16 [3, 1024], P(None, ('rows', 'seq')), may hold values from 0.099609375 to 1.8984375
- norm_bias: bfloat16 [3, 1024], P(None, ('rows', 'seq')), may hold values from -2 to 2
- self_qkv: bfloat16 [3, 1024, 1024], P(None, ('rows', 'seq')), may hold values from -0.25 to 0.25
- self_out: bfloat16 [1024, 1024], P(('rows', 'seq')), may hold values from -1.5 to 1.5
- cross_query: bfloat16 [1024, 1024], P(('rows', 'seq')), may hold values from -0.1875 to 0.1875
- cross_kv: bfloat16 [2, 768, 1024], P(None, ('rows', 'seq')), may hold values from -0.21875 to 0.21875
- cross_out: bfloat16 [1024, 1024], P(('rows', 'seq')), may hold values from -0.5 to 0.5
- ffn_in: bfloat16 [1024, 4096], P(('rows', 'seq')), may hold values from -0.1875 to 0.1875
- ffn_out: bfloat16 [4096, 1024], P(('rows', 'seq')), may hold values from -0.09375 to 0.09375
- out_grad: bfloat16 [4, 1024, 1024], P('rows', 'seq'), may hold values from -6 to 6
Outputs:
- block_out: bfloat16 [4, 1024, 1024], P('rows', 'seq')
- input_grad: float32 [4, 1024, 1024], P('rows', 'seq')
- text_grad: float32 [4, 1024, 768], P('rows', 'seq')
- grad_norm_gain: float32 [3, 1024], P(None, ('rows', 'seq'))
- grad_norm_bias: float32 [3, 1024], P(None, ('rows', 'seq'))
- grad_self_qkv: float32 [3, 1024, 1024], P(None, ('rows', 'seq'))
- grad_self_out: float32 [1024, 1024], P(('rows', 'seq'))
- grad_cross_query: float32 [1024, 1024], P(('rows', 'seq'))
- grad_cross_kv: float32 [2, 768, 1024], P(None, ('rows', 'seq'))
- grad_cross_out: float32 [1024, 1024], P(('rows', 'seq'))
- grad_ffn_in: float32 [1024, 4096], P(('rows', 'seq'))
- grad_ffn_out: float32 [4096, 1024], P(('rows', 'seq'))
The draws below stay inside these ranges and needn't reach their ends.
Inputs may be any that keep to these rules, and one draw needn't show every extreme that they name: `clip_lengths`: the 4 lengths of a row sum to 1024; clip c takes the frames right after clips 0 to c - 1. `text_lengths`: the lengths of a row sum to at most 1024; clip c's text takes the slots right after those of clips 0 to c - 1; slots after the sum are padding.
All inputs are finite; a program needn't handle non-finite values.
Results may differ from the reference program's by a relative error of at most 0.03.
Values may be sent and summed in bfloat16 or wider, within the bound.
A program may use at most 256 MiB of HBM per device.

```python
import jax
import jax.numpy as jnp
from jax import lax

ROWS_DEV = 1
D = 1024
HD = 64
FF = 4096
TW = 768
TEXT = 1024
CLIPS = 4
ROWS = 4
LEN = 1024


def long_rows(key):
    picked = jax.random.randint(jax.random.fold_in(key, 11), (ROWS // ROWS_DEV,), 0, ROWS_DEV)
    group_of = jnp.arange(ROWS) // ROWS_DEV
    place_in_group = jnp.arange(ROWS) % ROWS_DEV
    return place_in_group == picked[group_of]


def long_place(key):
    return jax.random.randint(jax.random.fold_in(key, 13), (ROWS,), 0, CLIPS)


def long_layout(key, whole_length):
    place = long_place(key)
    is_long = jnp.arange(CLIPS)[None, :] == place[:, None]
    return jnp.where(is_long, whole_length - CLIPS + 1, 1).astype(jnp.int32)


def draw_clip_lengths(key, part):
    chosen = long_rows(key)
    layout = long_layout(key, LEN)
    key = jax.random.fold_in(key, 3)
    pieces = jax.random.randint(key, (ROWS, CLIPS), 1, 5)
    cut_edges = jnp.cumsum(pieces, axis=1)
    bounds = LEN * cut_edges // cut_edges[:, -1:]
    before = jnp.concatenate([jnp.zeros((ROWS, 1), bounds.dtype), bounds[:, :-1]], axis=1)
    drawn = (bounds - before).astype(jnp.int32)
    return jnp.where(chosen[:, None], layout, drawn).astype(jnp.int32)


def draw_text_lengths(key, part):
    chosen = long_rows(key)
    layout = long_layout(key, TEXT)
    key = jax.random.fold_in(key, 5)
    drawn = jax.random.randint(key, (ROWS, CLIPS), 1, TEXT // CLIPS + 1)
    return jnp.where(chosen[:, None], layout, drawn).astype(jnp.int32)


def levels(key, dims, cuts, smallest, high):
    gain = 1.0
    for axis_at, shards_of in cuts:
        draws = jax.random.uniform(jax.random.fold_in(jax.random.fold_in(key, 6), axis_at), (shards_of,), jnp.float32, smallest / len(cuts), high / len(cuts))
        gain = gain * jnp.repeat(jnp.exp(draws), dims[axis_at] // shards_of).reshape((-1,) + (1,) * (len(dims) - 1 - axis_at))
    return gain


def bell_draw(own_key, extent, width, bound, cuts=(), held_as=jnp.bfloat16):
    level = levels(own_key, extent, cuts, -0.22, 0.18) if cuts else 1.0
    drawn = jax.random.normal(own_key, extent, jnp.float32) * width * level
    return jnp.minimum(jnp.maximum(drawn, -bound), bound).astype(held_as)


def setup_inputs(seed: int = 0) -> dict:
    splits = jax.random.split(jax.random.key(seed), 15)
    return {
        "hidden_in": bell_draw(splits[0], (ROWS, LEN, D), 1.0, 6.0, ((0, 4), (1, 8))),
        "clip_lengths": draw_clip_lengths(jax.random.fold_in(splits[14], 71), 0),
        "text_lengths": draw_text_lengths(jax.random.fold_in(splits[14], 71), 0),
        "text_states": bell_draw(splits[3], (ROWS, TEXT, TW), 1.0, 6.0, ((0, 4),)),
        "norm_gain": jnp.clip(1.0 + 0.18 * jax.random.normal(splits[4], (3, D), jnp.float32), 0.099609375, 1.8984375).astype(jnp.bfloat16),
        "norm_bias": bell_draw(splits[5], (3, D), 0.3, 2.0, ((1, 32),)),
        "self_qkv": bell_draw(splits[6], (3, D, D), (D // 2) ** -0.5, 0.25, ((1, 32),)),
        "self_out": bell_draw(splits[7], (D, D), (D // 64) ** -0.5, 1.5, ((0, 32),)),
        "cross_query": bell_draw(splits[8], (D, D), D ** -0.5, 0.1875, ((0, 32),)),
        "cross_kv": bell_draw(splits[9], (2, TW, D), TW ** -0.5, 0.21875, ((1, 32),)),
        "cross_out": bell_draw(splits[10], (D, D), (D // 8) ** -0.5, 0.5, ((0, 32),)),
        "ffn_in": bell_draw(splits[11], (D, FF), D ** -0.5, 0.1875, ((0, 32),)),
        "ffn_out": bell_draw(splits[12], (FF, D), FF ** -0.5, 0.09375, ((0, 32),)),
        "out_grad": bell_draw(splits[13], (ROWS, LEN, D), 1.0, 6.0, ((0, 4), (1, 8))),
    }


highest = lax.Precision.HIGHEST
epsilon = 1e-05
masked_score = -1e+30

@jax.custom_vjp
def low(v):
    return lax.optimization_barrier(v.astype(jnp.bfloat16)).astype(jnp.float32)

@jax.custom_vjp
def low_back(v):
    return v

def low_keep(v):
    return (low(v), None)

def low_pass(kept, grad):
    return (grad,)

def back_keep(v):
    return (v, None)

def back_low(kept, grad):
    return (low(grad),)
low.defvjp(low_keep, low_pass)
low_back.defvjp(back_keep, back_low)

def layer_norm(values, gains, biases):
    average = lax.optimization_barrier(jnp.mean(values, axis=-1, keepdims=True))
    centred = values - average
    variance = lax.optimization_barrier(jnp.mean(centred * centred, axis=-1, keepdims=True))
    return centred * lax.rsqrt(variance + epsilon) * gains + biases

def product(left, right):
    return jnp.matmul(left, right, precision=highest)

def split_heads(values):
    return values.reshape(values.shape[0], values.shape[1] // HD, HD).transpose(1, 0, 2)

def attend(queries, keys, values, allowed):

    @jax.checkpoint
    def one_head(triple):
        query_head, key_head, value_head = triple
        scores = low_back(product(query_head, key_head.T) * HD ** (-0.5))
        scores = jnp.where(allowed, scores, masked_score)
        largest = lax.optimization_barrier(jnp.max(scores, axis=-1, keepdims=True))
        weights = jnp.where(allowed, jnp.exp(scores - largest), 0.0)
        probability = weights / lax.optimization_barrier(jnp.sum(weights, axis=-1, keepdims=True))
        return product(low(probability), value_head)
    merged = lax.map(one_head, (split_heads(queries), split_heads(keys), split_heads(values)))
    return merged.transpose(1, 0, 2).reshape(queries.shape)

def row_forward(params, hidden_row, text_row, clip_row, slot_low, slot_high):
    gains, biases, w_qkv, w_self, w_query, w_text, w_cross, w_up, w_down = params
    frame_index = jnp.arange(hidden_row.shape[0], dtype=jnp.int32)
    causal = (frame_index[:, None] >= frame_index[None, :]) & (clip_row[:, None] == clip_row[None, :])
    normed = low(layer_norm(hidden_row, gains[0], biases[0]))
    queries = low_back(low(product(normed, w_qkv[0])))
    keys = low_back(low(product(normed, w_qkv[1])))
    values = low_back(low(product(normed, w_qkv[2])))
    attended = low_back(low(attend(queries, keys, values, causal)))
    after_self = hidden_row + low_back(product(attended, w_self))
    normed_two = low(layer_norm(after_self, gains[1], biases[1]))
    cross_queries = low_back(low(product(normed_two, w_query)))
    text_keys = low(product(text_row, w_text[0]))
    text_values = low(product(text_row, w_text[1]))
    slot_index = jnp.arange(text_row.shape[0], dtype=jnp.int32)
    readable = (slot_index[None, :] >= slot_low[:, None]) & (slot_index[None, :] < slot_high[:, None])
    crossed = low_back(low(attend(cross_queries, text_keys, text_values, readable)))
    after_cross = after_self + low_back(product(crossed, w_cross))
    normed_three = low(layer_norm(after_cross, gains[2], biases[2]))
    hidden_up = low_back(product(normed_three, w_up))
    activated = low(jax.nn.gelu(hidden_up, approximate=False))
    return after_cross + low_back(product(activated, w_down))

def reference(hidden_in, clip_lengths, text_lengths, text_states, norm_gain, norm_bias, self_qkv, self_out, cross_query, cross_kv, cross_out, ffn_in, ffn_out, out_grad):
    clip_ends = jnp.cumsum(clip_lengths, axis=1).astype(jnp.int32)
    frame_index = jnp.arange(LEN, dtype=jnp.int32)
    clip_ids = lax.optimization_barrier(jnp.sum((frame_index[None, :, None] >= clip_ends[:, None, :]).astype(jnp.int32), axis=2)).astype(jnp.int32)
    text_ends = jnp.cumsum(text_lengths, axis=1).astype(jnp.int32)
    text_starts = (text_ends - text_lengths).astype(jnp.int32)
    chosen = clip_ids[:, :, None] == jnp.arange(CLIPS, dtype=jnp.int32)[None, None, :]
    slot_low = lax.optimization_barrier(jnp.sum(jnp.where(chosen, text_starts[:, None, :], 0), axis=2)).astype(jnp.int32)
    slot_high = lax.optimization_barrier(jnp.sum(jnp.where(chosen, text_ends[:, None, :], 0), axis=2)).astype(jnp.int32)
    params = tuple((member.astype(jnp.float32) for member in (norm_gain, norm_bias, self_qkv, self_out, cross_query, cross_kv, cross_out, ffn_in, ffn_out)))

    def whole_layer(params, hidden, texts):

        @jax.checkpoint
        def one_row(bundle):
            hidden_row, text_row, clip_row, low_row, high_row = bundle
            return row_forward(params, hidden_row, text_row, clip_row, low_row, high_row)
        return lax.map(one_row, (hidden, texts, clip_ids, slot_low, slot_high))
    result, pull_back = jax.vjp(whole_layer, params, hidden_in.astype(jnp.float32), text_states.astype(jnp.float32))
    grad_params, grad_hidden, grad_text = pull_back(out_grad.astype(jnp.float32))
    return (result.astype(jnp.bfloat16), grad_hidden, grad_text, grad_params[0], grad_params[1], grad_params[2], grad_params[3], grad_params[4], grad_params[5], grad_params[6], grad_params[7], grad_params[8])
```

```python
import functools
import types

import jax
import jax.numpy as jnp
from jax import lax
from jax.experimental import pallas as pl
from jax.experimental.pallas import tpu as pltpu
from jax.sharding import PartitionSpec as P

HD = 64


epsilon = 1e-05
masked_score = -1e30
group_heads = 4
highest = lax.Precision.HIGHEST


def layer_norm(values, gains, biases):
    average = jnp.mean(values, axis=-1, keepdims=True)
    centred = values - average
    variance = jnp.mean(centred * centred, axis=-1, keepdims=True)
    return centred * lax.rsqrt(variance + epsilon) * gains + biases


def gelu_exact(values):
    return jax.nn.gelu(values, approximate=False)


def project(left, weight):
    return jnp.einsum("rtd,de->rte", left, weight, preferred_element_type=jnp.float32)


def weight_term(left, right):
    return jnp.einsum("rtd,rte->de", left, right, preferred_element_type=jnp.float32)


def back_project(gradient, weight):
    return jnp.einsum("rte,de->rtd", gradient, weight, preferred_element_type=jnp.float32)


def exact_weight_term(left, right):
    return jnp.einsum(
        "rtd,rte->de", left, right, precision=highest, preferred_element_type=jnp.float32
    )


def exact_back_project(gradient, weight):
    return jnp.einsum(
        "rte,de->rtd", gradient, weight, precision=highest, preferred_element_type=jnp.float32
    )


def split_heads(values):
    return values.reshape(values.shape[0], values.shape[1], values.shape[2] // HD, HD)


def clip_of(positions, clip_ends):
    return jnp.sum((positions[None, :, None] >= clip_ends[:, None, :]).astype(jnp.int32), axis=2)


def pair_mask(query_pos, query_clip, key_pos, key_clip):
    causal = query_pos[None, :, None] >= key_pos[None, None, :]
    return (causal & (query_clip[:, :, None] == key_clip[:, None, :]))[:, None]


def blocks_of(arrived, frame_span):
    block_count = arrived.shape[1] // frame_span
    shaped = arrived.reshape((arrived.shape[0], block_count, frame_span) + arrived.shape[2:])
    return jnp.moveaxis(shaped, 1, 0)


def block_fold(visit_block, frame_span, carried, arrived):
    block_count = arrived.shape[1] // frame_span
    starts = frame_span * jnp.arange(block_count, dtype=jnp.int32)

    def scan_step(state, block_pair):
        return (visit_block(state, block_pair[0], block_pair[1]), None)

    carried, unused = lax.scan(scan_step, carried, (blocks_of(arrived, frame_span), starts))
    return carried


def head_dot(gradient, output):
    summed = jnp.sum(split_heads(gradient).astype(jnp.float32) * split_heads(output), axis=3)
    return jnp.swapaxes(summed, 1, 2)


def text_project(texts, w_text):
    return jnp.concatenate([project(texts, w_text[0]), project(texts, w_text[1])], axis=2).astype(
        jnp.bfloat16
    )


def self_forward(queries, key_value, clip_ends, clip_ids, frames):
    row_count, frame_span, model_width = queries.shape
    head_count = model_width // HD
    score_scale = HD ** (-0.5)
    query_heads = split_heads(queries)
    last_frame = frames[frame_span - 1]

    def visit_block(state, key_block, first_key):
        key_pos = first_key + jnp.arange(frame_span, dtype=jnp.int32)

        def accumulate(carried):
            running_max, running_sum, output_sum = carried
            key_heads = split_heads(key_block[:, :, :model_width])
            value_heads = split_heads(key_block[:, :, model_width:])
            allowed = pair_mask(frames, clip_ids, key_pos, clip_of(key_pos, clip_ends))
            scores = (
                jnp.einsum(
                    "rqhd,rkhd->rhqk", query_heads, key_heads, preferred_element_type=jnp.float32
                )
                * score_scale
            )
            scores = jnp.where(allowed, scores, masked_score)
            new_max = jnp.maximum(running_max, jnp.max(scores, axis=3))
            weights = jnp.where(allowed, jnp.exp(scores - new_max[..., None]), 0.0)
            shrink = jnp.exp(running_max - new_max)
            running_sum = running_sum * shrink + jnp.sum(weights, axis=3)
            output_sum = output_sum * shrink[..., None] + jnp.einsum(
                "rhqk,rkhd->rhqd",
                weights.astype(jnp.bfloat16),
                value_heads,
                preferred_element_type=jnp.float32,
            )
            return (new_max, running_sum, output_sum)

        return lax.cond(first_key > last_frame, lambda carried: carried, accumulate, state)

    initial = (
        jnp.full((row_count, head_count, frame_span), masked_score, jnp.float32),
        jnp.zeros((row_count, head_count, frame_span), jnp.float32),
        jnp.zeros((row_count, head_count, frame_span, HD), jnp.float32),
    )
    running_max, running_sum, output_sum = block_fold(
        visit_block, frame_span, initial, lax.all_gather(key_value, "seq", axis=1, tiled=True)
    )
    attended = output_sum / running_sum[..., None]
    return (
        jnp.swapaxes(attended, 1, 2).reshape(row_count, frame_span, model_width),
        running_max + jnp.log(running_sum),
    )


def self_query_grad(queries, key_value, clip_ends, clip_ids, frames, log_norm, delta_sum, d_attn):
    row_count, frame_span, model_width = queries.shape
    head_count = model_width // HD
    score_scale = HD ** (-0.5)
    query_heads = split_heads(queries)
    grad_heads = split_heads(d_attn)
    last_frame = frames[frame_span - 1]

    def visit_block(state, key_block, first_key):
        key_pos = first_key + jnp.arange(frame_span, dtype=jnp.int32)

        def accumulate(carried):
            key_heads = split_heads(key_block[:, :, :model_width])
            value_heads = split_heads(key_block[:, :, model_width:])
            allowed = pair_mask(frames, clip_ids, key_pos, clip_of(key_pos, clip_ends))
            scores = (
                jnp.einsum(
                    "rqhd,rkhd->rhqk", query_heads, key_heads, preferred_element_type=jnp.float32
                )
                * score_scale
            )
            probability = jnp.where(allowed, jnp.exp(scores - log_norm[..., None]), 0.0)
            d_prob = jnp.einsum(
                "rqhd,rkhd->rhqk", grad_heads, value_heads, preferred_element_type=jnp.float32
            )
            d_score = (probability * (d_prob - delta_sum[..., None])).astype(jnp.bfloat16)
            return carried + jnp.einsum(
                "rhqk,rkhd->rhqd", d_score, key_heads, preferred_element_type=jnp.float32
            )

        return lax.cond(first_key > last_frame, lambda carried: carried, accumulate, state)

    initial = jnp.zeros((row_count, head_count, frame_span, HD), jnp.float32)
    d_query = block_fold(
        visit_block, frame_span, initial, lax.all_gather(key_value, "seq", axis=1, tiled=True)
    )
    d_query = jnp.swapaxes(d_query, 1, 2).reshape(row_count, frame_span, model_width) * score_scale
    return d_query.astype(jnp.bfloat16)


def self_key_grad(query_grad, key_value, clip_ends, clip_ids, frames, gathered_stats):
    row_count, frame_span, double_width = key_value.shape
    model_width = double_width // 2
    head_count = model_width // HD
    score_scale = HD ** (-0.5)
    key_heads = split_heads(key_value[:, :, :model_width])
    value_heads = split_heads(key_value[:, :, model_width:])
    all_norm, all_delta = gathered_stats
    first_own = frames[0]

    def visit_block(state, query_block, first_query):
        query_pos = first_query + jnp.arange(frame_span, dtype=jnp.int32)

        def accumulate(carried):
            d_key, d_value = carried
            query_heads = split_heads(query_block[:, :, :model_width])
            grad_heads = split_heads(query_block[:, :, model_width:])
            log_norm = jnp.swapaxes(
                lax.dynamic_slice_in_dim(all_norm, first_query, frame_span, 1), 1, 2
            )
            delta_sum = jnp.swapaxes(
                lax.dynamic_slice_in_dim(all_delta, first_query, frame_span, 1), 1, 2
            )
            allowed = pair_mask(query_pos, clip_of(query_pos, clip_ends), frames, clip_ids)
            scores = (
                jnp.einsum(
                    "rqhd,rkhd->rhqk", query_heads, key_heads, preferred_element_type=jnp.float32
                )
                * score_scale
            )
            probability = jnp.where(allowed, jnp.exp(scores - log_norm[..., None]), 0.0)
            d_value = d_value + jnp.einsum(
                "rhqk,rqhd->rhkd",
                probability.astype(jnp.bfloat16),
                grad_heads,
                preferred_element_type=jnp.float32,
            )
            d_prob = jnp.einsum(
                "rqhd,rkhd->rhqk", grad_heads, value_heads, preferred_element_type=jnp.float32
            )
            d_score = (probability * (d_prob - delta_sum[..., None])).astype(jnp.bfloat16)
            d_key = d_key + jnp.einsum(
                "rhqk,rqhd->rhkd", d_score, query_heads, preferred_element_type=jnp.float32
            )
            return (d_key, d_value)

        return lax.cond(
            first_query + frame_span - 1 < first_own, lambda carried: carried, accumulate, state
        )

    zeros_heads = jnp.zeros((row_count, head_count, frame_span, HD), jnp.float32)
    d_key, d_value = block_fold(
        visit_block,
        frame_span,
        (zeros_heads, zeros_heads),
        lax.all_gather(query_grad, "seq", axis=1, tiled=True),
    )
    d_key = jnp.swapaxes(d_key, 1, 2).reshape(row_count, frame_span, model_width) * score_scale
    d_value = jnp.swapaxes(d_value, 1, 2).reshape(row_count, frame_span, model_width)
    return (d_key.astype(jnp.bfloat16), d_value.astype(jnp.bfloat16))


def cross_forward(queries, text_kv, readable):
    row_count, frame_span, model_width = queries.shape
    group_width = group_heads * HD
    score_scale = HD ** (-0.5)
    outputs = []
    log_norms = []
    for group_index in range(model_width // group_width):
        lower_edge = group_index * group_width
        query_heads = split_heads(queries[:, :, lower_edge : lower_edge + group_width])
        key_heads = split_heads(text_kv[:, :, lower_edge : lower_edge + group_width])
        value_heads = split_heads(
            text_kv[:, :, model_width + lower_edge : model_width + lower_edge + group_width]
        )
        scores = (
            jnp.einsum(
                "rqhd,rkhd->rhqk", query_heads, key_heads, preferred_element_type=jnp.float32
            )
            * score_scale
        )
        scores = jnp.where(readable, scores, masked_score)
        largest = jnp.max(scores, axis=3)
        weights = jnp.where(readable, jnp.exp(scores - largest[..., None]), 0.0)
        totals = jnp.sum(weights, axis=3)
        probability = (weights / totals[..., None]).astype(jnp.bfloat16)
        attended = jnp.einsum(
            "rhqk,rkhd->rqhd", probability, value_heads, preferred_element_type=jnp.float32
        )
        outputs.append(attended.reshape(row_count, frame_span, group_width))
        log_norms.append(largest + jnp.log(totals))
    return (jnp.concatenate(outputs, axis=2), jnp.concatenate(log_norms, axis=1))


def cross_backward(queries, text_kv, readable, log_norm, d_cross, delta_sum):
    row_count, frame_span, model_width = queries.shape
    slot_count = text_kv.shape[1]
    group_width = group_heads * HD
    score_scale = HD ** (-0.5)
    d_queries = []
    d_keys = []
    d_values = []
    for group_index in range(model_width // group_width):
        lower_edge = group_index * group_width
        head_edge = group_index * group_heads
        query_heads = split_heads(queries[:, :, lower_edge : lower_edge + group_width])
        grad_heads = split_heads(d_cross[:, :, lower_edge : lower_edge + group_width])
        key_heads = split_heads(text_kv[:, :, lower_edge : lower_edge + group_width])
        value_heads = split_heads(
            text_kv[:, :, model_width + lower_edge : model_width + lower_edge + group_width]
        )
        group_norm = log_norm[:, head_edge : head_edge + group_heads]
        group_delta = delta_sum[:, head_edge : head_edge + group_heads]
        scores = (
            jnp.einsum(
                "rqhd,rkhd->rhqk", query_heads, key_heads, preferred_element_type=jnp.float32
            )
            * score_scale
        )
        probability = jnp.where(readable, jnp.exp(scores - group_norm[..., None]), 0.0)
        d_value = jnp.einsum(
            "rhqk,rqhd->rkhd",
            probability.astype(jnp.bfloat16),
            grad_heads,
            preferred_element_type=jnp.float32,
        )
        d_values.append(d_value.reshape(row_count, slot_count, group_width))
        d_prob = jnp.einsum(
            "rqhd,rkhd->rhqk", grad_heads, value_heads, preferred_element_type=jnp.float32
        )
        d_score = (probability * (d_prob - group_delta[..., None])).astype(jnp.bfloat16)
        d_query = jnp.einsum(
            "rhqk,rkhd->rqhd", d_score, key_heads, preferred_element_type=jnp.float32
        )
        d_queries.append(d_query.reshape(row_count, frame_span, group_width) * score_scale)
        d_key = jnp.einsum(
            "rhqk,rqhd->rkhd", d_score, query_heads, preferred_element_type=jnp.float32
        )
        d_keys.append(d_key.reshape(row_count, slot_count, group_width) * score_scale)
    return (jnp.concatenate(d_queries, axis=2), jnp.concatenate(d_keys + d_values, axis=2))


def shards(
    hidden_in,
    clip_lengths,
    text_lengths,
    text_states,
    norm_gain,
    norm_bias,
    self_qkv,
    self_out,
    cross_query,
    cross_kv,
    cross_out,
    ffn_in,
    ffn_out,
    out_grad,
):
    gathered = (
        lax.all_gather(norm_gain, ("rows", "seq"), axis=1, tiled=True),
        lax.all_gather(norm_bias, ("rows", "seq"), axis=1, tiled=True),
        lax.all_gather(self_qkv, ("rows", "seq"), axis=1, tiled=True),
        lax.all_gather(self_out, ("rows", "seq"), axis=0, tiled=True),
        lax.all_gather(cross_query, ("rows", "seq"), axis=0, tiled=True),
        lax.all_gather(cross_kv, ("rows", "seq"), axis=1, tiled=True),
        lax.all_gather(cross_out, ("rows", "seq"), axis=0, tiled=True),
        lax.all_gather(ffn_in, ("rows", "seq"), axis=0, tiled=True),
        lax.all_gather(ffn_out, ("rows", "seq"), axis=0, tiled=True),
    )
    gains_all, biases_all, w_qkv, w_self, w_query, w_text, w_cross, w_up, w_down = gathered
    gains = gains_all.astype(jnp.float32)
    biases = biases_all.astype(jnp.float32)
    row_count, frame_span, model_width = hidden_in.shape
    seq_index = lax.axis_index("seq")
    frames = seq_index * frame_span + jnp.arange(frame_span, dtype=jnp.int32)
    clip_ends = jnp.cumsum(clip_lengths, axis=1)
    clip_ids = clip_of(frames, clip_ends)
    text_ends = jnp.cumsum(text_lengths, axis=1)
    text_starts = text_ends - text_lengths
    chosen = (
        clip_ids[:, :, None] == jnp.arange(clip_lengths.shape[1], dtype=jnp.int32)[None, None, :]
    )
    slot_low = jnp.sum(jnp.where(chosen, text_starts[:, None, :], 0), axis=2)
    slot_high = jnp.sum(jnp.where(chosen, text_ends[:, None, :], 0), axis=2)
    slot_index = jnp.arange(text_states.shape[1], dtype=jnp.int32)
    readable = (
        (slot_index[None, None, :] >= slot_low[:, :, None])
        & (slot_index[None, None, :] < slot_high[:, :, None])
    )[:, None]
    slot_share = text_states.shape[1] // lax.axis_size("seq")
    own_text = lax.dynamic_slice_in_dim(text_states, seq_index * slot_share, slot_share, 1)
    resid = hidden_in.astype(jnp.float32)
    normed_full, pull_first = jax.vjp(layer_norm, resid, gains[0], biases[0])
    normed = normed_full.astype(jnp.bfloat16)
    queries = project(normed, w_qkv[0]).astype(jnp.bfloat16)
    keys_low = project(normed, w_qkv[1]).astype(jnp.bfloat16)
    values_low = project(normed, w_qkv[2]).astype(jnp.bfloat16)
    key_value = jnp.concatenate([keys_low, values_low], axis=2)
    self_full, self_norm = self_forward(queries, key_value, clip_ends, clip_ids, frames)
    attended = self_full.astype(jnp.bfloat16)
    after_self = resid + project(attended, w_self)
    normed_full, pull_second = jax.vjp(layer_norm, after_self, gains[1], biases[1])
    normed_two = normed_full.astype(jnp.bfloat16)
    cross_queries = project(normed_two, w_query).astype(jnp.bfloat16)
    text_kv = lax.all_gather(text_project(own_text, w_text), "seq", axis=1, tiled=True)
    cross_full, cross_norm = cross_forward(cross_queries, text_kv, readable)
    crossed = cross_full.astype(jnp.bfloat16)
    after_cross = after_self + project(crossed, w_cross)
    normed_full, pull_third = jax.vjp(layer_norm, after_cross, gains[2], biases[2])
    normed_three = normed_full.astype(jnp.bfloat16)
    hidden_up = project(normed_three, w_up)
    activated_full, pull_gelu = jax.vjp(gelu_exact, hidden_up)
    activated = activated_full.astype(jnp.bfloat16)
    block_out = (after_cross + project(activated, w_down)).astype(jnp.bfloat16)
    gradient = out_grad.astype(jnp.float32)
    g_down = weight_term(activated, out_grad)
    d_up = pull_gelu(back_project(out_grad, w_down))[0].astype(jnp.bfloat16)
    g_up = weight_term(normed_three, d_up)
    d_third, g_gain_three, g_bias_three = pull_third(back_project(d_up, w_up))
    gradient = gradient + d_third
    grad_low = gradient.astype(jnp.bfloat16)
    g_cross = weight_term(crossed, grad_low)
    d_cross = back_project(grad_low, w_cross).astype(jnp.bfloat16)
    cross_delta = head_dot(d_cross, cross_full)
    d_cross_query, d_text_kv = cross_backward(
        cross_queries, text_kv, readable, cross_norm, d_cross, cross_delta
    )
    key_weight = w_text[0].astype(jnp.float32)
    value_weight = w_text[1].astype(jnp.float32)
    own_grad = lax.psum_scatter(
        d_text_kv.astype(jnp.bfloat16), "seq", scatter_dimension=1, tiled=True
    ).astype(jnp.float32)
    grad_text_key = own_grad[:, :, :model_width]
    grad_text_value = own_grad[:, :, model_width:]
    own_exact = own_text.astype(jnp.float32)
    g_text = jnp.stack(
        [exact_weight_term(own_exact, grad_text_key), exact_weight_term(own_exact, grad_text_value)]
    )
    text_grad = exact_back_project(grad_text_key, key_weight) + exact_back_project(
        grad_text_value, value_weight
    )
    d_cross_query = d_cross_query.astype(jnp.bfloat16)
    g_query = weight_term(normed_two, d_cross_query)
    d_second, g_gain_two, g_bias_two = pull_second(back_project(d_cross_query, w_query))
    gradient = gradient + d_second
    grad_low = gradient.astype(jnp.bfloat16)
    g_self = weight_term(attended, grad_low)
    d_attn = back_project(grad_low, w_self).astype(jnp.bfloat16)
    self_delta = head_dot(d_attn, self_full)
    d_query = self_query_grad(
        queries, key_value, clip_ends, clip_ids, frames, self_norm, self_delta, d_attn
    )
    gathered_stats = (
        lax.all_gather(jnp.swapaxes(self_norm, 1, 2), "seq", axis=1, tiled=True),
        lax.all_gather(jnp.swapaxes(self_delta, 1, 2), "seq", axis=1, tiled=True),
    )
    query_grad = jnp.concatenate([queries, d_attn], axis=2)
    d_key, d_value = self_key_grad(
        query_grad, key_value, clip_ends, clip_ids, frames, gathered_stats
    )
    g_qkv = jnp.stack(
        [weight_term(normed, d_query), weight_term(normed, d_key), weight_term(normed, d_value)]
    )
    d_normed = (
        back_project(d_query, w_qkv[0])
        + back_project(d_key, w_qkv[1])
        + back_project(d_value, w_qkv[2])
    )
    d_first, g_gain_one, g_bias_one = pull_first(d_normed)
    input_grad = gradient + d_first
    g_gain = jnp.stack([g_gain_one, g_gain_two, g_gain_three])
    g_bias = jnp.stack([g_bias_one, g_bias_two, g_bias_three])
    reduced = (
        lax.psum_scatter(g_gain, ("rows", "seq"), scatter_dimension=1, tiled=True),
        lax.psum_scatter(g_bias, ("rows", "seq"), scatter_dimension=1, tiled=True),
        lax.psum_scatter(g_qkv, ("rows", "seq"), scatter_dimension=1, tiled=True),
        lax.psum_scatter(g_self, ("rows", "seq"), scatter_dimension=0, tiled=True),
        lax.psum_scatter(g_query, ("rows", "seq"), scatter_dimension=0, tiled=True),
        lax.psum_scatter(g_text, ("rows", "seq"), scatter_dimension=1, tiled=True),
        lax.psum_scatter(g_cross, ("rows", "seq"), scatter_dimension=0, tiled=True),
        lax.psum_scatter(g_up, ("rows", "seq"), scatter_dimension=0, tiled=True),
        lax.psum_scatter(g_down, ("rows", "seq"), scatter_dimension=0, tiled=True),
    )
    return (
        block_out,
        input_grad,
        text_grad,
        reduced[0],
        reduced[1],
        reduced[2],
        reduced[3],
        reduced[4],
        reduced[5],
        reduced[6],
        reduced[7],
        reduced[8],
    )


MESH = pl.DeviceIdType.MESH
BF = jnp.bfloat16
F32 = jnp.float32
GROUP = 4
NEG = -1e30


def dot(a, b):
    return lax.dot_general(a, b, (((1,), (0,)), ((), ())), preferred_element_type=F32)


def dot_nt(a, b):
    return lax.dot_general(a, b, (((1,), (1,)), ((), ())), preferred_element_type=F32)


def dot_tn(a, b):
    return lax.dot_general(a, b, (((0,), (0,)), ((), ())), preferred_element_type=F32)


def mult(index, step):
    return pl.multiple_of(index * step, step)


def rows_of(index, step):
    return pl.ds(mult(index, step), step)


def each(count, step, body):
    def turn(i, carry):
        body(pl.ds(pl.multiple_of(i * step, step), step))
        return carry

    lax.fori_loop(0, count // step, turn, 0)


def three_parts(value):
    first = value.astype(BF).astype(F32)
    rest = value - first
    second = rest.astype(BF).astype(F32)
    return first, second, (rest - second).astype(BF).astype(F32)


def normalise(values):
    average = jnp.mean(values, axis=-1, keepdims=True)
    centred = values - average
    rstd = lax.rsqrt(jnp.mean(centred * centred, axis=-1, keepdims=True) + epsilon)
    return centred * rstd, rstd


def semaphore_plan(group_chips):
    sizes = dict(
        gb_s=8, gb_r=4, q_s=8, q_r=4, kv_s=8, kv_r=4, in_s=8, in_r=4, ow_g=8, ow_r=4, ow_x=4 * 8,
        n1=16, og=16, n3=16, a_at=8, a_cq=8, a_cr=8, b_cr=8, b_cq=8, b_at=8,
        e_c=4, e_z=4, o_c=4, o_z=4, t_c=4, t_z=4, s_c=4, s_z=4,
        gq_r=4, gq_s=8, gi_r=4, gi_s=8, go_r=4, go_g=8, gk_r=4, gk_s=8, gg_r=4, gg_s=8,
        m_z=12, m_r=12, m_c=6, h_c=6, h_r=12, h_z=12,
    )
    base, plan = 0, {}
    for name, size in sizes.items():
        plan[name] = base
        base += size
    return types.SimpleNamespace(**plan), base


def layer_kernel(plan, names, *refs):
    n = types.SimpleNamespace(**dict(zip(names, refs)))
    R, S, NZ, D = 4, 8, 4, n.x.shape[1]
    TB = n.x.shape[0]
    CH = 2 * TB
    T = S * TB
    HP = D // S
    FF = n.win.shape[1]
    G = GROUP
    GZ = G // 2
    E = S // G
    U = FF // G
    UB = FF // (R * S)
    DB = D // (R * S)
    TW = n.text.shape[1]
    KB = n.wckv.shape[0]
    r, s = lax.axis_index("rows"), lax.axis_index("seq")
    z, c = s // 2, s % 2
    sib = s + 1 - 2 * c
    ffn_z0 = (z // GZ) * GZ
    grp, mem = s // G, s % G
    ss, rs = n.ss, n.rs
    pending = {}

    def push(src, dst, name, to, origin, dev, send_shift=0, when=None):
        cp = pltpu.make_async_remote_copy(
            src_ref=src, dst_ref=dst,
            send_sem=ss.at[name + send_shift + to],
            recv_sem=rs.at[name + origin],
            device_id=dev, device_id_type=MESH,
        )
        pending.setdefault(name, []).append((cp, when))
        if when is None:
            cp.start()
        else:
            pl.when(when)(cp.start)

    def drain(*which):
        for name in which:
            for cp, when in pending.pop(name, []):
                if when is None:
                    cp.wait_send()
                else:
                    pl.when(when)(cp.wait_send)

    def arrive(landing, name, origin, when=None):
        cp = pltpu.make_async_remote_copy(
            src_ref=landing, dst_ref=landing, send_sem=ss.at[name],
            recv_sem=rs.at[name + origin], device_id=(r, sib), device_id_type=MESH,
        )
        if when is None:
            cp.wait_recv()
        else:
            pl.when(when)(cp.wait_recv)

    seq_peers = [(s + k) % S for k in range(1, S)]
    row_peers = [(r + k) % R for k in range(1, R)]
    z_peers = [(z + k) % NZ for k in range(1, NZ)]

    barrier = pltpu.get_barrier_semaphore()
    for p in seq_peers:
        pl.semaphore_signal(barrier, inc=1, device_id=(r, p), device_id_type=MESH)
    for p in row_peers:
        pl.semaphore_signal(barrier, inc=1, device_id=(p, s), device_id_type=MESH)
    pl.semaphore_wait(barrier, S + R - 2)

    gbt = n.gbt
    gbt[r, s] = n.gb[...]
    for p in row_peers:
        push(n.gb, gbt.at[r, s], plan.gb_r, p, r, (p, s))
    Wq3 = n.Wq3
    own_rows = rows_of(r * S + s, DB)
    for p in seq_peers:
        push(n.wqkv.at[:, :, rows_of(p, HP)], Wq3.at[:, own_rows, :], plan.q_s, p, s, (r, p))
    Win, Wout = n.Win, n.Wout
    out_rows = rows_of(r * E + grp, UB)
    for p in row_peers:
        push(n.wout, Wout.at[out_rows, :], plan.ow_r, p, r, (p, s))
    Wout[out_rows, :] = n.wout[...]
    Wq3[:, own_rows, :] = n.wqkv[:, :, rows_of(s, HP)]

    xf = n.x[...].astype(F32)
    xh, rstd = normalise(xf)
    n.XH[0] = xh
    n.RS[0] = rstd

    for p in row_peers:
        arrive(gbt.at[p, s], plan.gb_r, p)
    for p in seq_peers:
        push(gbt.at[:, s], gbt.at[:, s], plan.gb_s, p, s, (r, p))

    Wkv3 = n.Wkv3
    kv_rows = rows_of(r * S + s, KB)
    for p in seq_peers:
        push(n.wckv.at[:, rows_of(p, HP)], Wkv3.at[kv_rows, :], plan.kv_s, p, s, (r, p))
    Wkv3[kv_rows, :] = n.wckv[:, rows_of(s, HP)]

    mats = [n.Wm0, n.Wm1, n.Wm2]
    own_mats = [n.wo, n.wcq, n.wco]

    def mat_z(i):
        mats[i][r * NZ + z, c] = own_mats[i][...]
        for p in z_peers:
            push(own_mats[i], mats[i].at[r * NZ + z, c], plan.m_z + 4 * i, p, z, (r, 2 * p + c))

    def mat_r(i):
        for p in z_peers:
            arrive(mats[i].at[r * NZ + p, c], plan.m_z + 4 * i, p)
        block = mats[i].at[pl.ds(r * NZ, NZ), c]
        for p in row_peers:
            push(block, block, plan.m_r + 4 * i, p, r, (p, s))

    def mat_c(i):
        for p in row_peers:
            arrive(mats[i].at[pl.ds(p * NZ, NZ), c], plan.m_r + 4 * i, p)
        block = mats[i].at[:, c]
        push(block, block, plan.m_c + 2 * i, 0, 0, (r, sib))

    def mat_take(i):
        arrive(mats[i].at[:, 1 - c], plan.m_c + 2 * i, 0)

    def mat(i):
        return mats[i][...].reshape(D, D)

    mat_z(0)

    for p in seq_peers:
        arrive(Wq3.at[:, rows_of(r * S + p, DB), :], plan.q_s, p)
    q_block = rows_of(r, S * DB)
    for p in row_peers:
        push(Wq3.at[:, q_block, :], Wq3.at[:, q_block, :], plan.q_r, p, r, (p, s))

    for p in seq_peers:
        arrive(gbt.at[:, p], plan.gb_s, p)
    per = 128 // DB
    gbf = n.gbf
    for g in range(D // 128):
        total = None
        for k in range(per):
            rr, sx = divmod(g * per + k, S)
            tile = gbt[rr, sx].astype(F32)
            total = tile if total is None else total + tile
        gbf[:, g * 128 : (g + 1) * 128] = total

    def gain(i):
        return gbf[i : i + 1, :]

    def bias(i):
        return gbf[3 + i : 4 + i, :]

    n1f = n.n1f
    n1f[rows_of(s, TB), :] = (n.XH[0] * gain(0) + bias(0)).astype(BF)

    def gather_start(buf, name, z0, nz):
        m = s - 2 * z0
        block = buf.at[rows_of(m, TB), :]
        for k in range(1, nz):
            zl = (z - z0 + k) % nz
            push(block, block, name, 2 * zl + c, m, (r, 2 * (z0 + zl) + c))
        push(block, block, name, sib - 2 * z0, m, (r, sib))

    def gather_pass(buf, name, z0, nz, k):
        zl = (z - z0 + k) % nz
        if k:
            block = buf.at[rows_of(2 * zl + c, TB), :]
            arrive(block, name, 2 * zl + c)
            push(block, block, name, 2 * zl + c, 2 * zl + c, (r, sib), send_shift=8)

    def gather_take(buf, name, z0, nz, k):
        zl = (z - z0 + k) % nz
        arrive(buf.at[rows_of(2 * zl + 1 - c, TB), :], name, 2 * zl + 1 - c)
        return rows_of(zl, CH)

    gather_start(n1f, plan.n1, 0, NZ)

    mat_z(1)
    winp = n.winp
    for m in range(G):
        for rr in range(R):
            for j in range(E):
                b = rr * S + j * G + m
                at = m * U + (rr * E + j) * UB
                winp[:, at : at + UB] = n.win[:, b * UB : (b + 1) * UB]
    Win[own_rows, :] = winp[:, rows_of(mem, U)]
    for p in seq_peers:
        push(winp.at[:, rows_of(p % G, U)], Win.at[own_rows, :], plan.in_s, p, s, (r, p))

    lane = lax.broadcasted_iota(jnp.int32, (T, HP), 1)
    row = lax.broadcasted_iota(jnp.int32, (T, HP), 0)
    slot = lane % HD
    cl, tl = n.cl, n.tl

    def inside(lengths):
        low, found = jnp.int32(0), jnp.zeros((T, HP), jnp.bool_)
        for k in range(4):
            high = low + lengths[0, k]
            found = found | ((slot == k) & (row >= low) & (row < high))
            low = high
        return found

    ones_tail = jnp.where((slot >= 4) & (slot < 7), 1.0, 0.0)
    def mask_block():
        in_clip = inside(cl)
        n.oh[...] = jnp.where(in_clip, 1.0, 0.0).astype(BF)
        n.kbs[...] = jnp.where(slot < 4, jnp.where(in_clip, 0.0, NEG), ones_tail).astype(BF)
        n.kbc[...] = jnp.where(slot < 4, jnp.where(inside(tl), 0.0, NEG), ones_tail).astype(BF)

    mask_block()

    def first_half(shape):
        return lax.broadcasted_iota(jnp.int32, shape, 1) < HD

    def split_pair(value, other):
        front = first_half(value.shape)
        v, o = value.astype(F32), other.astype(F32)
        return jnp.where(front, v, o).astype(BF), jnp.where(front, o, v).astype(BF)

    for p in seq_peers:
        arrive(Wkv3.at[rows_of(r * S + p, KB), :], plan.kv_s, p)
    kv_block = rows_of(r, S * KB)
    for p in row_peers:
        push(Wkv3.at[kv_block, :], Wkv3.at[kv_block, :], plan.kv_r, p, r, (p, s))
    mat_r(0)

    Wq = n.Wq
    for p in row_peers:
        arrive(Wq3.at[:, rows_of(p, S * DB), :], plan.q_r, p)
    for i in range(3):
        Wq[:, i * HP : (i + 1) * HP] = Wq3[i]
    Q, K, V = n.Q, n.K, n.V
    KA = n.KA
    scale = HD ** (-0.5)

    def qkv_chunk(rows):
        def block():
            qkv_block(rows)

        block()

    def qkv_block(rows):
        got = dot(n1f[rows, :], Wq[...])
        Q[rows, :] = (got[:, :HP].astype(BF).astype(F32) * scale).astype(BF)
        K[rows, :] = got[:, HP : 2 * HP].astype(BF)
        V[rows, :] = got[:, 2 * HP :].astype(BF)
        KA[0, rows, :], KA[1, rows, :] = split_pair(K[rows, :], n.kbs[rows, :])

    qkv_chunk(gather_take(n1f, plan.n1, 0, NZ, 0))

    for k in range(1, NZ):
        gather_pass(n1f, plan.n1, 0, NZ, k)
        qkv_chunk(gather_take(n1f, plan.n1, 0, NZ, k))

    mat_c(0)

    AF, QB = n.AF, n.QB
    oh = n.oh
    AB = n.out
    ao = n.ao

    def finish(o0, o1, l0, l1):
        return jnp.where(first_half(o0.shape), o0 / l0, o1 / l1)

    def with_norm(q_aug, head, norm):
        spot = lax.broadcasted_iota(jnp.int32, q_aug.shape, 1)
        base = (1 - head) * HD
        a, b, d = three_parts(-norm)
        w = q_aug.astype(F32)
        w = jnp.where(spot == base + 4, a, w)
        w = jnp.where(spot == base + 5, b, w)
        return jnp.where(spot == base + 6, d, w).astype(BF)

    kpos = lax.broadcasted_iota(jnp.int32, (CH, CH), 1)
    qpos = lax.broadcasted_iota(jnp.int32, (CH, CH), 0)
    def self_rows(i, low, high):
        qa = split_pair(Q[low:high, :], oh[low:high, :])
        outs, sums = [], []
        for h in range(2):
            diag = jnp.where(kpos <= qpos, dot_nt(qa[h], KA[h, low:high, :]), NEG)
            top = jnp.max(diag, axis=1, keepdims=True)
            if i:
                left = dot_nt(qa[h], KA[h, :low, :])
                top = jnp.maximum(top, jnp.max(left, axis=1, keepdims=True))
            diag = jnp.exp(diag - top)
            total = jnp.sum(diag, axis=1, keepdims=True)
            got = dot(diag.astype(BF), V[low:high, :])
            if i:
                left = jnp.exp(left - top)
                total = total + jnp.sum(left, axis=1, keepdims=True)
                got = got + dot(left.astype(BF), V[:low, :])
            outs.append(got)
            sums.append(total)
            QB[h, low:high, :] = with_norm(qa[h], h, top + jnp.log(total))
        full = finish(outs[0], outs[1], sums[0], sums[1])
        AF[low:high, :] = full
        AB[low:high, :] = full.astype(BF)

    for i in range(NZ):
        def self_block():
            self_rows(i, i * CH, (i + 1) * CH)

        self_block()
        for p in (2 * i, 2 * i + 1):
            push(AB.at[p * TB : (p + 1) * TB, :], ao.at[:, rows_of(s, HP)], plan.a_at, p, s, (r, p), when=s != p)
    ao[:, rows_of(s, HP)] = AB[rows_of(s, TB), :]

    mat_z(2)
    mat_r(1)
    for p in seq_peers:
        arrive(Win.at[rows_of(r * S + p, DB), :], plan.in_s, p)
    in_block = rows_of(r, S * DB)
    for p in row_peers:
        push(Win.at[in_block, :], Win.at[in_block, :], plan.in_r, p, r, (p, s))

    for p in row_peers:
        arrive(Wkv3.at[rows_of(p, S * KB), :], plan.kv_r, p)
    wide = Wkv3[...].astype(F32).reshape(R * S, KB, HP)
    half = KB // 2
    Wkv = n.Wkv
    Wkv[:, :HP] = wide[:, :half, :].reshape(TW, HP).astype(BF)
    Wkv[:, HP:] = wide[:, half:, :].reshape(TW, HP).astype(BF)
    CK, CV = n.CK, n.CV

    def text_rows(rows):
        got = dot(n.text[rows, :], Wkv[...]).astype(BF)
        CK[rows, :] = got[:, :HP]
        CV[rows, :] = got[:, HP:]

    def text_block():
        each(T, CH, text_rows)

    text_block()

    mat_take(0)
    for p in seq_peers:
        arrive(ao.at[:, rows_of(p, HP)], plan.a_at, p)
    h1 = n.x[...].astype(F32) + dot(ao[...], mat(0))
    n.H[...] = h1
    xh, rstd = normalise(h1)
    n.XH[1] = xh
    n.RS[1] = rstd
    n2 = (xh * gain(1) + bias(1)).astype(BF)
    n.n2[...] = n2
    mat_c(1)
    mat_take(1)
    cqo = n.wide
    cqo[...] = dot(n2, mat(1)).astype(BF)
    CQ = n.CQ
    own_tokens = rows_of(s, TB)

    def to_heads(src, dst, name):
        for k in range(1, S):
            p = (s + k) % S
            push(src.at[:, rows_of(p, HP)], dst.at[own_tokens, :], name, p, s, (r, p))
        dst[own_tokens, :] = src[:, rows_of(s, HP)]

    def heads_take(dst, name, k):
        zl = (z + k) % NZ
        if k:
            arrive(dst.at[rows_of(2 * zl + c, TB), :], name, 2 * zl + c)
        arrive(dst.at[rows_of(2 * zl + 1 - c, TB), :], name, 2 * zl + 1 - c)
        return rows_of(zl, CH)

    def to_tokens(src, dst, name, k):
        zl = (z + k) % NZ
        for p in ([2 * zl + c] if k else []) + [2 * zl + 1 - c]:
            push(src.at[rows_of(p, TB), :], dst.at[:, rows_of(s, HP)], name, p, s, (r, p))
        if not k:
            dst[:, rows_of(s, HP)] = src[own_tokens, :]

    to_heads(cqo, CQ, plan.a_cq)
    for j in range(1, E):
        p = (s + j * G) % S
        push(n.wout, Wout.at[out_rows, :], plan.ow_g, p, s, (r, p))
    mat_r(2)

    CKA, CVA, CKT, CQB = n.CKA, n.CVA, n.CKT, n.CQB
    CF, CB, co = n.CF, n.out, n.co
    drain(plan.a_at)

    def prepare_cross(rows):
        CKA[0, rows, :], CKA[1, rows, :] = split_pair(CK[rows, :], n.kbc[rows, :])

    each(T, CH, prepare_cross)
    def cross_rows(rows):
        scaled = (CQ[rows, :].astype(F32) * scale).astype(BF)
        CQ[rows, :] = scaled
        qa = split_pair(scaled, oh[rows, :])
        outs, sums = [], []
        for h in range(2):
            got = dot_nt(qa[h], CKA[h])
            top = jnp.max(got, axis=1, keepdims=True)
            got = jnp.exp(got - top)
            total = jnp.sum(got, axis=1, keepdims=True)
            outs.append(dot(got.astype(BF), CV[...]))
            sums.append(total)
            CQB[h, rows, :] = with_norm(qa[h], h, top + jnp.log(total))
        full = finish(outs[0], outs[1], sums[0], sums[1])
        CF[rows, :] = full
        CB[rows, :] = full.astype(BF)

    for k in range(NZ):
        rows = heads_take(CQ, plan.a_cq, k)

        def cross_block():
            cross_rows(rows)

        cross_block()
        to_tokens(CB, co, plan.a_cr, k)
    ogf = n.ogf
    ogf[rows_of(mem, TB), :] = n.og[...]
    gather_start(ogf, plan.og, ffn_z0, GZ)
    out_block = rows_of(r, E * UB)
    for j in range(1, E):
        other = rows_of(r * E + (grp + j) % E, UB)
        arrive(Wout.at[other, :], plan.ow_g, (s + j * G) % S)
        for p in row_peers:
            push(Wout.at[other, :], Wout.at[other, :], plan.ow_x + 4 * j, p, r, (p, s))
    mat_c(2)
    mat_take(2)
    for p in seq_peers:
        arrive(co.at[:, rows_of(p, HP)], plan.a_cr, p)
    h2 = n.H[...] + dot(co[...], mat(2))
    n.H[...] = h2
    xh, rstd = normalise(h2)
    n.XH[2] = xh
    n.RS[2] = rstd
    n3f = n.n3f
    n3f[rows_of(mem, TB), :] = (xh * gain(2) + bias(2)).astype(BF)
    gather_start(n3f, plan.n3, ffn_z0, GZ)

    for p in row_peers:
        arrive(Win.at[rows_of(p, S * DB), :], plan.in_r, p)
        arrive(Wout.at[rows_of(p * E + grp, UB), :], plan.ow_r, p)
        for j in range(1, E):
            arrive(Wout.at[rows_of(p * E + (grp + j) % E, UB), :], plan.ow_x + 4 * j, p)
    AD = n.AD
    ACT, DUP = AD.at[: G * TB], AD.at[G * TB :]
    UT = 512

    def reduce_core(ps, rb, name, zl):
        push(ps.at[rows_of(2 * zl + 1 - c, TB), :], rb.at[zl], name, zl, zl, (r, sib))

    def reduce_z(ps, rb, rz, cname, zname, z0, nz, zl, when=None):
        arrive(rb.at[zl], cname, zl)
        mine = rows_of(2 * zl + c, TB)
        ps[mine, :] = (ps[mine, :].astype(F32) + rb[zl].astype(F32)).astype(BF)
        push(ps.at[mine, :], rz.at[(z - z0 - zl + nz - 1) % nz], zname, zl, z - z0, (r, 2 * (z0 + zl) + c), when=when)

    def reduce_take(ps, rb, rz, cname, zname, z0, nz, summed=False):
        own = z - z0
        mine = rows_of(2 * own + c, TB)
        total = ps[mine, :].astype(F32)
        if not summed:
            arrive(rb.at[own], cname, own)
            total = total + rb[own].astype(F32)
        for k in range(1, nz):
            zl = (own + k) % nz
            arrive(rz.at[k - 1], zname, zl)
            total = total + rz[k - 1].astype(F32)
        return total

    ps0 = n.ps0
    NT = G * TB
    psE = ps0.at[:NT]
    psO = ps0.at[NT:]
    for k in range(GZ):
        gather_pass(ogf, plan.og, ffn_z0, GZ, k)
        gather_take(ogf, plan.og, ffn_z0, GZ, k)
        gather_pass(n3f, plan.n3, ffn_z0, GZ, k)
        rows = gather_take(n3f, plan.n3, ffn_z0, GZ, k)

        def hidden(cols):
            up = dot(n3f[rows, :], Win[:, cols])
            d_act = dot_nt(ogf[rows, :], Wout[cols, :])
            cdf = 0.5 * (1.0 + lax.erf(up * (0.5**0.5)))
            pdf = jnp.exp(-0.5 * up * up) * 0.3989422804014327
            ACT[rows, cols] = (up * cdf).astype(BF)
            DUP[rows, cols] = (d_act * (cdf + up * pdf)).astype(BF)

        def hidden_block():
            each(U, UT, hidden)

        def back_block():
            psE[rows, :] = dot_nt(DUP[rows, :], Win[...]).astype(BF)

        hidden_block()
        back_block()
        zl = (z - ffn_z0 + k) % GZ
        reduce_core(psE, n.rbE, plan.e_c, zl)
    for k in range(1, GZ):
        reduce_z(psE, n.rbE, n.rzE, plan.e_c, plan.e_z, ffn_z0, GZ, (z - ffn_z0 + k) % GZ)
    drain(plan.ow_r, plan.ow_g, plan.in_r, plan.in_s, *[plan.ow_x + 4 * j for j in range(1, E)])

    def norm_back(i, e):
        n.gg[i : i + 1, :] = jnp.sum(e * n.XH[i], axis=0, keepdims=True)
        n.gg[3 + i : 4 + i, :] = jnp.sum(e, axis=0, keepdims=True)
        y = e * gain(i)
        xhat = n.XH[i]
        a = jnp.mean(y, axis=1, keepdims=True)
        b = jnp.mean(y * xhat, axis=1, keepdims=True)
        return (y - a - xhat * b) * n.RS[i]

    e = reduce_take(psE, n.rbE, n.rzE, plan.e_c, plan.e_z, ffn_z0, GZ)
    g2 = n.og[...].astype(F32) + norm_back(2, e)
    n.GR[...] = g2
    g2b = g2.astype(BF)
    dco = n.wide
    drain(plan.a_cq)
    dco[...] = dot_nt(g2b, mat(2)).astype(BF)
    DC = n.DC
    to_heads(dco, DC, plan.b_cr)

    def mat_grad(i, left, right):
        drain(plan.m_z + 4 * i, plan.m_r + 4 * i, plan.m_c + 2 * i)

        def mat_block():
            mats[i][...] = dot_tn(left, right).astype(BF).reshape(mats[i].shape)

        mat_block()
        push(mats[i].at[:, 1 - c], n.rmc.at[i], plan.h_c + 2 * i, 0, 0, (r, sib))

    def mat_grad_r(i):
        arrive(n.rmc.at[i], plan.h_c + 2 * i, 0)
        mine = mats[i].at[:, c]
        mine[...] = (mine[...].astype(F32) + n.rmc[i].astype(F32)).astype(BF)
        for k, p in enumerate(row_peers, 1):
            block = mats[i].at[pl.ds(p * NZ, NZ), c]
            push(block, n.rmr.at[i, R - 1 - k], plan.h_r + 4 * i, p, r, (p, s))

    def mat_grad_z(i):
        mine = mats[i].at[pl.ds(r * NZ, NZ), c]
        total = mine[...].astype(F32)
        for k, p in enumerate(row_peers):
            arrive(n.rmr.at[i, k], plan.h_r + 4 * i, p)
            total = total + n.rmr[i, k].astype(F32)
        mine[...] = total.astype(BF)
        for p in z_peers:
            push(mats[i].at[r * NZ + p, c], n.rmz.at[i, z], plan.h_z + 4 * i, p, z, (r, 2 * p + c))

    def mat_grad_take(i, out):
        total = mats[i][r * NZ + z, c].astype(F32)
        for p in z_peers:
            arrive(n.rmz.at[i, p], plan.h_z + 4 * i, p)
            total = total + n.rmz[i, p].astype(F32)
        out[...] = total

    for k in range(GZ):
        zl = (z - ffn_z0 + k) % GZ
        rows = rows_of(zl, CH)

        def out_block_rows():
            psO[rows, :] = dot(ACT[rows, :], Wout[...]).astype(BF)

        out_block_rows()
        reduce_core(psO, n.rbO, plan.o_c, zl)
    for k in range(1, GZ):
        reduce_z(psO, n.rbO, n.rzO, plan.o_c, plan.o_z, ffn_z0, GZ, (z - ffn_z0 + k) % GZ)
    def gout_rows(cols):
        Wout[cols, :] = dot_tn(ACT[:, cols], ogf[...]).astype(BF)

    def gout_block():
        each(U, 256, gout_rows)

    gout_block()
    rgo = n.rgo
    for k, p in enumerate(row_peers, 1):
        push(Wout.at[rows_of(p, E * UB), :], rgo.at[R - 1 - k], plan.go_r, p, r, (p, s))

    mat_grad(2, co[...], g2b)

    def gin_rows(cols):
        Win[cols, :] = dot_tn(n3f[:, cols], DUP[...]).astype(BF)

    def gin_block():
        each(D, 256, gin_rows)

    gin_block()
    rgi = n.rgi
    for k, p in enumerate(row_peers, 1):
        push(Win.at[rows_of(p, S * DB), :], rgi.at[R - 1 - k], plan.gi_r, p, r, (p, s))
    n.o_out[...] = (
        n.H[...] + reduce_take(psO, n.rbO, n.rzO, plan.o_c, plan.o_z, ffn_z0, GZ)
    ).astype(BF)

    def prepare_cross_back(rows):
        CVA[0, rows, :], CVA[1, rows, :] = split_pair(CV[rows, :], ones_rows(CH))
        CKT[:, rows] = jnp.transpose(CK[rows, :].astype(F32)).astype(BF)

    def ones_rows(count):
        spot = lax.broadcasted_iota(jnp.int32, (count, HP), 1) % HD
        return jnp.where((spot >= 4) & (spot < 7), 1.0, 0.0)

    def with_delta(grad, full):
        front = first_half(grad.shape)
        wide = grad.astype(F32)
        prod = wide * full
        d0 = jnp.sum(jnp.where(front, prod, 0.0), axis=1, keepdims=True)
        d1 = jnp.sum(jnp.where(front, 0.0, prod), axis=1, keepdims=True)
        zero = jnp.zeros_like(wide)
        return (
            with_norm(jnp.where(front, wide, zero), 0, d0),
            with_norm(jnp.where(front, zero, wide), 1, d1),
        )

    each(T, CH, prepare_cross_back)
    DCK, DCV, DQ, dqo = n.DCK, n.DCV, n.out, n.dqo
    drain(plan.a_cr)

    def heads_join(a, b, axis):
        spot = lax.broadcasted_iota(jnp.int32, a.shape, axis)
        return jnp.where(spot < HD, a, b)

    def cross_back_rows(k, rows):
        grad = DC[rows, :]
        ga = with_delta(grad, CF[rows, :])
        q2 = CQ[rows, :]
        dv, dk, dq = [], [], []
        for h in range(2):
            prob = jnp.exp(dot_nt(CKA[h], CQB[h, rows, :]))
            ds = (prob * dot_nt(CVA[h], ga[h])).astype(BF)
            dv.append(dot(prob.astype(BF), grad))
            dk.append(dot(ds, q2))
            dq.append(dot(CKT[...], ds))
        dvj, dkj = heads_join(dv[0], dv[1], 1), heads_join(dk[0], dk[1], 1)
        if k:
            DCV[...] += dvj
            DCK[...] += dkj
        else:
            DCV[...] = dvj
            DCK[...] = dkj
        DQ[rows, :] = (jnp.transpose(heads_join(dq[0], dq[1], 0)) * scale).astype(BF)

    for k in range(NZ):
        rows = heads_take(DC, plan.b_cr, k)

        def cross_back_block():
            cross_back_rows(k, rows)

        cross_back_block()
        to_tokens(DQ, dqo, plan.b_cq, k)
    mat_grad_r(2)

    DKV = n.DKV
    DKV[:, :HP] = DCK[...].astype(BF)
    DKV[:, HP:] = DCV[...].astype(BF)
    psT = AD.at[:T, :TW]

    for k in range(NZ):
        zl = (z + k) % NZ
        rows = rows_of(zl, CH)

        def text_back():
            psT[rows, :] = dot_nt(DKV[rows, :], Wkv[...]).astype(BF)

        text_back()
        reduce_core(psT, n.rbT, plan.t_c, zl)

    for p in seq_peers:
        arrive(dqo.at[:, rows_of(p, HP)], plan.b_cq, p)
    e = dot_nt(dqo[...], mat(1))
    g1 = n.GR[...] + norm_back(1, e)
    n.GR[...] = g1
    g1b = g1.astype(BF)
    dao = n.wide
    drain(plan.b_cr)
    dao[...] = dot_nt(g1b, mat(0)).astype(BF)
    DA = n.DA
    to_heads(dao, DA, plan.b_at)

    def sum_rows(own, landed, name):
        total = own.astype(F32)
        for k, p in enumerate(row_peers):
            arrive(landed.at[k], name, p)
            total = total + landed[k].astype(F32)
        return total

    total = sum_rows(Wout[out_block, :], rgo, plan.go_r)
    rgo2 = n.rgo2
    if E == 1:
        n.o_ow[...] = total
    else:
        Wout[out_block, :] = total.astype(BF)
        for j in range(1, E):
            p = (s + j * G) % S
            push(
                Wout.at[rows_of(r * E + (grp + j) % E, UB), :], rgo2.at[grp], plan.go_g, p, s, (r, p)
            )

    drain(plan.kv_s, plan.kv_r)
    span = TW // 2
    def gkv_rows(i):
        got = dot_tn(n.text[:, i * span : (i + 1) * span], DKV[...])
        both = [got[:, q * HP : (q + 1) * HP].reshape(span // half, half, HP) for q in range(2)]
        both = jnp.concatenate(both, axis=1).reshape(2 * span, HP)
        Wkv3[2 * i * span : 2 * (i + 1) * span, :] = both.astype(BF)

    def gkv_block():
        gkv_rows(0)
        gkv_rows(1)

    gkv_block()
    rgk = n.rgk
    for k, p in enumerate(row_peers, 1):
        push(Wkv3.at[rows_of(p, S * KB), :], rgk.at[R - 1 - k], plan.gk_r, p, r, (p, s))
    mat_grad(1, n.n2[...], dqo[...])
    mat_grad(0, ao[...], g1b)
    mat_grad_r(1)
    mat_grad_r(0)

    VA, KT, DOA = CVA, CKT, CQB
    DQT, DQKV = n.DQT, n.DQKV
    drain(plan.e_c, plan.e_z, plan.o_c, plan.o_z, plan.b_at)

    def prepare_self_back(rows):
        VA[0, rows, :], VA[1, rows, :] = split_pair(V[rows, :], ones_rows(CH))
        KT[:, rows] = jnp.transpose(K[rows, :].astype(F32)).astype(BF)

    each(T, CH, prepare_self_back)
    for k in range(NZ):
        rows = heads_take(DA, plan.b_at, k)
        DOA[0, rows, :], DOA[1, rows, :] = with_delta(DA[rows, :], AF[rows, :])
    def self_back_rows(j, low, high):
        grad, q2 = DA[low:, :], Q[low:, :]
        dv, dk, dq = [], [], []
        for h in range(2):
            sc = dot_nt(KA[h, low:high, :], QB[h, low:, :])
            head = jnp.where(qpos <= kpos, sc[:, :CH], NEG)
            sc = jnp.concatenate([head, sc[:, CH:]], axis=1) if j < NZ - 1 else head
            prob = jnp.exp(sc)
            ds = (prob * dot_nt(VA[h, low:high, :], DOA[h, low:, :])).astype(BF)
            dv.append(dot(prob.astype(BF), grad))
            dk.append(dot(ds, q2))
            dq.append(dot(KT[:, low:high], ds))
        if j:
            DQT[:, low:] += heads_join(dq[0], dq[1], 0)
        else:
            DQT[...] = heads_join(dq[0], dq[1], 0)
        DQKV[low:high, :HP] = (jnp.transpose(DQT[:, low:high]) * scale).astype(BF)
        DQKV[low:high, HP : 2 * HP] = heads_join(dk[0], dk[1], 1).astype(BF)
        DQKV[low:high, 2 * HP :] = heads_join(dv[0], dv[1], 1).astype(BF)
        ps0[low:high, :] = dot_nt(DQKV[low:high, :], Wq[...]).astype(BF)

    for j in range(NZ):
        def self_back_block():
            self_back_rows(j, j * CH, (j + 1) * CH)

        self_back_block()
        reduce_core(ps0, n.rb0, plan.s_c, j)
        if j:
            reduce_z(ps0, n.rb0, n.rz0, plan.s_c, plan.s_z, 0, NZ, j - 1, when=z != j - 1)
    reduce_z(ps0, n.rb0, n.rz0, plan.s_c, plan.s_z, 0, NZ, NZ - 1, when=z != NZ - 1)
    Win[in_block, :] = sum_rows(Win[in_block, :], rgi, plan.gi_r).astype(BF)
    rgi2 = n.rgi2
    for p in seq_peers:
        push(Win.at[rows_of(r * S + p, DB), :], rgi2.at[s], plan.gi_s, p, s, (r, p))
    rgi2[s] = Win[own_rows, :]
    mat_grad_z(2)
    for k in range(1, NZ):
        reduce_z(psT, n.rbT, n.rzT, plan.t_c, plan.t_z, 0, NZ, (z + k) % NZ)

    drain(plan.q_s, plan.q_r)

    def gq_rows(cols):
        got = dot_tn(n1f[:, cols], DQKV[...]).astype(BF)
        for i in range(3):
            Wq3[i, cols, :] = got[:, i * HP : (i + 1) * HP]

    def gq_block():
        each(D, 256, gq_rows)

    gq_block()
    rgq = n.rgq
    for k, p in enumerate(row_peers, 1):
        push(Wq3.at[:, rows_of(p, S * DB), :], rgq.at[R - 1 - k], plan.gq_r, p, r, (p, s))

    mat_grad_z(1)
    mat_grad_z(0)
    total = sum_rows(Wkv3[kv_block, :], rgk, plan.gk_r)
    Wkv3[kv_block, :] = total.astype(BF)
    GC = n.GC
    for p in seq_peers:
        push(Wkv3.at[rows_of(r * S + p, KB), :], GC.at[:, rows_of(s, HP)], plan.gk_s, p, s, (r, p))
    GC[:, rows_of(s, HP)] = Wkv3[kv_rows, :]
    n.o_tg[...] = reduce_take(psT, n.rbT, n.rzT, plan.t_c, plan.t_z, 0, NZ)
    if E > 1:
        total = Wout[out_rows, :].astype(F32)
        for j in range(1, E):
            g2i = (grp + j) % E
            arrive(rgo2.at[g2i], plan.go_g, (s + j * G) % S)
            total = total + rgo2[g2i].astype(F32)
        n.o_ow[...] = total
    for p in seq_peers:
        arrive(rgi2.at[p], plan.gi_s, p)
    for m in range(G):
        total = rgi2[m].astype(F32)
        for g in range(1, E):
            total = total + rgi2[g * G + m].astype(F32)
        for rr in range(R):
            for j in range(E):
                b = rr * S + j * G + m
                at = (rr * E + j) * UB
                n.o_in[:, b * UB : (b + 1) * UB] = total[:, at : at + UB]

    e = reduce_take(ps0, n.rb0, n.rz0, plan.s_c, plan.s_z, 0, NZ, summed=True)
    back = norm_back(0, e)
    gg, rgg, gg2, rgg2 = n.gg, n.rgg, n.gg2, n.rgg2
    GW = D // R
    for k, p in enumerate(row_peers, 1):
        push(gg.at[:, rows_of(p, GW)], rgg.at[R - 1 - k], plan.gg_r, p, r, (p, s))
    n.o_ig[...] = n.GR[...] + back
    Wq3[:, q_block, :] = sum_rows(Wq3[:, q_block, :], rgq, plan.gq_r).astype(BF)
    GQ = n.GQ
    for p in seq_peers:
        push(Wq3.at[:, rows_of(r * S + p, DB), :], GQ.at[:, :, rows_of(s, HP)], plan.gq_s, p, s, (r, p))
    GQ[:, :, rows_of(s, HP)] = Wq3[:, own_rows, :]
    gg2[...] = sum_rows(gg[:, rows_of(r, GW)], rgg, plan.gg_r)
    for p in seq_peers:
        push(gg2.at[:, rows_of(p // per, 128)], rgg2.at[s], plan.gg_s, p, s, (r, p))
    mat_grad_take(2, n.o_co)
    mat_grad_take(1, n.o_cq)
    mat_grad_take(0, n.o_so)
    for p in seq_peers:
        arrive(GC.at[:, rows_of(p, HP)], plan.gk_s, p)
    n.o_ckv[...] = GC[...].astype(F32)
    total = gg2[:, rows_of(s // per, 128)]
    for p in seq_peers:
        arrive(rgg2.at[p], plan.gg_s, p)
        total = total + rgg2[p]
    n.o_gb[...] = total
    for p in seq_peers:
        arrive(GQ.at[:, :, rows_of(p, HP)], plan.gq_s, p)
    n.o_qkv[...] = GQ[...].astype(F32)
    drain(*list(pending))


def fused_shards(
    hidden_in, clip_lengths, text_lengths, text_states, norm_gain, norm_bias, self_qkv,
    self_out, cross_query, cross_kv, cross_out, ffn_in, ffn_out, out_grad,
):
    R, S = lax.axis_size("rows"), lax.axis_size("seq")
    TB, D = hidden_in.shape[1:]
    TW = text_states.shape[2]
    T, HP, DB = TB * S, D // S, D // (R * S)
    FF = ffn_in.shape[1]
    G = GROUP
    E, U, UB, NT, NZ = S // G, FF // G, FF // (R * S), G * TB, S // 2
    GZ = G // 2
    KB = 2 * cross_kv.shape[1]
    index = lax.axis_index("rows") * S + lax.axis_index("seq")
    per = 128 // DB
    both = jnp.concatenate([norm_gain, norm_bias], axis=0)
    both = jnp.pad(both, ((0, 10), (0, 0)))
    spot = jnp.arange(128, dtype=jnp.int32)[None, :] // DB
    gb = jnp.where(spot == index % per, jnp.tile(both, (1, per)), jnp.zeros((), both.dtype))
    ins = dict(
        cl=clip_lengths, tl=text_lengths, x=hidden_in.reshape(TB, D), og=out_grad.reshape(TB, D),
        text=text_states.reshape(T, TW), gb=gb, wqkv=self_qkv, wo=self_out, wcq=cross_query,
        wco=cross_out, wckv=cross_kv.reshape(KB, D), win=ffn_in, wout=ffn_out,
    )
    outs = dict(
        o_out=((TB, D), BF), o_ig=((TB, D), F32), o_tg=((TB, TW), F32), o_gb=((8, 128), F32),
        o_qkv=(self_qkv.shape, F32), o_so=(self_out.shape, F32), o_cq=(cross_query.shape, F32),
        o_ckv=((KB, D), F32), o_co=(cross_out.shape, F32), o_in=(ffn_in.shape, F32),
        o_ow=(ffn_out.shape, F32),
    )
    plan, count = semaphore_plan(GZ)
    hp = (T, HP)
    pair = (2, T, HP)
    scratch = dict(
        gbt=((R, S, 16, 128), BF), gbf=((16, D), F32), Wq3=((3, D, HP), BF), Wq=((D, 3 * HP), BF),
        Wkv3=((R * S * KB, HP), BF), Wkv=((TW, 2 * HP), BF),
        Wm0=((R * NZ, 2, DB, D), BF), Wm1=((R * NZ, 2, DB, D), BF), Wm2=((R * NZ, 2, DB, D), BF),
        Win=((D, U), BF), Wout=((U, D), BF), winp=((DB, FF), BF),
        XH=((3, TB, D), F32), RS=((3, TB, 1), F32), H=((TB, D), F32), GR=((TB, D), F32),
        n1f=((T, D), BF), n3f=((NT, D), BF), ogf=((NT, D), BF), n2=((TB, D), BF),
        oh=(hp, BF), kbs=(hp, BF), kbc=(hp, BF),
        Q=(hp, BF), K=(hp, BF), V=(hp, BF), CK=(hp, BF), CV=(hp, BF), CQ=(hp, BF),
        KA=(pair, BF), QB=(pair, BF),
        CKA=(pair, BF), CVA=(pair, BF), CQB=(pair, BF), CKT=((HP, T), BF),
        AF=(hp, F32), CF=(hp, F32), out=(hp, BF), DC=(hp, BF), DA=(hp, BF),
        ao=((TB, D), BF), wide=((TB, D), BF), co=((TB, D), BF), dqo=((TB, D), BF),
        DCK=(hp, F32), DCV=(hp, F32), DKV=((T, 2 * HP), BF),
        DQT=((HP, T), F32), DQKV=((T, 3 * HP), BF),
        AD=((2 * NT, U), BF),
        ps0=((max(T, 2 * NT), D), BF),
        rbE=((GZ, TB, D), BF), rzE=((GZ - 1, TB, D), BF), rbO=((GZ, TB, D), BF), rzO=((GZ - 1, TB, D), BF),
        rbT=((NZ, TB, TW), BF), rzT=((NZ - 1, TB, TW), BF), rb0=((NZ, TB, D), BF), rz0=((NZ - 1, TB, D), BF),
        rgo=((R - 1, E * UB, D), BF), rgo2=((E, UB, D), BF), rgi=((R - 1, S * DB, U), BF), rgi2=((S, DB, U), BF),
        rgk=((R - 1, S * KB, HP), BF), GC=((KB, D), BF), rgq=((R - 1, 3, S * DB, HP), BF), GQ=((3, DB, D), BF),
        gg=((8, D), F32), rgg=((R - 1, 8, D // R), F32), gg2=((8, D // R), F32), rgg2=((S, 8, 128), F32),
        rmc=((3, R * NZ, DB, D), BF), rmr=((3, R - 1, NZ, DB, D), BF), rmz=((3, NZ, DB, D), BF),
    )
    names = list(ins) + list(outs) + list(scratch) + ["ss", "rs"]
    vmem = pl.BlockSpec(memory_space=pltpu.VMEM)
    smem = pl.BlockSpec(memory_space=pltpu.SMEM)
    got = pl.pallas_call(
        functools.partial(layer_kernel, plan, names),
        out_shape=[jax.ShapeDtypeStruct(*v) for v in outs.values()],
        in_specs=[smem, smem] + [vmem] * (len(ins) - 2),
        out_specs=[vmem] * len(outs),
        scratch_shapes=[pltpu.VMEM(*v) for v in scratch.values()]
        + [pltpu.SemaphoreType.DMA((count,)), pltpu.SemaphoreType.DMA((count,))],
        compiler_params=pltpu.CompilerParams(
            collective_id=0, has_side_effects=True, vmem_limit_bytes=63 << 20
        ),
    )(*ins.values())
    o = types.SimpleNamespace(**dict(zip(outs, got)))
    mine = lax.dynamic_slice(o.o_gb, (0, (index % per) * DB), (8, DB))
    return (
        o.o_out.reshape(hidden_in.shape), o.o_ig.reshape(hidden_in.shape),
        o.o_tg.reshape(1, TB, TW), mine[:3], mine[3:6], o.o_qkv, o.o_so, o.o_cq,
        o.o_ckv.reshape(cross_kv.shape), o.o_co, o.o_in, o.o_ow,
    )


def fits(mesh):
    return dict(mesh.shape) == {"rows": 4, "seq": 8}


def solution(mesh):
    placed = (
        P("rows", "seq", None),
        P("rows", None),
        P("rows", None),
        P("rows", None, None),
        P(None, ("rows", "seq")),
        P(None, ("rows", "seq")),
        P(None, ("rows", "seq"), None),
        P(("rows", "seq"), None),
        P(("rows", "seq"), None),
        P(None, ("rows", "seq"), None),
        P(("rows", "seq"), None),
        P(("rows", "seq"), None),
        P(("rows", "seq"), None),
        P("rows", "seq", None),
    )
    return jax.shard_map(
        fused_shards if fits(mesh) else shards,
        mesh=mesh,
        in_specs=placed,
        out_specs=(
            P("rows", "seq", None),
            P("rows", "seq", None),
            P("rows", "seq", None),
            P(None, ("rows", "seq")),
            P(None, ("rows", "seq")),
            P(None, ("rows", "seq"), None),
            P(("rows", "seq"), None),
            P(("rows", "seq"), None),
            P(None, ("rows", "seq"), None),
            P(("rows", "seq"), None),
            P(("rows", "seq"), None),
            P(("rows", "seq"), None),
        ),
        check_vma=False,
    )
```

```python
import functools
import types

import jax
import jax.numpy as jnp
from jax import lax
from jax.experimental import pallas as pl
from jax.experimental.pallas import tpu as pltpu
from jax.sharding import PartitionSpec as P

HD = 64


epsilon = 1e-05
masked_score = -1e30
group_heads = 4
highest = lax.Precision.HIGHEST


def layer_norm(values, gains, biases):
    average = jnp.mean(values, axis=-1, keepdims=True)
    centred = values - average
    variance = jnp.mean(centred * centred, axis=-1, keepdims=True)
    return centred * lax.rsqrt(variance + epsilon) * gains + biases


def gelu_exact(values):
    return jax.nn.gelu(values, approximate=False)


def project(left, weight):
    return jnp.einsum("rtd,de->rte", left, weight, preferred_element_type=jnp.float32)


def weight_term(left, right):
    return jnp.einsum("rtd,rte->de", left, right, preferred_element_type=jnp.float32)


def back_project(gradient, weight):
    return jnp.einsum("rte,de->rtd", gradient, weight, preferred_element_type=jnp.float32)


def exact_weight_term(left, right):
    return jnp.einsum(
        "rtd,rte->de", left, right, precision=highest, preferred_element_type=jnp.float32
    )


def exact_back_project(gradient, weight):
    return jnp.einsum(
        "rte,de->rtd", gradient, weight, precision=highest, preferred_element_type=jnp.float32
    )


def split_heads(values):
    return values.reshape(values.shape[0], values.shape[1], values.shape[2] // HD, HD)


def clip_of(positions, clip_ends):
    return jnp.sum((positions[None, :, None] >= clip_ends[:, None, :]).astype(jnp.int32), axis=2)


def pair_mask(query_pos, query_clip, key_pos, key_clip):
    causal = query_pos[None, :, None] >= key_pos[None, None, :]
    return (causal & (query_clip[:, :, None] == key_clip[:, None, :]))[:, None]


def blocks_of(arrived, frame_span):
    block_count = arrived.shape[1] // frame_span
    shaped = arrived.reshape((arrived.shape[0], block_count, frame_span) + arrived.shape[2:])
    return jnp.moveaxis(shaped, 1, 0)


def block_fold(visit_block, frame_span, carried, arrived):
    block_count = arrived.shape[1] // frame_span
    starts = frame_span * jnp.arange(block_count, dtype=jnp.int32)

    def scan_step(state, block_pair):
        return (visit_block(state, block_pair[0], block_pair[1]), None)

    carried, unused = lax.scan(scan_step, carried, (blocks_of(arrived, frame_span), starts))
    return carried


def head_dot(gradient, output):
    summed = jnp.sum(split_heads(gradient).astype(jnp.float32) * split_heads(output), axis=3)
    return jnp.swapaxes(summed, 1, 2)


def text_project(texts, w_text):
    return jnp.concatenate([project(texts, w_text[0]), project(texts, w_text[1])], axis=2).astype(
        jnp.bfloat16
    )


def self_forward(queries, key_value, clip_ends, clip_ids, frames):
    row_count, frame_span, model_width = queries.shape
    head_count = model_width // HD
    score_scale = HD ** (-0.5)
    query_heads = split_heads(queries)
    last_frame = frames[frame_span - 1]

    def visit_block(state, key_block, first_key):
        key_pos = first_key + jnp.arange(frame_span, dtype=jnp.int32)

        def accumulate(carried):
            running_max, running_sum, output_sum = carried
            key_heads = split_heads(key_block[:, :, :model_width])
            value_heads = split_heads(key_block[:, :, model_width:])
            allowed = pair_mask(frames, clip_ids, key_pos, clip_of(key_pos, clip_ends))
            scores = (
                jnp.einsum(
                    "rqhd,rkhd->rhqk", query_heads, key_heads, preferred_element_type=jnp.float32
                )
                * score_scale
            )
            scores = jnp.where(allowed, scores, masked_score)
            new_max = jnp.maximum(running_max, jnp.max(scores, axis=3))
            weights = jnp.where(allowed, jnp.exp(scores - new_max[..., None]), 0.0)
            shrink = jnp.exp(running_max - new_max)
            running_sum = running_sum * shrink + jnp.sum(weights, axis=3)
            output_sum = output_sum * shrink[..., None] + jnp.einsum(
                "rhqk,rkhd->rhqd",
                weights.astype(jnp.bfloat16),
                value_heads,
                preferred_element_type=jnp.float32,
            )
            return (new_max, running_sum, output_sum)

        return lax.cond(first_key > last_frame, lambda carried: carried, accumulate, state)

    initial = (
        jnp.full((row_count, head_count, frame_span), masked_score, jnp.float32),
        jnp.zeros((row_count, head_count, frame_span), jnp.float32),
        jnp.zeros((row_count, head_count, frame_span, HD), jnp.float32),
    )
    running_max, running_sum, output_sum = block_fold(
        visit_block, frame_span, initial, lax.all_gather(key_value, "seq", axis=1, tiled=True)
    )
    attended = output_sum / running_sum[..., None]
    return (
        jnp.swapaxes(attended, 1, 2).reshape(row_count, frame_span, model_width),
        running_max + jnp.log(running_sum),
    )


def self_query_grad(queries, key_value, clip_ends, clip_ids, frames, log_norm, delta_sum, d_attn):
    row_count, frame_span, model_width = queries.shape
    head_count = model_width // HD
    score_scale = HD ** (-0.5)
    query_heads = split_heads(queries)
    grad_heads = split_heads(d_attn)
    last_frame = frames[frame_span - 1]

    def visit_block(state, key_block, first_key):
        key_pos = first_key + jnp.arange(frame_span, dtype=jnp.int32)

        def accumulate(carried):
            key_heads = split_heads(key_block[:, :, :model_width])
            value_heads = split_heads(key_block[:, :, model_width:])
            allowed = pair_mask(frames, clip_ids, key_pos, clip_of(key_pos, clip_ends))
            scores = (
                jnp.einsum(
                    "rqhd,rkhd->rhqk", query_heads, key_heads, preferred_element_type=jnp.float32
                )
                * score_scale
            )
            probability = jnp.where(allowed, jnp.exp(scores - log_norm[..., None]), 0.0)
            d_prob = jnp.einsum(
                "rqhd,rkhd->rhqk", grad_heads, value_heads, preferred_element_type=jnp.float32
            )
            d_score = (probability * (d_prob - delta_sum[..., None])).astype(jnp.bfloat16)
            return carried + jnp.einsum(
                "rhqk,rkhd->rhqd", d_score, key_heads, preferred_element_type=jnp.float32
            )

        return lax.cond(first_key > last_frame, lambda carried: carried, accumulate, state)

    initial = jnp.zeros((row_count, head_count, frame_span, HD), jnp.float32)
    d_query = block_fold(
        visit_block, frame_span, initial, lax.all_gather(key_value, "seq", axis=1, tiled=True)
    )
    d_query = jnp.swapaxes(d_query, 1, 2).reshape(row_count, frame_span, model_width) * score_scale
    return d_query.astype(jnp.bfloat16)


def self_key_grad(query_grad, key_value, clip_ends, clip_ids, frames, gathered_stats):
    row_count, frame_span, double_width = key_value.shape
    model_width = double_width // 2
    head_count = model_width // HD
    score_scale = HD ** (-0.5)
    key_heads = split_heads(key_value[:, :, :model_width])
    value_heads = split_heads(key_value[:, :, model_width:])
    all_norm, all_delta = gathered_stats
    first_own = frames[0]

    def visit_block(state, query_block, first_query):
        query_pos = first_query + jnp.arange(frame_span, dtype=jnp.int32)

        def accumulate(carried):
            d_key, d_value = carried
            query_heads = split_heads(query_block[:, :, :model_width])
            grad_heads = split_heads(query_block[:, :, model_width:])
            log_norm = jnp.swapaxes(
                lax.dynamic_slice_in_dim(all_norm, first_query, frame_span, 1), 1, 2
            )
            delta_sum = jnp.swapaxes(
                lax.dynamic_slice_in_dim(all_delta, first_query, frame_span, 1), 1, 2
            )
            allowed = pair_mask(query_pos, clip_of(query_pos, clip_ends), frames, clip_ids)
            scores = (
                jnp.einsum(
                    "rqhd,rkhd->rhqk", query_heads, key_heads, preferred_element_type=jnp.float32
                )
                * score_scale
            )
            probability = jnp.where(allowed, jnp.exp(scores - log_norm[..., None]), 0.0)
            d_value = d_value + jnp.einsum(
                "rhqk,rqhd->rhkd",
                probability.astype(jnp.bfloat16),
                grad_heads,
                preferred_element_type=jnp.float32,
            )
            d_prob = jnp.einsum(
                "rqhd,rkhd->rhqk", grad_heads, value_heads, preferred_element_type=jnp.float32
            )
            d_score = (probability * (d_prob - delta_sum[..., None])).astype(jnp.bfloat16)
            d_key = d_key + jnp.einsum(
                "rhqk,rqhd->rhkd", d_score, query_heads, preferred_element_type=jnp.float32
            )
            return (d_key, d_value)

        return lax.cond(
            first_query + frame_span - 1 < first_own, lambda carried: carried, accumulate, state
        )

    zeros_heads = jnp.zeros((row_count, head_count, frame_span, HD), jnp.float32)
    d_key, d_value = block_fold(
        visit_block,
        frame_span,
        (zeros_heads, zeros_heads),
        lax.all_gather(query_grad, "seq", axis=1, tiled=True),
    )
    d_key = jnp.swapaxes(d_key, 1, 2).reshape(row_count, frame_span, model_width) * score_scale
    d_value = jnp.swapaxes(d_value, 1, 2).reshape(row_count, frame_span, model_width)
    return (d_key.astype(jnp.bfloat16), d_value.astype(jnp.bfloat16))


def cross_forward(queries, text_kv, readable):
    row_count, frame_span, model_width = queries.shape
    group_width = group_heads * HD
    score_scale = HD ** (-0.5)
    outputs = []
    log_norms = []
    for group_index in range(model_width // group_width):
        lower_edge = group_index * group_width
        query_heads = split_heads(queries[:, :, lower_edge : lower_edge + group_width])
        key_heads = split_heads(text_kv[:, :, lower_edge : lower_edge + group_width])
        value_heads = split_heads(
            text_kv[:, :, model_width + lower_edge : model_width + lower_edge + group_width]
        )
        scores = (
            jnp.einsum(
                "rqhd,rkhd->rhqk", query_heads, key_heads, preferred_element_type=jnp.float32
            )
            * score_scale
        )
        scores = jnp.where(readable, scores, masked_score)
        largest = jnp.max(scores, axis=3)
        weights = jnp.where(readable, jnp.exp(scores - largest[..., None]), 0.0)
        totals = jnp.sum(weights, axis=3)
        probability = (weights / totals[..., None]).astype(jnp.bfloat16)
        attended = jnp.einsum(
            "rhqk,rkhd->rqhd", probability, value_heads, preferred_element_type=jnp.float32
        )
        outputs.append(attended.reshape(row_count, frame_span, group_width))
        log_norms.append(largest + jnp.log(totals))
    return (jnp.concatenate(outputs, axis=2), jnp.concatenate(log_norms, axis=1))


def cross_backward(queries, text_kv, readable, log_norm, d_cross, delta_sum):
    row_count, frame_span, model_width = queries.shape
    slot_count = text_kv.shape[1]
    group_width = group_heads * HD
    score_scale = HD ** (-0.5)
    d_queries = []
    d_keys = []
    d_values = []
    for group_index in range(model_width // group_width):
        lower_edge = group_index * group_width
        head_edge = group_index * group_heads
        query_heads = split_heads(queries[:, :, lower_edge : lower_edge + group_width])
        grad_heads = split_heads(d_cross[:, :, lower_edge : lower_edge + group_width])
        key_heads = split_heads(text_kv[:, :, lower_edge : lower_edge + group_width])
        value_heads = split_heads(
            text_kv[:, :, model_width + lower_edge : model_width + lower_edge + group_width]
        )
        group_norm = log_norm[:, head_edge : head_edge + group_heads]
        group_delta = delta_sum[:, head_edge : head_edge + group_heads]
        scores = (
            jnp.einsum(
                "rqhd,rkhd->rhqk", query_heads, key_heads, preferred_element_type=jnp.float32
            )
            * score_scale
        )
        probability = jnp.where(readable, jnp.exp(scores - group_norm[..., None]), 0.0)
        d_value = jnp.einsum(
            "rhqk,rqhd->rkhd",
            probability.astype(jnp.bfloat16),
            grad_heads,
            preferred_element_type=jnp.float32,
        )
        d_values.append(d_value.reshape(row_count, slot_count, group_width))
        d_prob = jnp.einsum(
            "rqhd,rkhd->rhqk", grad_heads, value_heads, preferred_element_type=jnp.float32
        )
        d_score = (probability * (d_prob - group_delta[..., None])).astype(jnp.bfloat16)
        d_query = jnp.einsum(
            "rhqk,rkhd->rqhd", d_score, key_heads, preferred_element_type=jnp.float32
        )
        d_queries.append(d_query.reshape(row_count, frame_span, group_width) * score_scale)
        d_key = jnp.einsum(
            "rhqk,rqhd->rkhd", d_score, query_heads, preferred_element_type=jnp.float32
        )
        d_keys.append(d_key.reshape(row_count, slot_count, group_width) * score_scale)
    return (jnp.concatenate(d_queries, axis=2), jnp.concatenate(d_keys + d_values, axis=2))


def shards(
    hidden_in,
    clip_lengths,
    text_lengths,
    text_states,
    norm_gain,
    norm_bias,
    self_qkv,
    self_out,
    cross_query,
    cross_kv,
    cross_out,
    ffn_in,
    ffn_out,
    out_grad,
):
    gathered = (
        lax.all_gather(norm_gain, ("rows", "seq"), axis=1, tiled=True),
        lax.all_gather(norm_bias, ("rows", "seq"), axis=1, tiled=True),
        lax.all_gather(self_qkv, ("rows", "seq"), axis=1, tiled=True),
        lax.all_gather(self_out, ("rows", "seq"), axis=0, tiled=True),
        lax.all_gather(cross_query, ("rows", "seq"), axis=0, tiled=True),
        lax.all_gather(cross_kv, ("rows", "seq"), axis=1, tiled=True),
        lax.all_gather(cross_out, ("rows", "seq"), axis=0, tiled=True),
        lax.all_gather(ffn_in, ("rows", "seq"), axis=0, tiled=True),
        lax.all_gather(ffn_out, ("rows", "seq"), axis=0, tiled=True),
    )
    gains_all, biases_all, w_qkv, w_self, w_query, w_text, w_cross, w_up, w_down = gathered
    gains = gains_all.astype(jnp.float32)
    biases = biases_all.astype(jnp.float32)
    row_count, frame_span, model_width = hidden_in.shape
    seq_index = lax.axis_index("seq")
    frames = seq_index * frame_span + jnp.arange(frame_span, dtype=jnp.int32)
    clip_ends = jnp.cumsum(clip_lengths, axis=1)
    clip_ids = clip_of(frames, clip_ends)
    text_ends = jnp.cumsum(text_lengths, axis=1)
    text_starts = text_ends - text_lengths
    chosen = (
        clip_ids[:, :, None] == jnp.arange(clip_lengths.shape[1], dtype=jnp.int32)[None, None, :]
    )
    slot_low = jnp.sum(jnp.where(chosen, text_starts[:, None, :], 0), axis=2)
    slot_high = jnp.sum(jnp.where(chosen, text_ends[:, None, :], 0), axis=2)
    slot_index = jnp.arange(text_states.shape[1], dtype=jnp.int32)
    readable = (
        (slot_index[None, None, :] >= slot_low[:, :, None])
        & (slot_index[None, None, :] < slot_high[:, :, None])
    )[:, None]
    slot_share = text_states.shape[1] // lax.axis_size("seq")
    own_text = lax.dynamic_slice_in_dim(text_states, seq_index * slot_share, slot_share, 1)
    resid = hidden_in.astype(jnp.float32)
    normed_full, pull_first = jax.vjp(layer_norm, resid, gains[0], biases[0])
    normed = normed_full.astype(jnp.bfloat16)
    queries = project(normed, w_qkv[0]).astype(jnp.bfloat16)
    keys_low = project(normed, w_qkv[1]).astype(jnp.bfloat16)
    values_low = project(normed, w_qkv[2]).astype(jnp.bfloat16)
    key_value = jnp.concatenate([keys_low, values_low], axis=2)
    self_full, self_norm = self_forward(queries, key_value, clip_ends, clip_ids, frames)
    attended = self_full.astype(jnp.bfloat16)
    after_self = resid + project(attended, w_self)
    normed_full, pull_second = jax.vjp(layer_norm, after_self, gains[1], biases[1])
    normed_two = normed_full.astype(jnp.bfloat16)
    cross_queries = project(normed_two, w_query).astype(jnp.bfloat16)
    text_kv = lax.all_gather(text_project(own_text, w_text), "seq", axis=1, tiled=True)
    cross_full, cross_norm = cross_forward(cross_queries, text_kv, readable)
    crossed = cross_full.astype(jnp.bfloat16)
    after_cross = after_self + project(crossed, w_cross)
    normed_full, pull_third = jax.vjp(layer_norm, after_cross, gains[2], biases[2])
    normed_three = normed_full.astype(jnp.bfloat16)
    hidden_up = project(normed_three, w_up)
    activated_full, pull_gelu = jax.vjp(gelu_exact, hidden_up)
    activated = activated_full.astype(jnp.bfloat16)
    block_out = (after_cross + project(activated, w_down)).astype(jnp.bfloat16)
    gradient = out_grad.astype(jnp.float32)
    g_down = weight_term(activated, out_grad)
    d_up = pull_gelu(back_project(out_grad, w_down))[0].astype(jnp.bfloat16)
    g_up = weight_term(normed_three, d_up)
    d_third, g_gain_three, g_bias_three = pull_third(back_project(d_up, w_up))
    gradient = gradient + d_third
    grad_low = gradient.astype(jnp.bfloat16)
    g_cross = weight_term(crossed, grad_low)
    d_cross = back_project(grad_low, w_cross).astype(jnp.bfloat16)
    cross_delta = head_dot(d_cross, cross_full)
    d_cross_query, d_text_kv = cross_backward(
        cross_queries, text_kv, readable, cross_norm, d_cross, cross_delta
    )
    key_weight = w_text[0].astype(jnp.float32)
    value_weight = w_text[1].astype(jnp.float32)
    own_grad = lax.psum_scatter(
        d_text_kv.astype(jnp.bfloat16), "seq", scatter_dimension=1, tiled=True
    ).astype(jnp.float32)
    grad_text_key = own_grad[:, :, :model_width]
    grad_text_value = own_grad[:, :, model_width:]
    own_exact = own_text.astype(jnp.float32)
    g_text = jnp.stack(
        [exact_weight_term(own_exact, grad_text_key), exact_weight_term(own_exact, grad_text_value)]
    )
    text_grad = exact_back_project(grad_text_key, key_weight) + exact_back_project(
        grad_text_value, value_weight
    )
    d_cross_query = d_cross_query.astype(jnp.bfloat16)
    g_query = weight_term(normed_two, d_cross_query)
    d_second, g_gain_two, g_bias_two = pull_second(back_project(d_cross_query, w_query))
    gradient = gradient + d_second
    grad_low = gradient.astype(jnp.bfloat16)
    g_self = weight_term(attended, grad_low)
    d_attn = back_project(grad_low, w_self).astype(jnp.bfloat16)
    self_delta = head_dot(d_attn, self_full)
    d_query = self_query_grad(
        queries, key_value, clip_ends, clip_ids, frames, self_norm, self_delta, d_attn
    )
    gathered_stats = (
        lax.all_gather(jnp.swapaxes(self_norm, 1, 2), "seq", axis=1, tiled=True),
        lax.all_gather(jnp.swapaxes(self_delta, 1, 2), "seq", axis=1, tiled=True),
    )
    query_grad = jnp.concatenate([queries, d_attn], axis=2)
    d_key, d_value = self_key_grad(
        query_grad, key_value, clip_ends, clip_ids, frames, gathered_stats
    )
    g_qkv = jnp.stack(
        [weight_term(normed, d_query), weight_term(normed, d_key), weight_term(normed, d_value)]
    )
    d_normed = (
        back_project(d_query, w_qkv[0])
        + back_project(d_key, w_qkv[1])
        + back_project(d_value, w_qkv[2])
    )
    d_first, g_gain_one, g_bias_one = pull_first(d_normed)
    input_grad = gradient + d_first
    g_gain = jnp.stack([g_gain_one, g_gain_two, g_gain_three])
    g_bias = jnp.stack([g_bias_one, g_bias_two, g_bias_three])
    reduced = (
        lax.psum_scatter(g_gain, ("rows", "seq"), scatter_dimension=1, tiled=True),
        lax.psum_scatter(g_bias, ("rows", "seq"), scatter_dimension=1, tiled=True),
        lax.psum_scatter(g_qkv, ("rows", "seq"), scatter_dimension=1, tiled=True),
        lax.psum_scatter(g_self, ("rows", "seq"), scatter_dimension=0, tiled=True),
        lax.psum_scatter(g_query, ("rows", "seq"), scatter_dimension=0, tiled=True),
        lax.psum_scatter(g_text, ("rows", "seq"), scatter_dimension=1, tiled=True),
        lax.psum_scatter(g_cross, ("rows", "seq"), scatter_dimension=0, tiled=True),
        lax.psum_scatter(g_up, ("rows", "seq"), scatter_dimension=0, tiled=True),
        lax.psum_scatter(g_down, ("rows", "seq"), scatter_dimension=0, tiled=True),
    )
    return (
        block_out,
        input_grad,
        text_grad,
        reduced[0],
        reduced[1],
        reduced[2],
        reduced[3],
        reduced[4],
        reduced[5],
        reduced[6],
        reduced[7],
        reduced[8],
    )


MESH = pl.DeviceIdType.MESH
BF = jnp.bfloat16
F32 = jnp.float32
GROUP = 4
NEG = -1e30


def dot(a, b):
    return lax.dot_general(a, b, (((1,), (0,)), ((), ())), preferred_element_type=F32)


def dot_nt(a, b):
    return lax.dot_general(a, b, (((1,), (1,)), ((), ())), preferred_element_type=F32)


def dot_tn(a, b):
    return lax.dot_general(a, b, (((0,), (0,)), ((), ())), preferred_element_type=F32)


def mult(index, step):
    return pl.multiple_of(index * step, step)


def rows_of(index, step):
    return pl.ds(mult(index, step), step)


def each(count, step, body):
    def turn(i, carry):
        body(pl.ds(pl.multiple_of(i * step, step), step))
        return carry

    lax.fori_loop(0, count // step, turn, 0)


def three_parts(value):
    first = value.astype(BF).astype(F32)
    rest = value - first
    second = rest.astype(BF).astype(F32)
    return first, second, (rest - second).astype(BF).astype(F32)


def normalise(values):
    average = jnp.mean(values, axis=-1, keepdims=True)
    centred = values - average
    rstd = lax.rsqrt(jnp.mean(centred * centred, axis=-1, keepdims=True) + epsilon)
    return centred * rstd, rstd


def semaphore_plan(group_chips):
    sizes = dict(
        gb_s=8, gb_r=4, q_s=8, q_r=4, kv_s=8, kv_r=4, in_s=8, in_r=4, ow_g=8, ow_r=4, ow_x=4 * 8,
        n1=24, og=16, n3=16, a_at=8, a_cq=8, a_cr=8, b_cr=8, b_cq=8, b_at=8,
        e_c=4, e_z=4, o_c=4, o_z=4, t_c=4, t_z=8, s_c=4, s_z=8,
        gq_r=8, gq_s=8, gi_r=8, gi_s=8, go_r=8, go_g=8, gk_r=8, gk_s=8, gg_r=4, gg_s=8,
        m_z=12, m_r=12, m_c=6, h_c=6, h_r=24, h_z=24,
    )
    base, plan = 0, {}
    for name, size in sizes.items():
        plan[name] = base
        base += size
    return types.SimpleNamespace(**plan), base


def layer_kernel(plan, names, *refs):
    n = types.SimpleNamespace(**dict(zip(names, refs)))
    R, S, NZ, D = 4, 8, 4, n.x.shape[1]
    TB = n.x.shape[0]
    CH = 2 * TB
    T = S * TB
    HP = D // S
    FF = n.win.shape[1]
    G = GROUP
    GZ = G // 2
    E = S // G
    U = FF // G
    UB = FF // (R * S)
    DB = D // (R * S)
    TW = n.text.shape[1]
    KB = n.wckv.shape[0]
    r, s = lax.axis_index("rows"), lax.axis_index("seq")
    z, c = s // 2, s % 2
    sib = s + 1 - 2 * c
    ffn_z0 = (z // GZ) * GZ
    grp, mem = s // G, s % G
    ss, rs = n.ss, n.rs
    pending = {}
    gbt, Wq3, Wkv3, Win, Wout, winp, ogf = n.gbt, n.Wq3, n.Wkv3, n.Win, n.Wout, n.winp, n.ogf
    mats = [n.Wm0, n.Wm1, n.Wm2]

    def push(src, dst, name, to, origin, dev, send_shift=0, when=None):
        cp = pltpu.make_async_remote_copy(
            src_ref=src, dst_ref=dst,
            send_sem=ss.at[name + send_shift + to],
            recv_sem=rs.at[name + origin],
            device_id=dev, device_id_type=MESH,
        )
        pending.setdefault(name, []).append((cp, when))
        if when is None:
            cp.start()
        else:
            pl.when(when)(cp.start)

    def drain(*which):
        for name in which:
            for cp, when in pending.pop(name, []):
                if when is None:
                    cp.wait_send()
                else:
                    pl.when(when)(cp.wait_send)

    def arrive(landing, name, origin, when=None):
        cp = pltpu.make_async_remote_copy(
            src_ref=landing, dst_ref=landing, send_sem=ss.at[name],
            recv_sem=rs.at[name + origin], device_id=(r, sib), device_id_type=MESH,
        )
        if when is None:
            cp.wait_recv()
        else:
            pl.when(when)(cp.wait_recv)

    side = z // 2
    inner, outer = (z + 1) % NZ // 2 == 1, (z + 1) % NZ // 2 == 0
    beside = z + 1 - 2 * (z % 2)
    far_inner, far_outer = 2 - side, 3 - 3 * side
    across_x, across_y = r + 1 - 2 * (r % 2), (r + 2) % R
    corner = (across_x + 2) % R

    def plane_start(block, name):
        push(block(r), block(r), name, 0, 0, (across_x, s))
        push(block(r), block(r), name, 1, 1, (across_y, s))

    def plane_pass(block, half, name):
        arrive(block(across_x), name, 0)
        push(half(across_x, 0), half(across_x, 0), name, 2, 2, (across_y, s))
        arrive(block(across_y), name, 1)
        push(half(across_y, 1), half(across_y, 1), name, 3, 3, (across_x, s))

    def plane_take(half, name):
        arrive(half(corner, 0), name, 2)
        arrive(half(corner, 1), name, 3)

    def fold_start(half, landed, name):
        push(half(corner, 0), landed.at[1], name, 1, 1, (across_x, s))
        push(half(corner, 1), landed.at[3], name, 3, 3, (across_y, s))
        push(half(across_x, 0), landed.at[0], name, 0, 0, (across_x, s))
        push(half(across_y, 1), landed.at[2], name, 2, 2, (across_y, s))

    def fold_pass(half, landed, name):
        for k, (near, to) in enumerate(((across_y, across_y), (across_x, across_x))):
            arrive(landed.at[1 + 2 * k], name, 1 + 2 * k)
            mine = half(near, k)
            mine[...] = (mine[...].astype(F32) + landed[1 + 2 * k].astype(F32)).astype(BF)
            push(mine, landed.at[4 + k], name, 4 + k, 4 + k, (to, s))

    def fold_take(half, landed, name):
        for k in range(2):
            arrive(landed.at[2 * k], name, 2 * k)
            arrive(landed.at[4 + k], name, 4 + k)
            mine = half(r, k)
            total = mine[...].astype(F32) + landed[2 * k].astype(F32) + landed[4 + k].astype(F32)
            mine[...] = total.astype(BF)

    def rows_view(ref, step):
        def block(p):
            return ref.at[rows_of(p, step), :]

        def half(p, k):
            return ref.at[rows_of(2 * p + k, step // 2), :]

        return block, half

    def mid_view(ref, step):
        def block(p):
            return ref.at[:, rows_of(p, step), :]

        def half(p, k):
            return ref.at[:, rows_of(2 * p + k, step // 2), :]

        return block, half

    def mat_view(i):
        def block(p):
            return mats[i].at[pl.ds(p * NZ, NZ), c]

        def half(p, k):
            return mats[i].at[pl.ds(p * NZ + 2 * k, 2), c]

        return block, half

    def out_view(j):
        def block(p):
            return Wout.at[rows_of(p * E + (grp + j) % E, UB), :]

        def half(p, k):
            return Wout.at[rows_of(2 * (p * E + (grp + j) % E) + k, UB // 2), :]

        return block, half

    seq_peers = [(s + k) % S for k in range(1, S)]
    row_peers = [(r + k) % R for k in range(1, R)]
    z_peers = [(z + k) % NZ for k in range(1, NZ)]

    finals = []

    def local(src, dst, i):
        cp = pltpu.make_async_copy(src, dst, n.ls.at[i])
        cp.start()
        return cp

    def emit(stage, out, value):
        stage[...] = value
        finals.append(local(stage, out, 16 + len(finals)))

    own_mats = [n.wo, n.wcq, n.wco]
    own_rows = rows_of(r * S + s, DB)
    kv_rows = rows_of(r * S + s, KB)
    out_rows = rows_of(r * E + grp, UB)
    xs, own_tokens = n.ps0, rows_of(s, TB)
    got_x = local(n.x, xs.at[own_tokens, :], 0)
    got_gb = local(n.gb, gbt.at[r, s], 1)
    got_q = local(n.wqkv.at[:, :, rows_of(s, HP)], Wq3.at[:, own_rows, :], 2)
    got_kv = local(n.wckv.at[:, rows_of(s, HP)], Wkv3.at[kv_rows, :], 3)
    got_mats = [local(own_mats[i], mats[i].at[r * NZ + z, c], 4 + i) for i in range(3)]
    for m in range(G):
        for rr in range(R):
            for j in range(E):
                b = rr * S + j * G + m
                at = m * U + (rr * E + j) * UB
                local(n.win.at[:, b * UB : (b + 1) * UB], winp.at[:, at : at + UB], 7)
    got_ow = local(n.wout, Wout.at[out_rows, :], 8)
    got_og = local(n.og, ogf.at[rows_of(mem, TB), :], 9)
    got_text = local(n.text, n.textv, 10)

    barrier = pltpu.get_barrier_semaphore()
    for p in seq_peers:
        pl.semaphore_signal(barrier, inc=1, device_id=(r, p), device_id_type=MESH)
    for p in row_peers:
        pl.semaphore_signal(barrier, inc=1, device_id=(p, s), device_id_type=MESH)
    pl.semaphore_wait(barrier, S + R - 2)

    for p in seq_peers:
        push(n.gb, gbt.at[r, s], plan.gb_s, p, s, (r, p))
    for p in seq_peers:
        push(n.wqkv.at[:, :, rows_of(p, HP)], Wq3.at[:, own_rows, :], plan.q_s, p, s, (r, p))

    def mat_z(i):
        for p in z_peers:
            push(own_mats[i], mats[i].at[r * NZ + z, c], plan.m_z + 4 * i, p, z, (r, 2 * p + c))

    def mat_r(i):
        for p in z_peers:
            arrive(mats[i].at[r * NZ + p, c], plan.m_z + 4 * i, p)
        got_mats[i].wait()
        plane_start(mat_view(i)[0], plan.m_r + 4 * i)

    def mat_p(i):
        plane_pass(*mat_view(i), plan.m_r + 4 * i)

    def mat_c(i):
        plane_take(mat_view(i)[1], plan.m_r + 4 * i)
        block = mats[i].at[:, c]
        push(block, block, plan.m_c + 2 * i, 0, 0, (r, sib))

    def mat_take(i):
        arrive(mats[i].at[:, 1 - c], plan.m_c + 2 * i, 0)

    def mat(i):
        return mats[i][...].reshape(D, D)

    mat_z(0)
    for zl in (far_inner, beside):
        push(n.x, xs.at[own_tokens, :], plan.n1, 2 * zl + c, s, (r, 2 * zl + c))
    push(n.x, xs.at[own_tokens, :], plan.n1, sib, s, (r, sib))

    for p in seq_peers:
        arrive(gbt.at[r, p], plan.gb_s, p)
    got_gb.wait()
    for p in row_peers:
        push(gbt.at[r], gbt.at[r], plan.gb_r, p, r, (p, s))
    q_block, q_half = mid_view(Wq3, S * DB)
    kv_block, kv_half = rows_view(Wkv3, S * KB)
    in_block, in_half = rows_view(Win, S * DB)
    ow_block, ow_half = out_view(0)
    push(n.wout, ow_block(r), plan.ow_r, 0, 0, (across_x, s))
    push(n.wout, ow_block(r), plan.ow_r, 1, 1, (across_y, s))
    for p in seq_peers:
        arrive(Wq3.at[:, rows_of(r * S + p, DB), :], plan.q_s, p)
    got_q.wait()
    plane_start(q_block, plan.q_r)

    lane = lax.broadcasted_iota(jnp.int32, (T, HP), 1)
    row = lax.broadcasted_iota(jnp.int32, (T, HP), 0)
    slot = lane % HD
    cl, tl = n.cl, n.tl

    def inside(lengths):
        low, found = jnp.int32(0), jnp.zeros((T, HP), jnp.bool_)
        for k in range(4):
            high = low + lengths[0, k]
            found = found | ((slot == k) & (row >= low) & (row < high))
            low = high
        return found

    ones_tail = jnp.where((slot >= 4) & (slot < 7), 1.0, 0.0)

    def mask_block():
        in_clip = inside(cl)
        n.oh[...] = jnp.where(in_clip, 1.0, 0.0).astype(BF)
        n.kbs[...] = jnp.where(slot < 4, jnp.where(in_clip, 0.0, NEG), ones_tail).astype(BF)
        n.kbc[...] = jnp.where(slot < 4, jnp.where(inside(tl), 0.0, NEG), ones_tail).astype(BF)

    mask_block()

    for p in row_peers:
        arrive(gbt.at[p], plan.gb_r, p)
    per = 128 // DB
    gbf = n.gbf
    for g in range(D // 128):
        total = None
        for k in range(per):
            rr, sx = divmod(g * per + k, S)
            tile = gbt[rr, sx].astype(F32)
            total = tile if total is None else total + tile
        gbf[:, g * 128 : (g + 1) * 128] = total

    def gain(i):
        return gbf[i : i + 1, :]

    def bias(i):
        return gbf[3 + i : 4 + i, :]

    def first_half(shape):
        return lax.broadcasted_iota(jnp.int32, shape, 1) < HD

    def split_pair(value, other):
        front = first_half(value.shape)
        v, o = value.astype(F32), other.astype(F32)
        return jnp.where(front, v, o).astype(BF), jnp.where(front, o, v).astype(BF)

    def gather_start(buf, name, z0, nz):
        m = s - 2 * z0
        block = buf.at[rows_of(m, TB), :]
        for k in range(1, nz):
            zl = (z - z0 + k) % nz
            push(block, block, name, 2 * zl + c, m, (r, 2 * (z0 + zl) + c))
        push(block, block, name, sib - 2 * z0, m, (r, sib))

    def gather_pass(buf, name, z0, nz, k):
        zl = (z - z0 + k) % nz
        if k:
            block = buf.at[rows_of(2 * zl + c, TB), :]
            arrive(block, name, 2 * zl + c)
            push(block, block, name, 2 * zl + c, 2 * zl + c, (r, sib), send_shift=8)

    def gather_take(buf, name, z0, nz, k):
        zl = (z - z0 + k) % nz
        arrive(buf.at[rows_of(2 * zl + 1 - c, TB), :], name, 2 * zl + 1 - c)
        return rows_of(zl, CH)

    def chain_pass(buf, name, zl):
        origin = 2 * zl + c
        block = buf.at[rows_of(origin, TB), :]
        arrive(block, name, origin)
        push(block, block, name, 16 + origin, origin, (r, 2 * beside + c), when=inner & (zl // 2 != side))
        push(block, block, name, 8 + origin, origin, (r, sib))

    def chain_take(buf, name, zl):
        arrive(buf.at[rows_of(2 * zl + 1 - c, TB), :], name, 2 * zl + 1 - c)
        return rows_of(zl, CH)

    n1f, Wq = n.n1f, n.Wq
    Q, K, V = n.Q, n.K, n.V
    KA = n.KA
    scale = HD ** (-0.5)

    def norm_rows(rows):
        xh = normalise(xs[rows, :].astype(F32))[0]
        n1f[rows, :] = (xh * gain(0) + bias(0)).astype(BF)

    def qkv_chunk(rows):
        def block():
            qkv_block(rows)

        block()

    def qkv_block(rows):
        got = dot(n1f[rows, :], Wq[...])
        Q[rows, :] = (got[:, :HP].astype(BF).astype(F32) * scale).astype(BF)
        K[rows, :] = got[:, HP : 2 * HP].astype(BF)
        V[rows, :] = got[:, 2 * HP :].astype(BF)
        KA[0, rows, :], KA[1, rows, :] = split_pair(K[rows, :], n.kbs[rows, :])

    got_x.wait()
    arrive(xs.at[rows_of(sib, TB), :], plan.n1, sib)
    rows = rows_of(z, CH)
    norm_rows(rows)
    mat_r(0)
    plane_pass(q_block, q_half, plan.q_r)
    chain_pass(xs, plan.n1, far_inner)
    rows_1 = chain_take(xs, plan.n1, far_inner)
    norm_rows(rows_1)
    plane_pass(ow_block, ow_half, plan.ow_r)
    chain_pass(xs, plan.n1, far_outer)
    mat_z(1)
    for p in seq_peers:
        push(n.wckv.at[:, rows_of(p, HP)], Wkv3.at[kv_rows, :], plan.kv_s, p, s, (r, p))
    mat_z(2)
    rows_2 = chain_take(xs, plan.n1, far_outer)
    norm_rows(rows_2)
    mat_p(0)
    plane_take(q_half, plan.q_r)
    for i in range(3):
        Wq[:, i * HP : (i + 1) * HP] = Wq3[i]
    qkv_chunk(rows)
    qkv_chunk(rows_1)
    qkv_chunk(rows_2)
    chain_pass(xs, plan.n1, beside)
    rows = chain_take(xs, plan.n1, beside)
    norm_rows(rows)
    qkv_chunk(rows)
    mat_c(0)
    pltpu.make_async_copy(n.win, winp, n.ls.at[7]).wait()
    Win[own_rows, :] = winp[:, rows_of(mem, U)]

    AF, QB = n.AF, n.QB
    oh = n.oh
    AB = n.out
    ao = n.ao

    def finish(o0, o1, l0, l1):
        return jnp.where(first_half(o0.shape), o0 / l0, o1 / l1)

    def with_norm(q_aug, head, norm):
        spot = lax.broadcasted_iota(jnp.int32, q_aug.shape, 1)
        base = (1 - head) * HD
        a, b, d = three_parts(-norm)
        w = q_aug.astype(F32)
        w = jnp.where(spot == base + 4, a, w)
        w = jnp.where(spot == base + 5, b, w)
        return jnp.where(spot == base + 6, d, w).astype(BF)

    kpos = lax.broadcasted_iota(jnp.int32, (CH, CH), 1)
    qpos = lax.broadcasted_iota(jnp.int32, (CH, CH), 0)
    def self_rows(i, low, high):
        qa = split_pair(Q[low:high, :], oh[low:high, :])
        outs, sums = [], []
        for h in range(2):
            diag = jnp.where(kpos <= qpos, dot_nt(qa[h], KA[h, low:high, :]), NEG)
            top = jnp.max(diag, axis=1, keepdims=True)
            if i:
                left = dot_nt(qa[h], KA[h, :low, :])
                top = jnp.maximum(top, jnp.max(left, axis=1, keepdims=True))
            diag = jnp.exp(diag - top)
            total = jnp.sum(diag, axis=1, keepdims=True)
            got = dot(diag.astype(BF), V[low:high, :])
            if i:
                left = jnp.exp(left - top)
                total = total + jnp.sum(left, axis=1, keepdims=True)
                got = got + dot(left.astype(BF), V[:low, :])
            outs.append(got)
            sums.append(total)
            QB[h, low:high, :] = with_norm(qa[h], h, top + jnp.log(total))
        full = finish(outs[0], outs[1], sums[0], sums[1])
        AF[low:high, :] = full
        AB[low:high, :] = full.astype(BF)

    for i in range(NZ):
        def self_block():
            self_rows(i, i * CH, (i + 1) * CH)

        self_block()
        for p in (2 * i, 2 * i + 1):
            push(AB.at[p * TB : (p + 1) * TB, :], ao.at[:, rows_of(s, HP)], plan.a_at, p, s, (r, p), when=s != p)
        if i == 1:
            mat_r(1)
    ao[:, rows_of(s, HP)] = AB[rows_of(s, TB), :]

    for p in seq_peers:
        push(winp.at[:, rows_of(p % G, U)], Win.at[own_rows, :], plan.in_s, p, s, (r, p))
    for p in seq_peers:
        arrive(Wkv3.at[rows_of(r * S + p, KB), :], plan.kv_s, p)
    got_kv.wait()
    plane_start(kv_block, plan.kv_r)
    xh, rstd = normalise(xs[own_tokens, :].astype(F32))
    n.XH[0] = xh
    n.RS[0] = rstd
    mat_p(1)
    mat_r(2)

    mat_take(0)
    for p in seq_peers:
        arrive(ao.at[:, rows_of(p, HP)], plan.a_at, p)
    h1 = xs[own_tokens, :].astype(F32) + dot(ao[...], mat(0))
    n.H[...] = h1
    xh, rstd = normalise(h1)
    n.XH[1] = xh
    n.RS[1] = rstd
    n2 = (xh * gain(1) + bias(1)).astype(BF)
    n.n2[...] = n2
    mat_c(1)
    mat_take(1)
    cqo = n.wide
    cqo[...] = dot(n2, mat(1)).astype(BF)
    CQ = n.CQ

    def to_heads(src, dst, name):
        for k in range(1, S):
            p = (s + k) % S
            push(src.at[:, rows_of(p, HP)], dst.at[own_tokens, :], name, p, s, (r, p))
        dst[own_tokens, :] = src[:, rows_of(s, HP)]

    def heads_take(dst, name, k):
        zl = (z + k) % NZ
        if k:
            arrive(dst.at[rows_of(2 * zl + c, TB), :], name, 2 * zl + c)
        arrive(dst.at[rows_of(2 * zl + 1 - c, TB), :], name, 2 * zl + 1 - c)
        return rows_of(zl, CH)

    def to_tokens(src, dst, name, k):
        zl = (z + k) % NZ
        for p in ([2 * zl + c] if k else []) + [2 * zl + 1 - c]:
            push(src.at[rows_of(p, TB), :], dst.at[:, rows_of(s, HP)], name, p, s, (r, p))
        if not k:
            dst[:, rows_of(s, HP)] = src[own_tokens, :]

    to_heads(cqo, CQ, plan.a_cq)
    for j in range(1, E):
        p = (s + j * G) % S
        push(n.wout, Wout.at[out_rows, :], plan.ow_g, p, s, (r, p))

    plane_pass(kv_block, kv_half, plan.kv_r)
    plane_take(kv_half, plan.kv_r)
    wide = Wkv3[...].astype(F32).reshape(R * S, KB, HP)
    half = KB // 2
    Wkv = n.Wkv
    Wkv[:, :HP] = wide[:, :half, :].reshape(TW, HP).astype(BF)
    Wkv[:, HP:] = wide[:, half:, :].reshape(TW, HP).astype(BF)
    CK, CV = n.CK, n.CV

    def text_rows(rows):
        got = dot(n.textv[rows, :], Wkv[...]).astype(BF)
        CK[rows, :] = got[:, :HP]
        CV[rows, :] = got[:, HP:]

    def text_block():
        each(T, CH, text_rows)

    got_text.wait()
    text_block()

    for p in seq_peers:
        arrive(Win.at[rows_of(r * S + p, DB), :], plan.in_s, p)
    plane_start(in_block, plan.in_r)
    mat_p(2)

    CKA, CVA, CKT, CQB = n.CKA, n.CVA, n.CKT, n.CQB
    CF, CB, co = n.CF, n.out, n.co
    drain(plan.a_at)

    def prepare_cross(rows):
        CKA[0, rows, :], CKA[1, rows, :] = split_pair(CK[rows, :], n.kbc[rows, :])

    each(T, CH, prepare_cross)
    def cross_rows(rows):
        scaled = (CQ[rows, :].astype(F32) * scale).astype(BF)
        CQ[rows, :] = scaled
        qa = split_pair(scaled, oh[rows, :])
        outs, sums = [], []
        for h in range(2):
            got = dot_nt(qa[h], CKA[h])
            top = jnp.max(got, axis=1, keepdims=True)
            got = jnp.exp(got - top)
            total = jnp.sum(got, axis=1, keepdims=True)
            outs.append(dot(got.astype(BF), CV[...]))
            sums.append(total)
            CQB[h, rows, :] = with_norm(qa[h], h, top + jnp.log(total))
        full = finish(outs[0], outs[1], sums[0], sums[1])
        CF[rows, :] = full
        CB[rows, :] = full.astype(BF)

    for k in range(NZ):
        rows = heads_take(CQ, plan.a_cq, k)

        def cross_block():
            cross_rows(rows)

        cross_block()
        to_tokens(CB, co, plan.a_cr, k)
    plane_pass(in_block, in_half, plan.in_r)
    got_og.wait()
    gather_start(ogf, plan.og, ffn_z0, GZ)
    for j in range(1, E):
        arrive(out_view(j)[0](r), plan.ow_g, (s + j * G) % S)
        plane_start(out_view(j)[0], plan.ow_x + 4 * j)
    mat_c(2)
    mat_take(2)
    for p in seq_peers:
        arrive(co.at[:, rows_of(p, HP)], plan.a_cr, p)
    h2 = n.H[...] + dot(co[...], mat(2))
    n.H[...] = h2
    xh, rstd = normalise(h2)
    n.XH[2] = xh
    n.RS[2] = rstd
    n3f = n.n3f
    n3f[rows_of(mem, TB), :] = (xh * gain(2) + bias(2)).astype(BF)
    gather_start(n3f, plan.n3, ffn_z0, GZ)

    got_ow.wait()
    for j in range(1, E):
        plane_pass(*out_view(j), plan.ow_x + 4 * j)
    plane_take(in_half, plan.in_r)
    plane_take(ow_half, plan.ow_r)
    for j in range(1, E):
        plane_take(out_view(j)[1], plan.ow_x + 4 * j)
    AD = n.AD
    ACT, DUP = AD.at[: G * TB], AD.at[G * TB :]
    UT = 512

    def reduce_core(ps, rb, name, zl):
        push(ps.at[rows_of(2 * zl + 1 - c, TB), :], rb.at[zl], name, zl, zl, (r, sib))

    def reduce_z(ps, rb, rz, cname, zname, z0, nz, zl, when=None):
        arrive(rb.at[zl], cname, zl)
        mine = rows_of(2 * zl + c, TB)
        ps[mine, :] = (ps[mine, :].astype(F32) + rb[zl].astype(F32)).astype(BF)
        push(ps.at[mine, :], rz.at[(z - z0 - zl + nz - 1) % nz], zname, zl, z - z0, (r, 2 * (z0 + zl) + c), when=when)

    def reduce_take(ps, rb, rz, cname, zname, z0, nz, summed=False):
        own = z - z0
        mine = rows_of(2 * own + c, TB)
        total = ps[mine, :].astype(F32)
        if not summed:
            arrive(rb.at[own], cname, own)
            total = total + rb[own].astype(F32)
        for k in range(1, nz):
            zl = (own + k) % nz
            arrive(rz.at[k - 1], zname, zl)
            total = total + rz[k - 1].astype(F32)
        return total

    def chain_send(mine, land, name, j):
        push(mine, land.at[0], name, 0, 0, (r, 2 * beside + c), when=beside == j)
        push(mine, land.at[1 + j % 2], name, 1 + j % 2, 1 + j % 2, (r, 2 * beside + c), when=outer & (j // 2 != side))

    def chain_relay(at, land, name):
        for k in range(2):
            to = 2 - 2 * side + k
            mine = at(to)

            def add():
                arrive(land.at[1 + k], name, 1 + k)
                mine[...] = (mine[...].astype(F32) + land[1 + k].astype(F32)).astype(BF)

            pl.when(inner)(add)
            push(mine, land.at[3], name, 3 + k, 3, (r, 2 * to + c), when=inner)

    def chain_total(at, land, name):
        arrive(land.at[0], name, 0)
        arrive(land.at[3], name, 3)
        return at(z)[...].astype(F32) + land[0].astype(F32) + land[3].astype(F32)

    def core_sum(ps, rb, cname, j):
        arrive(rb.at[j], cname, j)
        mine = ps.at[rows_of(2 * j + c, TB), :]
        mine[...] = (mine[...].astype(F32) + rb[j].astype(F32)).astype(BF)
        return mine

    def rows_at(ps):
        def at(j):
            return ps.at[rows_of(2 * j + c, TB), :]

        return at

    ps0 = n.ps0
    drain(plan.n1)
    NT = G * TB
    psE = ps0.at[:NT]
    psO = ps0.at[NT:]
    for k in range(GZ):
        gather_pass(ogf, plan.og, ffn_z0, GZ, k)
        gather_take(ogf, plan.og, ffn_z0, GZ, k)
        gather_pass(n3f, plan.n3, ffn_z0, GZ, k)
        rows = gather_take(n3f, plan.n3, ffn_z0, GZ, k)

        def hidden(cols):
            up = dot(n3f[rows, :], Win[:, cols])
            d_act = dot_nt(ogf[rows, :], Wout[cols, :])
            cdf = 0.5 * (1.0 + lax.erf(up * (0.5**0.5)))
            pdf = jnp.exp(-0.5 * up * up) * 0.3989422804014327
            ACT[rows, cols] = (up * cdf).astype(BF)
            DUP[rows, cols] = (d_act * (cdf + up * pdf)).astype(BF)

        def hidden_block():
            each(U, UT, hidden)

        def back_block():
            psE[rows, :] = dot_nt(DUP[rows, :], Win[...]).astype(BF)

        hidden_block()
        back_block()
        zl = (z - ffn_z0 + k) % GZ
        reduce_core(psE, n.rbE, plan.e_c, zl)
    for k in range(1, GZ):
        reduce_z(psE, n.rbE, n.rzE, plan.e_c, plan.e_z, ffn_z0, GZ, (z - ffn_z0 + k) % GZ)
    drain(plan.ow_r, plan.ow_g, plan.in_r, plan.in_s, *[plan.ow_x + 4 * j for j in range(1, E)])

    for k in range(GZ):
        zl = (z - ffn_z0 + k) % GZ
        rows = rows_of(zl, CH)

        def out_block_rows():
            psO[rows, :] = dot(ACT[rows, :], Wout[...]).astype(BF)

        out_block_rows()
    def gout_rows(cols):
        Wout[cols, :] = dot_tn(ACT[:, cols], ogf[...]).astype(BF)

    def gout_block():
        each(U, 256, gout_rows)

    gout_block()
    go_half = rows_view(Wout, E * UB)[1]
    fold_start(go_half, n.rgo, plan.go_r)

    def norm_back(i, e):
        n.gg[i : i + 1, :] = jnp.sum(e * n.XH[i], axis=0, keepdims=True)
        n.gg[3 + i : 4 + i, :] = jnp.sum(e, axis=0, keepdims=True)
        y = e * gain(i)
        xhat = n.XH[i]
        a = jnp.mean(y, axis=1, keepdims=True)
        b = jnp.mean(y * xhat, axis=1, keepdims=True)
        return (y - a - xhat * b) * n.RS[i]

    e = reduce_take(psE, n.rbE, n.rzE, plan.e_c, plan.e_z, ffn_z0, GZ)
    g2 = ogf[rows_of(mem, TB), :].astype(F32) + norm_back(2, e)
    n.GR[...] = g2
    g2b = g2.astype(BF)
    dco = n.wide
    drain(plan.a_cq)
    dco[...] = dot_nt(g2b, mat(2)).astype(BF)
    DC = n.DC
    to_heads(dco, DC, plan.b_cr)

    def mat_grad(i, left, right):
        drain(plan.m_z + 4 * i, plan.m_r + 4 * i, plan.m_c + 2 * i)

        def mat_block():
            mats[i][...] = dot_tn(left, right).astype(BF).reshape(mats[i].shape)

        mat_block()
        push(mats[i].at[:, 1 - c], n.rmc.at[i], plan.h_c + 2 * i, 0, 0, (r, sib))

    def mat_grad_r(i):
        arrive(n.rmc.at[i], plan.h_c + 2 * i, 0)
        mine = mats[i].at[:, c]
        mine[...] = (mine[...].astype(F32) + n.rmc[i].astype(F32)).astype(BF)
        fold_start(mat_view(i)[1], n.rmr.at[i], plan.h_r + 8 * i)

    def mat_grad_p(i):
        fold_pass(mat_view(i)[1], n.rmr.at[i], plan.h_r + 8 * i)

    def mat_grad_z(i):
        fold_take(mat_view(i)[1], n.rmr.at[i], plan.h_r + 8 * i)
        for j in range(NZ):
            chain_send(mat_at(i)(j), n.rmz.at[i], plan.h_z + 8 * i, j)

    def mat_at(i):
        def at(j):
            return mats[i].at[r * NZ + j, c]

        return at

    def mat_grad_f(i):
        chain_relay(mat_at(i), n.rmz.at[i], plan.h_z + 8 * i)

    def mat_grad_take(i, stage, out):
        emit(stage, out, chain_total(mat_at(i), n.rmz.at[i], plan.h_z + 8 * i))

    for k in range(GZ):
        reduce_core(psO, n.rbO, plan.o_c, (z - ffn_z0 + k) % GZ)
    for k in range(1, GZ):
        reduce_z(psO, n.rbO, n.rzO, plan.o_c, plan.o_z, ffn_z0, GZ, (z - ffn_z0 + k) % GZ)
    mat_grad(2, co[...], g2b)

    def gin_rows(cols):
        Win[cols, :] = dot_tn(n3f[:, cols], DUP[...]).astype(BF)

    def gin_block():
        each(D, 256, gin_rows)

    gin_block()
    fold_start(in_half, n.rgi, plan.gi_r)
    fold_pass(go_half, n.rgo, plan.go_r)
    total = n.H[...] + reduce_take(psO, n.rbO, n.rzO, plan.o_c, plan.o_z, ffn_z0, GZ)
    emit(n.s_out, n.o_out, total.astype(BF))

    def prepare_cross_back(rows):
        CVA[0, rows, :], CVA[1, rows, :] = split_pair(CV[rows, :], ones_rows(CH))
        CKT[:, rows] = jnp.transpose(CK[rows, :].astype(F32)).astype(BF)

    def ones_rows(count):
        spot = lax.broadcasted_iota(jnp.int32, (count, HP), 1) % HD
        return jnp.where((spot >= 4) & (spot < 7), 1.0, 0.0)

    def with_delta(grad, full):
        front = first_half(grad.shape)
        wide = grad.astype(F32)
        prod = wide * full
        d0 = jnp.sum(jnp.where(front, prod, 0.0), axis=1, keepdims=True)
        d1 = jnp.sum(jnp.where(front, 0.0, prod), axis=1, keepdims=True)
        zero = jnp.zeros_like(wide)
        return (
            with_norm(jnp.where(front, wide, zero), 0, d0),
            with_norm(jnp.where(front, zero, wide), 1, d1),
        )

    each(T, CH, prepare_cross_back)
    DCK, DCV, DQ, dqo = n.DCK, n.DCV, n.out, n.dqo
    drain(plan.a_cr)

    def heads_join(a, b, axis):
        spot = lax.broadcasted_iota(jnp.int32, a.shape, axis)
        return jnp.where(spot < HD, a, b)

    def cross_back_rows(k, rows):
        grad = DC[rows, :]
        ga = with_delta(grad, CF[rows, :])
        q2 = CQ[rows, :]
        dv, dk, dq = [], [], []
        for h in range(2):
            prob = jnp.exp(dot_nt(CKA[h], CQB[h, rows, :]))
            ds = (prob * dot_nt(CVA[h], ga[h])).astype(BF)
            dv.append(dot(prob.astype(BF), grad))
            dk.append(dot(ds, q2))
            dq.append(dot(CKT[...], ds))
        dvj, dkj = heads_join(dv[0], dv[1], 1), heads_join(dk[0], dk[1], 1)
        if k:
            DCV[...] += dvj
            DCK[...] += dkj
        else:
            DCV[...] = dvj
            DCK[...] = dkj
        DQ[rows, :] = (jnp.transpose(heads_join(dq[0], dq[1], 0)) * scale).astype(BF)

    for k in range(NZ):
        rows = heads_take(DC, plan.b_cr, k)

        def cross_back_block():
            cross_back_rows(k, rows)

        cross_back_block()
        to_tokens(DQ, dqo, plan.b_cq, k)
    mat_grad_r(2)

    DKV = n.DKV
    DKV[:, :HP] = DCK[...].astype(BF)
    DKV[:, HP:] = DCV[...].astype(BF)
    psT = AD.at[:T, :TW]

    for j in range(NZ):
        rows = pl.ds(j * CH, CH)

        def text_back():
            psT[rows, :] = dot_nt(DKV[rows, :], Wkv[...]).astype(BF)

        text_back()
        reduce_core(psT, n.rbT, plan.t_c, j)

    for p in seq_peers:
        arrive(dqo.at[:, rows_of(p, HP)], plan.b_cq, p)
    e = dot_nt(dqo[...], mat(1))
    g1 = n.GR[...] + norm_back(1, e)
    n.GR[...] = g1
    g1b = g1.astype(BF)
    dao = n.wide
    drain(plan.b_cr)
    dao[...] = dot_nt(g1b, mat(0)).astype(BF)
    DA = n.DA
    to_heads(dao, DA, plan.b_at)

    def sum_rows(own, landed, name):
        total = own.astype(F32)
        for k, p in enumerate(row_peers):
            arrive(landed.at[k], name, p)
            total = total + landed[k].astype(F32)
        return total

    fold_take(go_half, n.rgo, plan.go_r)
    rgo2 = n.rgo2
    if E == 1:
        emit(n.s_ow, n.o_ow, Wout[out_rows, :].astype(F32))
    else:
        for j in range(1, E):
            p = (s + j * G) % S
            push(
                Wout.at[rows_of(r * E + (grp + j) % E, UB), :], rgo2.at[grp], plan.go_g, p, s, (r, p)
            )

    drain(plan.kv_s, plan.kv_r)
    span = TW // 2
    def gkv_rows(i):
        got = dot_tn(n.textv[:, i * span : (i + 1) * span], DKV[...])
        both = [got[:, q * HP : (q + 1) * HP].reshape(span // half, half, HP) for q in range(2)]
        both = jnp.concatenate(both, axis=1).reshape(2 * span, HP)
        Wkv3[2 * i * span : 2 * (i + 1) * span, :] = both.astype(BF)

    def gkv_block():
        gkv_rows(0)
        gkv_rows(1)

    gkv_block()
    fold_start(kv_half, n.rgk, plan.gk_r)
    mat_grad(1, n.n2[...], dqo[...])
    mat_grad(0, ao[...], g1b)
    mat_grad_r(1)
    mat_grad_r(0)
    fold_pass(in_half, n.rgi, plan.gi_r)
    mat_grad_p(2)
    fold_pass(kv_half, n.rgk, plan.gk_r)

    VA, KT, DOA = CVA, CKT, CQB
    DQT, DQKV = n.DQT, n.DQKV
    drain(plan.e_c, plan.e_z, plan.o_c, plan.o_z, plan.b_at)

    def prepare_self_back(rows):
        VA[0, rows, :], VA[1, rows, :] = split_pair(V[rows, :], ones_rows(CH))
        KT[:, rows] = jnp.transpose(K[rows, :].astype(F32)).astype(BF)

    each(T, CH, prepare_self_back)
    for k in range(NZ):
        rows = heads_take(DA, plan.b_at, k)
        DOA[0, rows, :], DOA[1, rows, :] = with_delta(DA[rows, :], AF[rows, :])
    def self_back_rows(j, low, high):
        grad, q2 = DA[low:, :], Q[low:, :]
        dv, dk, dq = [], [], []
        for h in range(2):
            sc = dot_nt(KA[h, low:high, :], QB[h, low:, :])
            head = jnp.where(qpos <= kpos, sc[:, :CH], NEG)
            sc = jnp.concatenate([head, sc[:, CH:]], axis=1) if j < NZ - 1 else head
            prob = jnp.exp(sc)
            ds = (prob * dot_nt(VA[h, low:high, :], DOA[h, low:, :])).astype(BF)
            dv.append(dot(prob.astype(BF), grad))
            dk.append(dot(ds, q2))
            dq.append(dot(KT[:, low:high], ds))
        if j:
            DQT[:, low:] += heads_join(dq[0], dq[1], 0)
        else:
            DQT[...] = heads_join(dq[0], dq[1], 0)
        DQKV[low:high, :HP] = (jnp.transpose(DQT[:, low:high]) * scale).astype(BF)
        DQKV[low:high, HP : 2 * HP] = heads_join(dk[0], dk[1], 1).astype(BF)
        DQKV[low:high, 2 * HP :] = heads_join(dv[0], dv[1], 1).astype(BF)
        ps0[low:high, :] = dot_nt(DQKV[low:high, :], Wq[...]).astype(BF)

    for j in range(NZ):
        def self_back_block():
            self_back_rows(j, j * CH, (j + 1) * CH)

        self_back_block()
        reduce_core(ps0, n.rb0, plan.s_c, j)
        if j:
            chain_send(core_sum(ps0, n.rb0, plan.s_c, j - 1), n.rz0, plan.s_z, j - 1)
    chain_send(core_sum(ps0, n.rb0, plan.s_c, NZ - 1), n.rz0, plan.s_z, NZ - 1)
    for j in range(NZ):
        chain_send(core_sum(psT, n.rbT, plan.t_c, j), n.rzT, plan.t_z, j)
    chain_relay(rows_at(ps0), n.rz0, plan.s_z)
    mat_grad_p(1)
    mat_grad_p(0)
    fold_take(in_half, n.rgi, plan.gi_r)
    rgi2 = n.rgi2
    for p in seq_peers:
        push(Win.at[rows_of(r * S + p, DB), :], rgi2.at[s], plan.gi_s, p, s, (r, p))
    rgi2[s] = Win[own_rows, :]
    mat_grad_z(2)
    chain_relay(rows_at(psT), n.rzT, plan.t_z)

    drain(plan.q_s, plan.q_r)

    def gq_rows(cols):
        got = dot_tn(n1f[:, cols], DQKV[...]).astype(BF)
        for i in range(3):
            Wq3[i, cols, :] = got[:, i * HP : (i + 1) * HP]

    def gq_block():
        each(D, 256, gq_rows)

    gq_block()
    fold_start(q_half, n.rgq, plan.gq_r)

    mat_grad_f(2)
    mat_grad_z(1)
    mat_grad_z(0)
    fold_take(kv_half, n.rgk, plan.gk_r)
    fold_pass(q_half, n.rgq, plan.gq_r)
    GC = n.GC
    for p in seq_peers:
        push(Wkv3.at[rows_of(r * S + p, KB), :], GC.at[:, rows_of(s, HP)], plan.gk_s, p, s, (r, p))
    GC[:, rows_of(s, HP)] = Wkv3[kv_rows, :]
    emit(n.s_tg, n.o_tg, chain_total(rows_at(psT), n.rzT, plan.t_z))
    if E > 1:
        total = Wout[out_rows, :].astype(F32)
        for j in range(1, E):
            g2i = (grp + j) % E
            arrive(rgo2.at[g2i], plan.go_g, (s + j * G) % S)
            total = total + rgo2[g2i].astype(F32)
        emit(n.s_ow, n.o_ow, total)
    for p in seq_peers:
        arrive(rgi2.at[p], plan.gi_s, p)
    for m in range(G):
        total = rgi2[m].astype(F32)
        for g in range(1, E):
            total = total + rgi2[g * G + m].astype(F32)
        for rr in range(R):
            for j in range(E):
                b = rr * S + j * G + m
                at = (rr * E + j) * UB
                n.s_in[:, b * UB : (b + 1) * UB] = total[:, at : at + UB]
    finals.append(local(n.s_in, n.o_in, 16 + len(finals)))

    e = chain_total(rows_at(ps0), n.rz0, plan.s_z)
    back = norm_back(0, e)
    gg, rgg, gg2, rgg2 = n.gg, n.rgg, n.gg2, n.rgg2
    GW = D // R
    for k, p in enumerate(row_peers, 1):
        push(gg.at[:, rows_of(p, GW)], rgg.at[R - 1 - k], plan.gg_r, p, r, (p, s))
    emit(n.s_ig, n.o_ig, n.GR[...] + back)
    fold_take(q_half, n.rgq, plan.gq_r)
    GQ = n.GQ
    for p in seq_peers:
        push(Wq3.at[:, rows_of(r * S + p, DB), :], GQ.at[:, :, rows_of(s, HP)], plan.gq_s, p, s, (r, p))
    GQ[:, :, rows_of(s, HP)] = Wq3[:, own_rows, :]
    gg2[...] = sum_rows(gg[:, rows_of(r, GW)], rgg, plan.gg_r)
    for p in seq_peers:
        push(gg2.at[:, rows_of(p // per, 128)], rgg2.at[s], plan.gg_s, p, s, (r, p))
    mat_grad_f(1)
    mat_grad_f(0)
    mat_grad_take(2, n.s_co, n.o_co)
    mat_grad_take(1, n.s_cq, n.o_cq)
    mat_grad_take(0, n.s_so, n.o_so)
    for p in seq_peers:
        arrive(GC.at[:, rows_of(p, HP)], plan.gk_s, p)
    emit(n.s_ckv, n.o_ckv, GC[...].astype(F32))
    total = gg2[:, rows_of(s // per, 128)]
    for p in seq_peers:
        arrive(rgg2.at[p], plan.gg_s, p)
        total = total + rgg2[p]
    emit(n.s_gb, n.o_gb, total)
    for p in seq_peers:
        arrive(GQ.at[:, :, rows_of(p, HP)], plan.gq_s, p)
    emit(n.s_qkv, n.o_qkv, GQ[...].astype(F32))
    drain(*list(pending))
    for cp in finals:
        cp.wait()


def copy_kernel(count, *refs):
    stages, into, out_of = refs[2 * count : 3 * count], refs[3 * count], refs[3 * count + 1]
    loads = [pltpu.make_async_copy(refs[i], stages[i], into.at[i]) for i in range(count)]
    stores = [
        pltpu.make_async_copy(stages[i], refs[count + i], out_of.at[i]) for i in range(count)
    ]
    for cp in loads:
        cp.start()
    for load, store in zip(loads, stores):
        load.wait()
        store.start()
    for cp in stores:
        cp.wait()


def settle(arrays):
    anywhere = pl.BlockSpec(memory_space=pl.ANY)
    return pl.pallas_call(
        functools.partial(copy_kernel, len(arrays)),
        out_shape=[jax.ShapeDtypeStruct(a.shape, a.dtype) for a in arrays],
        in_specs=[anywhere] * len(arrays),
        out_specs=[anywhere] * len(arrays),
        scratch_shapes=[pltpu.VMEM(a.shape, a.dtype) for a in arrays]
        + [pltpu.SemaphoreType.DMA((len(arrays),))] * 2,
    )(*arrays)


def fused_shards(
    hidden_in, clip_lengths, text_lengths, text_states, norm_gain, norm_bias, self_qkv,
    self_out, cross_query, cross_kv, cross_out, ffn_in, ffn_out, out_grad,
):
    R, S = lax.axis_size("rows"), lax.axis_size("seq")
    TB, D = hidden_in.shape[1:]
    TW = text_states.shape[2]
    T, HP, DB = TB * S, D // S, D // (R * S)
    FF = ffn_in.shape[1]
    G = GROUP
    E, U, UB, NT, NZ = S // G, FF // G, FF // (R * S), G * TB, S // 2
    GZ = G // 2
    KB = 2 * cross_kv.shape[1]
    index = lax.axis_index("rows") * S + lax.axis_index("seq")
    per = 128 // DB
    both = jnp.concatenate([norm_gain, norm_bias], axis=0)
    both = jnp.pad(both, ((0, 10), (0, 0)))
    spot = jnp.arange(128, dtype=jnp.int32)[None, :] // DB
    gb = jnp.where(spot == index % per, jnp.tile(both, (1, per)), jnp.zeros((), both.dtype))
    ins = dict(
        cl=clip_lengths, tl=text_lengths, x=hidden_in.reshape(TB, D), og=out_grad.reshape(TB, D),
        text=text_states.reshape(T, TW), gb=gb, wqkv=self_qkv, wo=self_out, wcq=cross_query,
        wco=cross_out, wckv=cross_kv.reshape(KB, D), win=ffn_in, wout=ffn_out,
    )
    outs = dict(
        o_out=((TB, D), BF), o_ig=((TB, D), F32), o_tg=((TB, TW), F32), o_gb=((8, 128), F32),
        o_qkv=(self_qkv.shape, F32), o_so=(self_out.shape, F32), o_cq=(cross_query.shape, F32),
        o_ckv=((KB, D), F32), o_co=(cross_out.shape, F32), o_in=(ffn_in.shape, F32),
        o_ow=(ffn_out.shape, F32),
    )
    plan, count = semaphore_plan(GZ)
    hp = (T, HP)
    pair = (2, T, HP)
    scratch = dict(
        textv=((T, TW), BF),
        gbt=((R, S, 16, 128), BF), gbf=((16, D), F32), Wq3=((3, D, HP), BF), Wq=((D, 3 * HP), BF),
        Wkv3=((R * S * KB, HP), BF), Wkv=((TW, 2 * HP), BF),
        Wm0=((R * NZ, 2, DB, D), BF), Wm1=((R * NZ, 2, DB, D), BF), Wm2=((R * NZ, 2, DB, D), BF),
        Win=((D, U), BF), Wout=((U, D), BF), winp=((DB, FF), BF),
        XH=((3, TB, D), F32), RS=((3, TB, 1), F32), H=((TB, D), F32), GR=((TB, D), F32),
        n1f=((T, D), BF), n3f=((NT, D), BF), ogf=((NT, D), BF), n2=((TB, D), BF),
        oh=(hp, BF), kbs=(hp, BF), kbc=(hp, BF),
        Q=(hp, BF), K=(hp, BF), V=(hp, BF), CK=(hp, BF), CV=(hp, BF), CQ=(hp, BF),
        KA=(pair, BF), QB=(pair, BF),
        CKA=(pair, BF), CVA=(pair, BF), CQB=(pair, BF), CKT=((HP, T), BF),
        AF=(hp, F32), CF=(hp, F32), out=(hp, BF), DC=(hp, BF), DA=(hp, BF),
        ao=((TB, D), BF), wide=((TB, D), BF), co=((TB, D), BF), dqo=((TB, D), BF),
        DCK=(hp, F32), DCV=(hp, F32), DKV=((T, 2 * HP), BF),
        DQT=((HP, T), F32), DQKV=((T, 3 * HP), BF),
        AD=((2 * NT, U), BF),
        ps0=((max(T, 2 * NT), D), BF),
        rbE=((GZ, TB, D), BF), rzE=((GZ - 1, TB, D), BF), rbO=((GZ, TB, D), BF), rzO=((GZ - 1, TB, D), BF),
        rbT=((NZ, TB, TW), BF), rzT=((NZ, TB, TW), BF), rb0=((NZ, TB, D), BF), rz0=((NZ, TB, D), BF),
        rgo=((6, E * UB // 2, D), BF), rgo2=((E, UB, D), BF), rgi=((6, S * DB // 2, U), BF), rgi2=((S, DB, U), BF),
        rgk=((6, S * KB // 2, HP), BF), GC=((KB, D), BF), rgq=((6, 3, S * DB // 2, HP), BF), GQ=((3, DB, D), BF),
        gg=((8, D), F32), rgg=((R - 1, 8, D // R), F32), gg2=((8, D // R), F32), rgg2=((S, 8, 128), F32),
        rmc=((3, R * NZ, DB, D), BF), rmr=((3, 6, NZ // 2, DB, D), BF), rmz=((3, NZ, DB, D), BF),
    )
    for name, spec in outs.items():
        scratch[name.replace("o_", "s_")] = spec
    names = list(ins) + list(outs) + list(scratch) + ["ss", "rs", "ls"]
    anywhere = pl.BlockSpec(memory_space=pl.ANY)
    smem = pl.BlockSpec(memory_space=pltpu.SMEM)
    got = pl.pallas_call(
        functools.partial(layer_kernel, plan, names),
        out_shape=[jax.ShapeDtypeStruct(*v) for v in outs.values()],
        in_specs=[smem, smem] + [anywhere] * (len(ins) - 2),
        out_specs=[anywhere] * len(outs),
        scratch_shapes=[pltpu.VMEM(*v) for v in scratch.values()]
        + [pltpu.SemaphoreType.DMA((k,)) for k in (count, count, 32)],
        compiler_params=pltpu.CompilerParams(
            collective_id=0, has_side_effects=True, vmem_limit_bytes=63 << 20
        ),
    )(*ins.values())
    got = list(got)
    got = list(settle(got[:3] + got[4:])) + [got[3]]
    o = types.SimpleNamespace(**dict(zip([k for k in outs if k != "o_gb"] + ["o_gb"], got)))
    mine = lax.dynamic_slice(o.o_gb, (0, (index % per) * DB), (8, DB))
    return (
        o.o_out.reshape(hidden_in.shape), o.o_ig.reshape(hidden_in.shape),
        o.o_tg.reshape(1, TB, TW), mine[:3], mine[3:6], o.o_qkv, o.o_so, o.o_cq,
        o.o_ckv.reshape(cross_kv.shape), o.o_co, o.o_in, o.o_ow,
    )


def fits(mesh):
    return dict(mesh.shape) == {"rows": 4, "seq": 8}


def solution(mesh):
    placed = (
        P("rows", "seq", None),
        P("rows", None),
        P("rows", None),
        P("rows", None, None),
        P(None, ("rows", "seq")),
        P(None, ("rows", "seq")),
        P(None, ("rows", "seq"), None),
        P(("rows", "seq"), None),
        P(("rows", "seq"), None),
        P(None, ("rows", "seq"), None),
        P(("rows", "seq"), None),
        P(("rows", "seq"), None),
        P(("rows", "seq"), None),
        P("rows", "seq", None),
    )
    return jax.shard_map(
        fused_shards if fits(mesh) else shards,
        mesh=mesh,
        in_specs=placed,
        out_specs=(
            P("rows", "seq", None),
            P("rows", "seq", None),
            P("rows", "seq", None),
            P(None, ("rows", "seq")),
            P(None, ("rows", "seq")),
            P(None, ("rows", "seq"), None),
            P(("rows", "seq"), None),
            P(("rows", "seq"), None),
            P(None, ("rows", "seq"), None),
            P(("rows", "seq"), None),
            P(("rows", "seq"), None),
            P(("rows", "seq"), None),
        ),
        check_vma=False,
    )
```

```python
import functools
import types

import jax
import jax.numpy as jnp
from jax import lax
from jax.experimental import pallas as pl
from jax.experimental.pallas import tpu as pltpu
from jax.sharding import PartitionSpec as P

HD = 64


epsilon = 1e-05
masked_score = -1e30
group_heads = 4
highest = lax.Precision.HIGHEST


def layer_norm(values, gains, biases):
    average = jnp.mean(values, axis=-1, keepdims=True)
    centred = values - average
    variance = jnp.mean(centred * centred, axis=-1, keepdims=True)
    return centred * lax.rsqrt(variance + epsilon) * gains + biases


def gelu_exact(values):
    return jax.nn.gelu(values, approximate=False)


def project(left, weight):
    return jnp.einsum("rtd,de->rte", left, weight, preferred_element_type=jnp.float32)


def weight_term(left, right):
    return jnp.einsum("rtd,rte->de", left, right, preferred_element_type=jnp.float32)


def back_project(gradient, weight):
    return jnp.einsum("rte,de->rtd", gradient, weight, preferred_element_type=jnp.float32)


def exact_weight_term(left, right):
    return jnp.einsum(
        "rtd,rte->de", left, right, precision=highest, preferred_element_type=jnp.float32
    )


def exact_back_project(gradient, weight):
    return jnp.einsum(
        "rte,de->rtd", gradient, weight, precision=highest, preferred_element_type=jnp.float32
    )


def split_heads(values):
    return values.reshape(values.shape[0], values.shape[1], values.shape[2] // HD, HD)


def clip_of(positions, clip_ends):
    return jnp.sum((positions[None, :, None] >= clip_ends[:, None, :]).astype(jnp.int32), axis=2)


def pair_mask(query_pos, query_clip, key_pos, key_clip):
    causal = query_pos[None, :, None] >= key_pos[None, None, :]
    return (causal & (query_clip[:, :, None] == key_clip[:, None, :]))[:, None]


def blocks_of(arrived, frame_span):
    block_count = arrived.shape[1] // frame_span
    shaped = arrived.reshape((arrived.shape[0], block_count, frame_span) + arrived.shape[2:])
    return jnp.moveaxis(shaped, 1, 0)


def block_fold(visit_block, frame_span, carried, arrived):
    block_count = arrived.shape[1] // frame_span
    starts = frame_span * jnp.arange(block_count, dtype=jnp.int32)

    def scan_step(state, block_pair):
        return (visit_block(state, block_pair[0], block_pair[1]), None)

    carried, unused = lax.scan(scan_step, carried, (blocks_of(arrived, frame_span), starts))
    return carried


def head_dot(gradient, output):
    summed = jnp.sum(split_heads(gradient).astype(jnp.float32) * split_heads(output), axis=3)
    return jnp.swapaxes(summed, 1, 2)


def text_project(texts, w_text):
    return jnp.concatenate([project(texts, w_text[0]), project(texts, w_text[1])], axis=2).astype(
        jnp.bfloat16
    )


def self_forward(queries, key_value, clip_ends, clip_ids, frames):
    row_count, frame_span, model_width = queries.shape
    head_count = model_width // HD
    score_scale = HD ** (-0.5)
    query_heads = split_heads(queries)
    last_frame = frames[frame_span - 1]

    def visit_block(state, key_block, first_key):
        key_pos = first_key + jnp.arange(frame_span, dtype=jnp.int32)

        def accumulate(carried):
            running_max, running_sum, output_sum = carried
            key_heads = split_heads(key_block[:, :, :model_width])
            value_heads = split_heads(key_block[:, :, model_width:])
            allowed = pair_mask(frames, clip_ids, key_pos, clip_of(key_pos, clip_ends))
            scores = (
                jnp.einsum(
                    "rqhd,rkhd->rhqk", query_heads, key_heads, preferred_element_type=jnp.float32
                )
                * score_scale
            )
            scores = jnp.where(allowed, scores, masked_score)
            new_max = jnp.maximum(running_max, jnp.max(scores, axis=3))
            weights = jnp.where(allowed, jnp.exp(scores - new_max[..., None]), 0.0)
            shrink = jnp.exp(running_max - new_max)
            running_sum = running_sum * shrink + jnp.sum(weights, axis=3)
            output_sum = output_sum * shrink[..., None] + jnp.einsum(
                "rhqk,rkhd->rhqd",
                weights.astype(jnp.bfloat16),
                value_heads,
                preferred_element_type=jnp.float32,
            )
            return (new_max, running_sum, output_sum)

        return lax.cond(first_key > last_frame, lambda carried: carried, accumulate, state)

    initial = (
        jnp.full((row_count, head_count, frame_span), masked_score, jnp.float32),
        jnp.zeros((row_count, head_count, frame_span), jnp.float32),
        jnp.zeros((row_count, head_count, frame_span, HD), jnp.float32),
    )
    running_max, running_sum, output_sum = block_fold(
        visit_block, frame_span, initial, lax.all_gather(key_value, "seq", axis=1, tiled=True)
    )
    attended = output_sum / running_sum[..., None]
    return (
        jnp.swapaxes(attended, 1, 2).reshape(row_count, frame_span, model_width),
        running_max + jnp.log(running_sum),
    )


def self_query_grad(queries, key_value, clip_ends, clip_ids, frames, log_norm, delta_sum, d_attn):
    row_count, frame_span, model_width = queries.shape
    head_count = model_width // HD
    score_scale = HD ** (-0.5)
    query_heads = split_heads(queries)
    grad_heads = split_heads(d_attn)
    last_frame = frames[frame_span - 1]

    def visit_block(state, key_block, first_key):
        key_pos = first_key + jnp.arange(frame_span, dtype=jnp.int32)

        def accumulate(carried):
            key_heads = split_heads(key_block[:, :, :model_width])
            value_heads = split_heads(key_block[:, :, model_width:])
            allowed = pair_mask(frames, clip_ids, key_pos, clip_of(key_pos, clip_ends))
            scores = (
                jnp.einsum(
                    "rqhd,rkhd->rhqk", query_heads, key_heads, preferred_element_type=jnp.float32
                )
                * score_scale
            )
            probability = jnp.where(allowed, jnp.exp(scores - log_norm[..., None]), 0.0)
            d_prob = jnp.einsum(
                "rqhd,rkhd->rhqk", grad_heads, value_heads, preferred_element_type=jnp.float32
            )
            d_score = (probability * (d_prob - delta_sum[..., None])).astype(jnp.bfloat16)
            return carried + jnp.einsum(
                "rhqk,rkhd->rhqd", d_score, key_heads, preferred_element_type=jnp.float32
            )

        return lax.cond(first_key > last_frame, lambda carried: carried, accumulate, state)

    initial = jnp.zeros((row_count, head_count, frame_span, HD), jnp.float32)
    d_query = block_fold(
        visit_block, frame_span, initial, lax.all_gather(key_value, "seq", axis=1, tiled=True)
    )
    d_query = jnp.swapaxes(d_query, 1, 2).reshape(row_count, frame_span, model_width) * score_scale
    return d_query.astype(jnp.bfloat16)


def self_key_grad(query_grad, key_value, clip_ends, clip_ids, frames, gathered_stats):
    row_count, frame_span, double_width = key_value.shape
    model_width = double_width // 2
    head_count = model_width // HD
    score_scale = HD ** (-0.5)
    key_heads = split_heads(key_value[:, :, :model_width])
    value_heads = split_heads(key_value[:, :, model_width:])
    all_norm, all_delta = gathered_stats
    first_own = frames[0]

    def visit_block(state, query_block, first_query):
        query_pos = first_query + jnp.arange(frame_span, dtype=jnp.int32)

        def accumulate(carried):
            d_key, d_value = carried
            query_heads = split_heads(query_block[:, :, :model_width])
            grad_heads = split_heads(query_block[:, :, model_width:])
            log_norm = jnp.swapaxes(
                lax.dynamic_slice_in_dim(all_norm, first_query, frame_span, 1), 1, 2
            )
            delta_sum = jnp.swapaxes(
                lax.dynamic_slice_in_dim(all_delta, first_query, frame_span, 1), 1, 2
            )
            allowed = pair_mask(query_pos, clip_of(query_pos, clip_ends), frames, clip_ids)
            scores = (
                jnp.einsum(
                    "rqhd,rkhd->rhqk", query_heads, key_heads, preferred_element_type=jnp.float32
                )
                * score_scale
            )
            probability = jnp.where(allowed, jnp.exp(scores - log_norm[..., None]), 0.0)
            d_value = d_value + jnp.einsum(
                "rhqk,rqhd->rhkd",
                probability.astype(jnp.bfloat16),
                grad_heads,
                preferred_element_type=jnp.float32,
            )
            d_prob = jnp.einsum(
                "rqhd,rkhd->rhqk", grad_heads, value_heads, preferred_element_type=jnp.float32
            )
            d_score = (probability * (d_prob - delta_sum[..., None])).astype(jnp.bfloat16)
            d_key = d_key + jnp.einsum(
                "rhqk,rqhd->rhkd", d_score, query_heads, preferred_element_type=jnp.float32
            )
            return (d_key, d_value)

        return lax.cond(
            first_query + frame_span - 1 < first_own, lambda carried: carried, accumulate, state
        )

    zeros_heads = jnp.zeros((row_count, head_count, frame_span, HD), jnp.float32)
    d_key, d_value = block_fold(
        visit_block,
        frame_span,
        (zeros_heads, zeros_heads),
        lax.all_gather(query_grad, "seq", axis=1, tiled=True),
    )
    d_key = jnp.swapaxes(d_key, 1, 2).reshape(row_count, frame_span, model_width) * score_scale
    d_value = jnp.swapaxes(d_value, 1, 2).reshape(row_count, frame_span, model_width)
    return (d_key.astype(jnp.bfloat16), d_value.astype(jnp.bfloat16))


def cross_forward(queries, text_kv, readable):
    row_count, frame_span, model_width = queries.shape
    group_width = group_heads * HD
    score_scale = HD ** (-0.5)
    outputs = []
    log_norms = []
    for group_index in range(model_width // group_width):
        lower_edge = group_index * group_width
        query_heads = split_heads(queries[:, :, lower_edge : lower_edge + group_width])
        key_heads = split_heads(text_kv[:, :, lower_edge : lower_edge + group_width])
        value_heads = split_heads(
            text_kv[:, :, model_width + lower_edge : model_width + lower_edge + group_width]
        )
        scores = (
            jnp.einsum(
                "rqhd,rkhd->rhqk", query_heads, key_heads, preferred_element_type=jnp.float32
            )
            * score_scale
        )
        scores = jnp.where(readable, scores, masked_score)
        largest = jnp.max(scores, axis=3)
        weights = jnp.where(readable, jnp.exp(scores - largest[..., None]), 0.0)
        totals = jnp.sum(weights, axis=3)
        probability = (weights / totals[..., None]).astype(jnp.bfloat16)
        attended = jnp.einsum(
            "rhqk,rkhd->rqhd", probability, value_heads, preferred_element_type=jnp.float32
        )
        outputs.append(attended.reshape(row_count, frame_span, group_width))
        log_norms.append(largest + jnp.log(totals))
    return (jnp.concatenate(outputs, axis=2), jnp.concatenate(log_norms, axis=1))


def cross_backward(queries, text_kv, readable, log_norm, d_cross, delta_sum):
    row_count, frame_span, model_width = queries.shape
    slot_count = text_kv.shape[1]
    group_width = group_heads * HD
    score_scale = HD ** (-0.5)
    d_queries = []
    d_keys = []
    d_values = []
    for group_index in range(model_width // group_width):
        lower_edge = group_index * group_width
        head_edge = group_index * group_heads
        query_heads = split_heads(queries[:, :, lower_edge : lower_edge + group_width])
        grad_heads = split_heads(d_cross[:, :, lower_edge : lower_edge + group_width])
        key_heads = split_heads(text_kv[:, :, lower_edge : lower_edge + group_width])
        value_heads = split_heads(
            text_kv[:, :, model_width + lower_edge : model_width + lower_edge + group_width]
        )
        group_norm = log_norm[:, head_edge : head_edge + group_heads]
        group_delta = delta_sum[:, head_edge : head_edge + group_heads]
        scores = (
            jnp.einsum(
                "rqhd,rkhd->rhqk", query_heads, key_heads, preferred_element_type=jnp.float32
            )
            * score_scale
        )
        probability = jnp.where(readable, jnp.exp(scores - group_norm[..., None]), 0.0)
        d_value = jnp.einsum(
            "rhqk,rqhd->rkhd",
            probability.astype(jnp.bfloat16),
            grad_heads,
            preferred_element_type=jnp.float32,
        )
        d_values.append(d_value.reshape(row_count, slot_count, group_width))
        d_prob = jnp.einsum(
            "rqhd,rkhd->rhqk", grad_heads, value_heads, preferred_element_type=jnp.float32
        )
        d_score = (probability * (d_prob - group_delta[..., None])).astype(jnp.bfloat16)
        d_query = jnp.einsum(
            "rhqk,rkhd->rqhd", d_score, key_heads, preferred_element_type=jnp.float32
        )
        d_queries.append(d_query.reshape(row_count, frame_span, group_width) * score_scale)
        d_key = jnp.einsum(
            "rhqk,rqhd->rkhd", d_score, query_heads, preferred_element_type=jnp.float32
        )
        d_keys.append(d_key.reshape(row_count, slot_count, group_width) * score_scale)
    return (jnp.concatenate(d_queries, axis=2), jnp.concatenate(d_keys + d_values, axis=2))


def shards(
    hidden_in,
    clip_lengths,
    text_lengths,
    text_states,
    norm_gain,
    norm_bias,
    self_qkv,
    self_out,
    cross_query,
    cross_kv,
    cross_out,
    ffn_in,
    ffn_out,
    out_grad,
):
    gathered = (
        lax.all_gather(norm_gain, ("rows", "seq"), axis=1, tiled=True),
        lax.all_gather(norm_bias, ("rows", "seq"), axis=1, tiled=True),
        lax.all_gather(self_qkv, ("rows", "seq"), axis=1, tiled=True),
        lax.all_gather(self_out, ("rows", "seq"), axis=0, tiled=True),
        lax.all_gather(cross_query, ("rows", "seq"), axis=0, tiled=True),
        lax.all_gather(cross_kv, ("rows", "seq"), axis=1, tiled=True),
        lax.all_gather(cross_out, ("rows", "seq"), axis=0, tiled=True),
        lax.all_gather(ffn_in, ("rows", "seq"), axis=0, tiled=True),
        lax.all_gather(ffn_out, ("rows", "seq"), axis=0, tiled=True),
    )
    gains_all, biases_all, w_qkv, w_self, w_query, w_text, w_cross, w_up, w_down = gathered
    gains = gains_all.astype(jnp.float32)
    biases = biases_all.astype(jnp.float32)
    row_count, frame_span, model_width = hidden_in.shape
    seq_index = lax.axis_index("seq")
    frames = seq_index * frame_span + jnp.arange(frame_span, dtype=jnp.int32)
    clip_ends = jnp.cumsum(clip_lengths, axis=1)
    clip_ids = clip_of(frames, clip_ends)
    text_ends = jnp.cumsum(text_lengths, axis=1)
    text_starts = text_ends - text_lengths
    chosen = (
        clip_ids[:, :, None] == jnp.arange(clip_lengths.shape[1], dtype=jnp.int32)[None, None, :]
    )
    slot_low = jnp.sum(jnp.where(chosen, text_starts[:, None, :], 0), axis=2)
    slot_high = jnp.sum(jnp.where(chosen, text_ends[:, None, :], 0), axis=2)
    slot_index = jnp.arange(text_states.shape[1], dtype=jnp.int32)
    readable = (
        (slot_index[None, None, :] >= slot_low[:, :, None])
        & (slot_index[None, None, :] < slot_high[:, :, None])
    )[:, None]
    slot_share = text_states.shape[1] // lax.axis_size("seq")
    own_text = lax.dynamic_slice_in_dim(text_states, seq_index * slot_share, slot_share, 1)
    resid = hidden_in.astype(jnp.float32)
    normed_full, pull_first = jax.vjp(layer_norm, resid, gains[0], biases[0])
    normed = normed_full.astype(jnp.bfloat16)
    queries = project(normed, w_qkv[0]).astype(jnp.bfloat16)
    keys_low = project(normed, w_qkv[1]).astype(jnp.bfloat16)
    values_low = project(normed, w_qkv[2]).astype(jnp.bfloat16)
    key_value = jnp.concatenate([keys_low, values_low], axis=2)
    self_full, self_norm = self_forward(queries, key_value, clip_ends, clip_ids, frames)
    attended = self_full.astype(jnp.bfloat16)
    after_self = resid + project(attended, w_self)
    normed_full, pull_second = jax.vjp(layer_norm, after_self, gains[1], biases[1])
    normed_two = normed_full.astype(jnp.bfloat16)
    cross_queries = project(normed_two, w_query).astype(jnp.bfloat16)
    text_kv = lax.all_gather(text_project(own_text, w_text), "seq", axis=1, tiled=True)
    cross_full, cross_norm = cross_forward(cross_queries, text_kv, readable)
    crossed = cross_full.astype(jnp.bfloat16)
    after_cross = after_self + project(crossed, w_cross)
    normed_full, pull_third = jax.vjp(layer_norm, after_cross, gains[2], biases[2])
    normed_three = normed_full.astype(jnp.bfloat16)
    hidden_up = project(normed_three, w_up)
    activated_full, pull_gelu = jax.vjp(gelu_exact, hidden_up)
    activated = activated_full.astype(jnp.bfloat16)
    block_out = (after_cross + project(activated, w_down)).astype(jnp.bfloat16)
    gradient = out_grad.astype(jnp.float32)
    g_down = weight_term(activated, out_grad)
    d_up = pull_gelu(back_project(out_grad, w_down))[0].astype(jnp.bfloat16)
    g_up = weight_term(normed_three, d_up)
    d_third, g_gain_three, g_bias_three = pull_third(back_project(d_up, w_up))
    gradient = gradient + d_third
    grad_low = gradient.astype(jnp.bfloat16)
    g_cross = weight_term(crossed, grad_low)
    d_cross = back_project(grad_low, w_cross).astype(jnp.bfloat16)
    cross_delta = head_dot(d_cross, cross_full)
    d_cross_query, d_text_kv = cross_backward(
        cross_queries, text_kv, readable, cross_norm, d_cross, cross_delta
    )
    key_weight = w_text[0].astype(jnp.float32)
    value_weight = w_text[1].astype(jnp.float32)
    own_grad = lax.psum_scatter(
        d_text_kv.astype(jnp.bfloat16), "seq", scatter_dimension=1, tiled=True
    ).astype(jnp.float32)
    grad_text_key = own_grad[:, :, :model_width]
    grad_text_value = own_grad[:, :, model_width:]
    own_exact = own_text.astype(jnp.float32)
    g_text = jnp.stack(
        [exact_weight_term(own_exact, grad_text_key), exact_weight_term(own_exact, grad_text_value)]
    )
    text_grad = exact_back_project(grad_text_key, key_weight) + exact_back_project(
        grad_text_value, value_weight
    )
    d_cross_query = d_cross_query.astype(jnp.bfloat16)
    g_query = weight_term(normed_two, d_cross_query)
    d_second, g_gain_two, g_bias_two = pull_second(back_project(d_cross_query, w_query))
    gradient = gradient + d_second
    grad_low = gradient.astype(jnp.bfloat16)
    g_self = weight_term(attended, grad_low)
    d_attn = back_project(grad_low, w_self).astype(jnp.bfloat16)
    self_delta = head_dot(d_attn, self_full)
    d_query = self_query_grad(
        queries, key_value, clip_ends, clip_ids, frames, self_norm, self_delta, d_attn
    )
    gathered_stats = (
        lax.all_gather(jnp.swapaxes(self_norm, 1, 2), "seq", axis=1, tiled=True),
        lax.all_gather(jnp.swapaxes(self_delta, 1, 2), "seq", axis=1, tiled=True),
    )
    query_grad = jnp.concatenate([queries, d_attn], axis=2)
    d_key, d_value = self_key_grad(
        query_grad, key_value, clip_ends, clip_ids, frames, gathered_stats
    )
    g_qkv = jnp.stack(
        [weight_term(normed, d_query), weight_term(normed, d_key), weight_term(normed, d_value)]
    )
    d_normed = (
        back_project(d_query, w_qkv[0])
        + back_project(d_key, w_qkv[1])
        + back_project(d_value, w_qkv[2])
    )
    d_first, g_gain_one, g_bias_one = pull_first(d_normed)
    input_grad = gradient + d_first
    g_gain = jnp.stack([g_gain_one, g_gain_two, g_gain_three])
    g_bias = jnp.stack([g_bias_one, g_bias_two, g_bias_three])
    reduced = (
        lax.psum_scatter(g_gain, ("rows", "seq"), scatter_dimension=1, tiled=True),
        lax.psum_scatter(g_bias, ("rows", "seq"), scatter_dimension=1, tiled=True),
        lax.psum_scatter(g_qkv, ("rows", "seq"), scatter_dimension=1, tiled=True),
        lax.psum_scatter(g_self, ("rows", "seq"), scatter_dimension=0, tiled=True),
        lax.psum_scatter(g_query, ("rows", "seq"), scatter_dimension=0, tiled=True),
        lax.psum_scatter(g_text, ("rows", "seq"), scatter_dimension=1, tiled=True),
        lax.psum_scatter(g_cross, ("rows", "seq"), scatter_dimension=0, tiled=True),
        lax.psum_scatter(g_up, ("rows", "seq"), scatter_dimension=0, tiled=True),
        lax.psum_scatter(g_down, ("rows", "seq"), scatter_dimension=0, tiled=True),
    )
    return (
        block_out,
        input_grad,
        text_grad,
        reduced[0],
        reduced[1],
        reduced[2],
        reduced[3],
        reduced[4],
        reduced[5],
        reduced[6],
        reduced[7],
        reduced[8],
    )


MESH = pl.DeviceIdType.MESH
BF = jnp.bfloat16
F32 = jnp.float32
GROUP = 4
NEG = -1e30


def dot(a, b):
    return lax.dot_general(a, b, (((1,), (0,)), ((), ())), preferred_element_type=F32)


def dot_nt(a, b):
    return lax.dot_general(a, b, (((1,), (1,)), ((), ())), preferred_element_type=F32)


def dot_tn(a, b):
    return lax.dot_general(a, b, (((0,), (0,)), ((), ())), preferred_element_type=F32)


def mult(index, step):
    return pl.multiple_of(index * step, step)


def rows_of(index, step):
    return pl.ds(mult(index, step), step)


def each(count, step, body):
    def turn(i, carry):
        body(pl.ds(pl.multiple_of(i * step, step), step))
        return carry

    lax.fori_loop(0, count // step, turn, 0)


def three_parts(value):
    first = value.astype(BF).astype(F32)
    rest = value - first
    second = rest.astype(BF).astype(F32)
    return first, second, (rest - second).astype(BF).astype(F32)


def normalise(values):
    average = jnp.mean(values, axis=-1, keepdims=True)
    centred = values - average
    rstd = lax.rsqrt(jnp.mean(centred * centred, axis=-1, keepdims=True) + epsilon)
    return centred * rstd, rstd


def semaphore_plan(group_chips):
    sizes = dict(
        gb_s=8, gb_r=4, q_s=8, q_r=4, kv_s=8, kv_r=4, in_s=8, in_r=4, ow_g=8, ow_r=4, ow_x=4 * 8,
        n1=48, og=16, n3=16, a_at=8, a_cq=8, a_cr=8, b_cr=8, b_cq=8, b_at=8,
        e_c=4, e_z=4, o_c=4, o_z=4, t_c=4, t_z=8, s_c=4, s_z=8,
        gq_r=8, gq_s=8, gi_r=8, gi_s=8, go_r=8, go_g=8, gk_r=8, gk_s=8, gg_r=4, gg_s=8,
        m_z=12, m_r=12, m_c=6, h_c=6, h_r=24, h_z=24,
    )
    base, plan = 0, {}
    for name, size in sizes.items():
        plan[name] = base
        base += size
    return types.SimpleNamespace(**plan), base


def layer_kernel(plan, names, *refs):
    n = types.SimpleNamespace(**dict(zip(names, refs)))
    R, S, NZ, D = 4, 8, 4, n.x.shape[1]
    TB = n.x.shape[0]
    CH = 2 * TB
    T = S * TB
    HP = D // S
    FF = n.win.shape[1]
    G = GROUP
    GZ = G // 2
    E = S // G
    U = FF // G
    UB = FF // (R * S)
    DB = D // (R * S)
    TW = n.text.shape[1]
    KB = n.wckv.shape[0]
    r, s = lax.axis_index("rows"), lax.axis_index("seq")
    z, c = s // 2, s % 2
    sib = s + 1 - 2 * c
    ffn_z0 = (z // GZ) * GZ
    grp, mem = s // G, s % G
    ss, rs = n.ss, n.rs
    pending = {}
    gbt, Wq3, Wkv3, Win, Wout, winp, ogf = n.gbt, n.Wq3, n.Wkv3, n.Win, n.Wout, n.winp, n.ogf
    mats = [n.Wm0, n.Wm1, n.Wm2]

    def push(src, dst, name, to, origin, dev, send_shift=0, when=None):
        cp = pltpu.make_async_remote_copy(
            src_ref=src, dst_ref=dst,
            send_sem=ss.at[name + send_shift + to],
            recv_sem=rs.at[name + origin],
            device_id=dev, device_id_type=MESH,
        )
        pending.setdefault(name, []).append((cp, when))
        if when is None:
            cp.start()
        else:
            pl.when(when)(cp.start)

    def drain(*which):
        for name in which:
            for cp, when in pending.pop(name, []):
                if when is None:
                    cp.wait_send()
                else:
                    pl.when(when)(cp.wait_send)

    def arrive(landing, name, origin, when=None):
        cp = pltpu.make_async_remote_copy(
            src_ref=landing, dst_ref=landing, send_sem=ss.at[name],
            recv_sem=rs.at[name + origin], device_id=(r, sib), device_id_type=MESH,
        )
        if when is None:
            cp.wait_recv()
        else:
            pl.when(when)(cp.wait_recv)

    side = z // 2
    inner, outer = (z + 1) % NZ // 2 == 1, (z + 1) % NZ // 2 == 0
    beside = z + 1 - 2 * (z % 2)
    far_inner, far_outer = 2 - side, 3 - 3 * side
    legs = (((far_inner, None), (beside, outer)), ((far_outer, None), (beside, inner)))

    def spread(leg, send):
        for zl, when in legs[leg]:
            for core in range(2):
                send(2 * zl + core, when)

    across_x, across_y = r + 1 - 2 * (r % 2), (r + 2) % R
    corner = (across_x + 2) % R

    def plane_start(block, name):
        push(block(r), block(r), name, 0, 0, (across_x, s))
        push(block(r), block(r), name, 1, 1, (across_y, s))

    def plane_pass(block, half, name):
        arrive(block(across_x), name, 0)
        push(half(across_x, 0), half(across_x, 0), name, 2, 2, (across_y, s))
        arrive(block(across_y), name, 1)
        push(half(across_y, 1), half(across_y, 1), name, 3, 3, (across_x, s))

    def plane_take(half, name):
        arrive(half(corner, 0), name, 2)
        arrive(half(corner, 1), name, 3)

    def fold_start(half, landed, name):
        push(half(corner, 0), landed.at[1], name, 1, 1, (across_x, s))
        push(half(corner, 1), landed.at[3], name, 3, 3, (across_y, s))
        push(half(across_x, 0), landed.at[0], name, 0, 0, (across_x, s))
        push(half(across_y, 1), landed.at[2], name, 2, 2, (across_y, s))

    def fold_pass(half, landed, name):
        for k, (near, to) in enumerate(((across_y, across_y), (across_x, across_x))):
            arrive(landed.at[1 + 2 * k], name, 1 + 2 * k)
            mine = half(near, k)
            mine[...] = (mine[...].astype(F32) + landed[1 + 2 * k].astype(F32)).astype(BF)
            push(mine, landed.at[4 + k], name, 4 + k, 4 + k, (to, s))

    def fold_take(half, landed, name):
        for k in range(2):
            arrive(landed.at[2 * k], name, 2 * k)
            arrive(landed.at[4 + k], name, 4 + k)
            mine = half(r, k)
            total = mine[...].astype(F32) + landed[2 * k].astype(F32) + landed[4 + k].astype(F32)
            mine[...] = total.astype(BF)

    def rows_view(ref, step):
        def block(p):
            return ref.at[rows_of(p, step), :]

        def half(p, k):
            return ref.at[rows_of(2 * p + k, step // 2), :]

        return block, half

    def mid_view(ref, step):
        def block(p):
            return ref.at[:, rows_of(p, step), :]

        def half(p, k):
            return ref.at[:, rows_of(2 * p + k, step // 2), :]

        return block, half

    def mat_view(i):
        def block(p):
            return mats[i].at[pl.ds(p * NZ, NZ), c]

        def half(p, k):
            return mats[i].at[pl.ds(p * NZ + 2 * k, 2), c]

        return block, half

    def out_view(j):
        def block(p):
            return Wout.at[rows_of(p * E + (grp + j) % E, UB), :]

        def half(p, k):
            return Wout.at[rows_of(2 * (p * E + (grp + j) % E) + k, UB // 2), :]

        return block, half

    seq_peers = [(s + k) % S for k in range(1, S)]
    row_peers = [(r + k) % R for k in range(1, R)]
    z_peers = [(z + k) % NZ for k in range(1, NZ)]

    finals = []

    def local(src, dst, i):
        cp = pltpu.make_async_copy(src, dst, n.ls.at[i])
        cp.start()
        return cp

    def emit(stage, out, value):
        stage[...] = value
        finals.append(local(stage, out, 16 + len(finals)))

    own_mats = [n.wo, n.wcq, n.wco]
    own_rows = rows_of(r * S + s, DB)
    kv_rows = rows_of(r * S + s, KB)
    out_rows = rows_of(r * E + grp, UB)
    xs, own_tokens = n.ps0, rows_of(s, TB)
    got_x = local(n.x, xs.at[own_tokens, :], 0)
    got_gb = local(n.gb, gbt.at[r, s], 1)
    got_q = local(n.wqkv.at[:, :, rows_of(s, HP)], Wq3.at[:, own_rows, :], 2)
    got_kv = local(n.wckv.at[:, rows_of(s, HP)], Wkv3.at[kv_rows, :], 3)
    got_mats = [local(own_mats[i], mats[i].at[r * NZ + z, c], 4 + i) for i in range(3)]
    for m in range(G):
        for rr in range(R):
            for j in range(E):
                b = rr * S + j * G + m
                at = m * U + (rr * E + j) * UB
                local(n.win.at[:, b * UB : (b + 1) * UB], winp.at[:, at : at + UB], 7)
    got_ow = local(n.wout, Wout.at[out_rows, :], 8)
    got_og = local(n.og, ogf.at[rows_of(mem, TB), :], 9)
    got_text = local(n.text, n.textv, 10)

    barrier = pltpu.get_barrier_semaphore()
    for p in seq_peers:
        pl.semaphore_signal(barrier, inc=1, device_id=(r, p), device_id_type=MESH)
    for p in row_peers:
        pl.semaphore_signal(barrier, inc=1, device_id=(p, s), device_id_type=MESH)
    pl.semaphore_wait(barrier, S + R - 2)

    q_block, q_half = mid_view(Wq3, S * DB)
    kv_block, kv_half = rows_view(Wkv3, S * KB)
    in_block, in_half = rows_view(Win, S * DB)
    ow_block, ow_half = out_view(0)

    def mat_z(i, leg):
        for p, when in legs[leg]:
            dst = mats[i].at[r * NZ + z, c]
            push(own_mats[i], dst, plan.m_z + 4 * i, p, z, (r, 2 * p + c), when=when)

    def mat_r(i):
        for p in z_peers:
            arrive(mats[i].at[r * NZ + p, c], plan.m_z + 4 * i, p)
        got_mats[i].wait()
        plane_start(mat_view(i)[0], plan.m_r + 4 * i)

    def mat_p(i):
        plane_pass(*mat_view(i), plan.m_r + 4 * i)

    def mat_c(i):
        plane_take(mat_view(i)[1], plan.m_r + 4 * i)
        block = mats[i].at[:, c]
        push(block, block, plan.m_c + 2 * i, 0, 0, (r, sib))

    def mat_take(i):
        arrive(mats[i].at[:, 1 - c], plan.m_c + 2 * i, 0)

    def mat(i):
        return mats[i][...].reshape(D, D)

    def kv_send(p, when):
        src = n.wckv.at[:, rows_of(p, HP)]
        push(src, Wkv3.at[kv_rows, :], plan.kv_s, p, s, (r, p), when=when)

    def kv_first():
        kv_send(sib, None)
        spread(0, kv_send)

    def kv_plane():
        for p in seq_peers:
            arrive(Wkv3.at[rows_of(r * S + p, KB), :], plan.kv_s, p)
        got_kv.wait()
        plane_start(kv_block, plan.kv_r)

    def kv_pass():
        plane_pass(kv_block, kv_half, plan.kv_r)

    def in_send(p, when):
        src = winp.at[:, rows_of(p % G, U)]
        push(src, Win.at[own_rows, :], plan.in_s, p, s, (r, p), when=when)

    def in_first():
        in_send(sib, None)
        spread(0, in_send)

    def in_plane():
        for p in seq_peers:
            arrive(Win.at[rows_of(r * S + p, DB), :], plan.in_s, p)
        plane_start(in_block, plan.in_r)

    def in_pass():
        plane_pass(in_block, in_half, plan.in_r)

    def ow_send(when):
        for j in range(1, E):
            p = (s + j * G) % S
            push(n.wout, Wout.at[out_rows, :], plan.ow_g, p, s, (r, p), when=when)

    def ow_first():
        push(n.wout, ow_block(r), plan.ow_r, 0, 0, (across_x, s))
        push(n.wout, ow_block(r), plan.ow_r, 1, 1, (across_y, s))

    def ow_pass():
        plane_pass(ow_block, ow_half, plan.ow_r)

    def ow_second():
        for j in range(1, E):
            arrive(out_view(j)[0](r), plan.ow_g, (s + j * G) % S)
            plane_start(out_view(j)[0], plan.ow_x + 4 * j)

    def ow_second_pass():
        for j in range(1, E):
            plane_pass(*out_view(j), plan.ow_x + 4 * j)

    def gather_start(buf, name, z0, nz):
        m = s - 2 * z0
        block = buf.at[rows_of(m, TB), :]
        for k in range(1, nz):
            zl = (z - z0 + k) % nz
            push(block, block, name, 2 * zl + c, m, (r, 2 * (z0 + zl) + c))
        push(block, block, name, sib - 2 * z0, m, (r, sib))

    def og_start():
        got_og.wait()
        gather_start(ogf, plan.og, ffn_z0, GZ)

    for p in seq_peers:
        push(n.gb, gbt.at[r, s], plan.gb_s, p, s, (r, p))
    for p in seq_peers:
        push(n.wqkv.at[:, :, rows_of(p, HP)], Wq3.at[:, own_rows, :], plan.q_s, p, s, (r, p))

    mat_z(1, 1)
    mat_z(1, 0)
    spread(1, kv_send)
    TH = TB // 2
    for q in range(2):
        src, dst = n.x.at[q * TH : (q + 1) * TH, :], xs.at[rows_of(2 * s + q, TH), :]
        for zl in (far_inner, beside):
            push(src, dst, plan.n1 + 24 * q, 2 * zl + c, s, (r, 2 * zl + c))
        push(src, dst, plan.n1 + 24 * q, sib, s, (r, sib))

    for p in seq_peers:
        arrive(gbt.at[r, p], plan.gb_s, p)
    got_gb.wait()
    for p in row_peers:
        push(gbt.at[r], gbt.at[r], plan.gb_r, p, r, (p, s))
    pltpu.make_async_copy(n.win, winp, n.ls.at[7]).wait()
    Win[own_rows, :] = winp[:, rows_of(mem, U)]
    ow_first()
    mat_z(0, 1)
    for p in seq_peers:
        arrive(Wq3.at[:, rows_of(r * S + p, DB), :], plan.q_s, p)
    got_q.wait()
    plane_start(q_block, plan.q_r)
    mat_z(0, 0)

    lane = lax.broadcasted_iota(jnp.int32, (T, HP), 1)
    row = lax.broadcasted_iota(jnp.int32, (T, HP), 0)
    slot = lane % HD
    cl, tl = n.cl, n.tl

    def inside(lengths):
        low, found = jnp.int32(0), jnp.zeros((T, HP), jnp.bool_)
        for k in range(4):
            high = low + lengths[0, k]
            found = found | ((slot == k) & (row >= low) & (row < high))
            low = high
        return found

    ones_tail = jnp.where((slot >= 4) & (slot < 7), 1.0, 0.0)

    def mask_block():
        in_clip = inside(cl)
        n.oh[...] = jnp.where(in_clip, 1.0, 0.0).astype(BF)
        n.kbs[...] = jnp.where(slot < 4, jnp.where(in_clip, 0.0, NEG), ones_tail).astype(BF)
        n.kbc[...] = jnp.where(slot < 4, jnp.where(inside(tl), 0.0, NEG), ones_tail).astype(BF)

    mask_block()

    for p in row_peers:
        arrive(gbt.at[p], plan.gb_r, p)
    per = 128 // DB
    gbf = n.gbf
    for g in range(D // 128):
        total = None
        for k in range(per):
            rr, sx = divmod(g * per + k, S)
            tile = gbt[rr, sx].astype(F32)
            total = tile if total is None else total + tile
        gbf[:, g * 128 : (g + 1) * 128] = total

    def gain(i):
        return gbf[i : i + 1, :]

    def bias(i):
        return gbf[3 + i : 4 + i, :]

    def first_half(shape):
        return lax.broadcasted_iota(jnp.int32, shape, 1) < HD

    def split_pair(value, other):
        front = first_half(value.shape)
        v, o = value.astype(F32), other.astype(F32)
        return jnp.where(front, v, o).astype(BF), jnp.where(front, o, v).astype(BF)

    def gather_pass(buf, name, z0, nz, k):
        zl = (z - z0 + k) % nz
        if k:
            block = buf.at[rows_of(2 * zl + c, TB), :]
            arrive(block, name, 2 * zl + c)
            push(block, block, name, 2 * zl + c, 2 * zl + c, (r, sib), send_shift=8)

    def gather_take(buf, name, z0, nz, k):
        zl = (z - z0 + k) % nz
        arrive(buf.at[rows_of(2 * zl + 1 - c, TB), :], name, 2 * zl + 1 - c)
        return rows_of(zl, CH)

    def chain_pass(zl, q):
        origin, name = 2 * zl + c, plan.n1 + 24 * q
        block = xs.at[rows_of(2 * origin + q, TH), :]
        arrive(block, name, origin)
        push(block, block, name, 16 + origin, origin, (r, 2 * beside + c), when=inner & (zl // 2 != side))
        push(block, block, name, 8 + origin, origin, (r, sib))

    def chain_take(zl):
        origin = 2 * zl + 1 - c
        for q in range(2):
            arrive(xs.at[rows_of(2 * origin + q, TH), :], plan.n1 + 24 * q, origin)
        return rows_of(zl, CH)

    n1f, Wq = n.n1f, n.Wq
    Q, K, V = n.Q, n.K, n.V
    KA = n.KA
    scale = HD ** (-0.5)

    def norm_rows(rows):
        xh = normalise(xs[rows, :].astype(F32))[0]
        n1f[rows, :] = (xh * gain(0) + bias(0)).astype(BF)

    def qkv_chunk(rows):
        def block():
            qkv_block(rows)

        block()

    def qkv_block(rows):
        got = dot(n1f[rows, :], Wq[...])
        Q[rows, :] = (got[:, :HP].astype(BF).astype(F32) * scale).astype(BF)
        K[rows, :] = got[:, HP : 2 * HP].astype(BF)
        V[rows, :] = got[:, 2 * HP :].astype(BF)
        KA[0, rows, :], KA[1, rows, :] = split_pair(K[rows, :], n.kbs[rows, :])

    got_x.wait()
    rows = chain_take(z)
    norm_rows(rows)
    kv_first()
    chain_pass(far_inner, 0)
    chain_pass(far_outer, 0)
    in_first()
    mat_r(1)
    mat_z(2, 0)
    plane_pass(q_block, q_half, plan.q_r)
    chain_pass(far_inner, 1)
    chain_pass(far_outer, 1)
    mat_r(0)
    mat_z(2, 1)
    rows_1 = chain_take(far_inner)
    norm_rows(rows_1)
    og_start()
    rows_2 = chain_take(far_outer)
    norm_rows(rows_2)
    ow_pass()
    kv_plane()
    mat_p(1)
    plane_take(q_half, plan.q_r)
    for i in range(3):
        Wq[:, i * HP : (i + 1) * HP] = Wq3[i]
    qkv_chunk(rows)
    qkv_chunk(rows_1)
    qkv_chunk(rows_2)
    chain_pass(beside, 0)
    chain_pass(beside, 1)
    rows = chain_take(beside)
    norm_rows(rows)
    qkv_chunk(rows)
    spread(1, in_send)
    CK, CV = n.CK, n.CV
    half = KB // 2
    Wkv = n.Wkv

    def text_rows(rows):
        got = dot(n.textv[rows, :], Wkv[...]).astype(BF)
        CK[rows, :] = got[:, :HP]
        CV[rows, :] = got[:, HP:]

    def text_block():
        each(T, CH, text_rows)

    def text_all():
        plane_take(kv_half, plan.kv_r)
        wide = Wkv3[...].astype(F32).reshape(R * S, KB, HP)
        Wkv[:, :HP] = wide[:, :half, :].reshape(TW, HP).astype(BF)
        Wkv[:, HP:] = wide[:, half:, :].reshape(TW, HP).astype(BF)
        got_text.wait()
        text_block()

    AF, QB = n.AF, n.QB
    oh = n.oh
    AB = n.out
    ao = n.ao

    def finish(o0, o1, l0, l1):
        return jnp.where(first_half(o0.shape), o0 / l0, o1 / l1)

    def with_norm(q_aug, head, norm):
        spot = lax.broadcasted_iota(jnp.int32, q_aug.shape, 1)
        base = (1 - head) * HD
        a, b, d = three_parts(-norm)
        w = q_aug.astype(F32)
        w = jnp.where(spot == base + 4, a, w)
        w = jnp.where(spot == base + 5, b, w)
        return jnp.where(spot == base + 6, d, w).astype(BF)

    kpos = lax.broadcasted_iota(jnp.int32, (CH, CH), 1)
    qpos = lax.broadcasted_iota(jnp.int32, (CH, CH), 0)
    def self_rows(i, low, high):
        qa = split_pair(Q[low:high, :], oh[low:high, :])
        outs, sums = [], []
        for h in range(2):
            diag = jnp.where(kpos <= qpos, dot_nt(qa[h], KA[h, low:high, :]), NEG)
            top = jnp.max(diag, axis=1, keepdims=True)
            if i:
                left = dot_nt(qa[h], KA[h, :low, :])
                top = jnp.maximum(top, jnp.max(left, axis=1, keepdims=True))
            diag = jnp.exp(diag - top)
            total = jnp.sum(diag, axis=1, keepdims=True)
            got = dot(diag.astype(BF), V[low:high, :])
            if i:
                left = jnp.exp(left - top)
                total = total + jnp.sum(left, axis=1, keepdims=True)
                got = got + dot(left.astype(BF), V[:low, :])
            outs.append(got)
            sums.append(total)
            QB[h, low:high, :] = with_norm(qa[h], h, top + jnp.log(total))
        full = finish(outs[0], outs[1], sums[0], sums[1])
        AF[low:high, :] = full
        AB[low:high, :] = full.astype(BF)

    def self_part(i):
        def self_block():
            self_rows(i, i * CH, (i + 1) * CH)

        self_block()
        for p in (2 * i, 2 * i + 1):
            src, dst = AB.at[p * TB : (p + 1) * TB, :], ao.at[:, rows_of(s, HP)]
            push(src, dst, plan.a_at, p, s, (r, p), when=s != p)

    self_part(0)
    mat_p(0)
    self_part(1)
    mat_r(2)
    self_part(2)
    self_part(3)
    ao[:, rows_of(s, HP)] = AB[rows_of(s, TB), :]

    ow_send(outer)
    mat_c(0)
    kv_pass()
    mat_p(2)
    xh, rstd = normalise(xs[own_tokens, :].astype(F32))
    n.XH[0] = xh
    n.RS[0] = rstd
    mat_take(0)
    for p in seq_peers:
        arrive(ao.at[:, rows_of(p, HP)], plan.a_at, p)
    h1 = xs[own_tokens, :].astype(F32) + dot(ao[...], mat(0))
    n.H[...] = h1
    xh, rstd = normalise(h1)
    n.XH[1] = xh
    n.RS[1] = rstd
    n2 = (xh * gain(1) + bias(1)).astype(BF)
    n.n2[...] = n2
    ow_send(inner)
    mat_c(1)
    in_plane()
    mat_take(1)
    cqo = n.wide
    cqo[...] = dot(n2, mat(1)).astype(BF)
    CQ = n.CQ

    def to_heads(src, dst, name):
        for k in range(1, S):
            p = (s + k) % S
            push(src.at[:, rows_of(p, HP)], dst.at[own_tokens, :], name, p, s, (r, p))
        dst[own_tokens, :] = src[:, rows_of(s, HP)]

    def heads_take(dst, name, k):
        zl = (z + k) % NZ
        if k:
            arrive(dst.at[rows_of(2 * zl + c, TB), :], name, 2 * zl + c)
        arrive(dst.at[rows_of(2 * zl + 1 - c, TB), :], name, 2 * zl + 1 - c)
        return rows_of(zl, CH)

    def to_tokens(src, dst, name, k):
        zl = (z + k) % NZ
        for p in ([2 * zl + c] if k else []) + [2 * zl + 1 - c]:
            push(src.at[rows_of(p, TB), :], dst.at[:, rows_of(s, HP)], name, p, s, (r, p))
        if not k:
            dst[:, rows_of(s, HP)] = src[own_tokens, :]

    to_heads(cqo, CQ, plan.a_cq)
    text_all()
    ow_second()

    CKA, CVA, CKT, CQB = n.CKA, n.CVA, n.CKT, n.CQB
    CF, CB, co = n.CF, n.out, n.co
    drain(plan.a_at)

    def prepare_cross(rows):
        CKA[0, rows, :], CKA[1, rows, :] = split_pair(CK[rows, :], n.kbc[rows, :])

    each(T, CH, prepare_cross)
    def cross_rows(rows):
        scaled = (CQ[rows, :].astype(F32) * scale).astype(BF)
        CQ[rows, :] = scaled
        qa = split_pair(scaled, oh[rows, :])
        outs, sums = [], []
        for h in range(2):
            got = dot_nt(qa[h], CKA[h])
            top = jnp.max(got, axis=1, keepdims=True)
            got = jnp.exp(got - top)
            total = jnp.sum(got, axis=1, keepdims=True)
            outs.append(dot(got.astype(BF), CV[...]))
            sums.append(total)
            CQB[h, rows, :] = with_norm(qa[h], h, top + jnp.log(total))
        full = finish(outs[0], outs[1], sums[0], sums[1])
        CF[rows, :] = full
        CB[rows, :] = full.astype(BF)

    def cross_part(k):
        rows = heads_take(CQ, plan.a_cq, k)

        def cross_block():
            cross_rows(rows)

        cross_block()
        to_tokens(CB, co, plan.a_cr, k)

    cross_part(0)
    mat_c(2)
    cross_part(1)
    cross_part(2)
    in_pass()
    cross_part(3)
    mat_take(2)
    for p in seq_peers:
        arrive(co.at[:, rows_of(p, HP)], plan.a_cr, p)
    h2 = n.H[...] + dot(co[...], mat(2))
    n.H[...] = h2
    xh, rstd = normalise(h2)
    n.XH[2] = xh
    n.RS[2] = rstd
    n3f = n.n3f
    n3f[rows_of(mem, TB), :] = (xh * gain(2) + bias(2)).astype(BF)
    gather_start(n3f, plan.n3, ffn_z0, GZ)

    got_ow.wait()
    ow_second_pass()
    plane_take(in_half, plan.in_r)
    plane_take(ow_half, plan.ow_r)
    for j in range(1, E):
        plane_take(out_view(j)[1], plan.ow_x + 4 * j)
    AD = n.AD
    ACT, DUP = AD.at[: G * TB], AD.at[G * TB :]
    UT = 512

    def reduce_core(ps, rb, name, zl):
        push(ps.at[rows_of(2 * zl + 1 - c, TB), :], rb.at[zl], name, zl, zl, (r, sib))

    def reduce_z(ps, rb, rz, cname, zname, z0, nz, zl, when=None):
        arrive(rb.at[zl], cname, zl)
        mine = rows_of(2 * zl + c, TB)
        ps[mine, :] = (ps[mine, :].astype(F32) + rb[zl].astype(F32)).astype(BF)
        push(ps.at[mine, :], rz.at[(z - z0 - zl + nz - 1) % nz], zname, zl, z - z0, (r, 2 * (z0 + zl) + c), when=when)

    def reduce_take(ps, rb, rz, cname, zname, z0, nz, summed=False):
        own = z - z0
        mine = rows_of(2 * own + c, TB)
        total = ps[mine, :].astype(F32)
        if not summed:
            arrive(rb.at[own], cname, own)
            total = total + rb[own].astype(F32)
        for k in range(1, nz):
            zl = (own + k) % nz
            arrive(rz.at[k - 1], zname, zl)
            total = total + rz[k - 1].astype(F32)
        return total

    def chain_send(mine, land, name, j):
        push(mine, land.at[0], name, 0, 0, (r, 2 * beside + c), when=beside == j)
        push(mine, land.at[1 + j % 2], name, 1 + j % 2, 1 + j % 2, (r, 2 * beside + c), when=outer & (j // 2 != side))

    def chain_relay(at, land, name):
        for k in range(2):
            to = 2 - 2 * side + k
            mine = at(to)

            def add():
                arrive(land.at[1 + k], name, 1 + k)
                mine[...] = (mine[...].astype(F32) + land[1 + k].astype(F32)).astype(BF)

            pl.when(inner)(add)
            push(mine, land.at[3], name, 3 + k, 3, (r, 2 * to + c), when=inner)

    def chain_total(at, land, name):
        arrive(land.at[0], name, 0)
        arrive(land.at[3], name, 3)
        return at(z)[...].astype(F32) + land[0].astype(F32) + land[3].astype(F32)

    def core_sum(ps, rb, cname, j):
        arrive(rb.at[j], cname, j)
        mine = ps.at[rows_of(2 * j + c, TB), :]
        mine[...] = (mine[...].astype(F32) + rb[j].astype(F32)).astype(BF)
        return mine

    def rows_at(ps):
        def at(j):
            return ps.at[rows_of(2 * j + c, TB), :]

        return at

    ps0 = n.ps0
    drain(plan.n1, plan.n1 + 24)
    NT = G * TB
    psE = ps0.at[:NT]
    psO = ps0.at[NT:]
    for k in range(GZ):
        gather_pass(ogf, plan.og, ffn_z0, GZ, k)
        gather_take(ogf, plan.og, ffn_z0, GZ, k)
        gather_pass(n3f, plan.n3, ffn_z0, GZ, k)
        rows = gather_take(n3f, plan.n3, ffn_z0, GZ, k)

        def hidden(cols):
            up = dot(n3f[rows, :], Win[:, cols])
            d_act = dot_nt(ogf[rows, :], Wout[cols, :])
            cdf = 0.5 * (1.0 + lax.erf(up * (0.5**0.5)))
            pdf = jnp.exp(-0.5 * up * up) * 0.3989422804014327
            ACT[rows, cols] = (up * cdf).astype(BF)
            DUP[rows, cols] = (d_act * (cdf + up * pdf)).astype(BF)

        def hidden_block():
            each(U, UT, hidden)

        def back_block():
            psE[rows, :] = dot_nt(DUP[rows, :], Win[...]).astype(BF)

        hidden_block()
        back_block()
        zl = (z - ffn_z0 + k) % GZ
        reduce_core(psE, n.rbE, plan.e_c, zl)
    for k in range(1, GZ):
        reduce_z(psE, n.rbE, n.rzE, plan.e_c, plan.e_z, ffn_z0, GZ, (z - ffn_z0 + k) % GZ)
    drain(plan.ow_r, plan.ow_g, plan.in_r, plan.in_s, *[plan.ow_x + 4 * j for j in range(1, E)])

    def out_core():
        for k in range(GZ):
            reduce_core(psO, n.rbO, plan.o_c, (z - ffn_z0 + k) % GZ)

    def out_z():
        for k in range(1, GZ):
            zl = (z - ffn_z0 + k) % GZ
            reduce_z(psO, n.rbO, n.rzO, plan.o_c, plan.o_z, ffn_z0, GZ, zl)

    def out_take():
        total = n.H[...] + reduce_take(psO, n.rbO, n.rzO, plan.o_c, plan.o_z, ffn_z0, GZ)
        emit(n.s_out, n.o_out, total.astype(BF))

    def gin_rows(cols):
        Win[cols, :] = dot_tn(n3f[:, cols], DUP[...]).astype(BF)

    def gin_block():
        each(D, 256, gin_rows)

    def gin_start():
        gin_block()
        fold_start(in_half, n.rgi, plan.gi_r)

    def gin_pass():
        fold_pass(in_half, n.rgi, plan.gi_r)

    rgi2 = n.rgi2

    def gin_send():
        fold_take(in_half, n.rgi, plan.gi_r)
        for p in seq_peers:
            push(Win.at[rows_of(r * S + p, DB), :], rgi2.at[s], plan.gi_s, p, s, (r, p))
        rgi2[s] = Win[own_rows, :]

    go_half = rows_view(Wout, E * UB)[1]
    rgo2 = n.rgo2

    def gout_pass():
        fold_pass(go_half, n.rgo, plan.go_r)

    def gout_send():
        fold_take(go_half, n.rgo, plan.go_r)
        for j in range(1, E):
            src = Wout.at[rows_of(r * E + (grp + j) % E, UB), :]
            p = (s + j * G) % S
            push(src, rgo2.at[grp], plan.go_g, p, s, (r, p))

    def mat_grad(i, left, right):
        drain(plan.m_z + 4 * i, plan.m_r + 4 * i, plan.m_c + 2 * i)

        def mat_block():
            mats[i][...] = dot_tn(left, right).astype(BF).reshape(mats[i].shape)

        mat_block()
        push(mats[i].at[:, 1 - c], n.rmc.at[i], plan.h_c + 2 * i, 0, 0, (r, sib))

    def mat_grad_2():
        mat_grad(2, co[...], n.GR[...].astype(BF))

    def mat_grad_1():
        mat_grad(1, n.n2[...], n.dqo[...])

    def mat_grad_0():
        mat_grad(0, ao[...], n.GR[...].astype(BF))

    def mat_grad_r(i):
        arrive(n.rmc.at[i], plan.h_c + 2 * i, 0)
        mine = mats[i].at[:, c]
        mine[...] = (mine[...].astype(F32) + n.rmc[i].astype(F32)).astype(BF)
        fold_start(mat_view(i)[1], n.rmr.at[i], plan.h_r + 8 * i)

    def mat_grad_p(i):
        fold_pass(mat_view(i)[1], n.rmr.at[i], plan.h_r + 8 * i)

    def mat_at(i):
        def at(j):
            return mats[i].at[r * NZ + j, c]

        return at

    def mat_grad_z(i):
        fold_take(mat_view(i)[1], n.rmr.at[i], plan.h_r + 8 * i)
        for j in range(NZ):
            chain_send(mat_at(i)(j), n.rmz.at[i], plan.h_z + 8 * i, j)

    def mat_grad_f(i):
        chain_relay(mat_at(i), n.rmz.at[i], plan.h_z + 8 * i)

    def mat_grad_take(i, stage, out):
        emit(stage, out, chain_total(mat_at(i), n.rmz.at[i], plan.h_z + 8 * i))

    psT = AD.at[:T, :TW]
    DKV = n.DKV
    GC, GQ = n.GC, n.GQ

    def text_send():
        for j in range(NZ):
            chain_send(core_sum(psT, n.rbT, plan.t_c, j), n.rzT, plan.t_z, j)

    def text_relay():
        chain_relay(rows_at(psT), n.rzT, plan.t_z)

    def sum_relay():
        chain_relay(rows_at(ps0), n.rz0, plan.s_z)

    span = TW // 2

    def gkv_rows(i):
        got = dot_tn(n.textv[:, i * span : (i + 1) * span], DKV[...])
        both = [got[:, q * HP : (q + 1) * HP].reshape(span // half, half, HP) for q in range(2)]
        both = jnp.concatenate(both, axis=1).reshape(2 * span, HP)
        Wkv3[2 * i * span : 2 * (i + 1) * span, :] = both.astype(BF)

    def gkv_block():
        gkv_rows(0)
        gkv_rows(1)

    def gkv_start():
        drain(plan.kv_s, plan.kv_r)
        gkv_block()
        fold_start(kv_half, n.rgk, plan.gk_r)

    def gkv_pass():
        fold_pass(kv_half, n.rgk, plan.gk_r)

    def gkv_send():
        fold_take(kv_half, n.rgk, plan.gk_r)
        for p in seq_peers:
            src = Wkv3.at[rows_of(r * S + p, KB), :]
            push(src, GC.at[:, rows_of(s, HP)], plan.gk_s, p, s, (r, p))
        GC[:, rows_of(s, HP)] = Wkv3[kv_rows, :]

    def gq_rows(cols):
        got = dot_tn(n1f[:, cols], n.DQKV[...]).astype(BF)
        for i in range(3):
            Wq3[i, cols, :] = got[:, i * HP : (i + 1) * HP]

    def gq_block():
        each(D, 256, gq_rows)

    def gq_start():
        drain(plan.q_s, plan.q_r)
        gq_block()
        fold_start(q_half, n.rgq, plan.gq_r)

    def gq_pass():
        fold_pass(q_half, n.rgq, plan.gq_r)

    def gq_send():
        fold_take(q_half, n.rgq, plan.gq_r)
        for p in seq_peers:
            src = Wq3.at[:, rows_of(r * S + p, DB), :]
            push(src, GQ.at[:, :, rows_of(s, HP)], plan.gq_s, p, s, (r, p))
        GQ[:, :, rows_of(s, HP)] = Wq3[:, own_rows, :]

    gin_start()
    for k in range(GZ):
        rows = rows_of((z - ffn_z0 + k) % GZ, CH)

        def out_block_rows():
            psO[rows, :] = dot(ACT[rows, :], Wout[...]).astype(BF)

        out_block_rows()

    def gout_rows(cols):
        Wout[cols, :] = dot_tn(ACT[:, cols], ogf[...]).astype(BF)

    def gout_block():
        each(U, 256, gout_rows)

    gout_block()
    fold_start(go_half, n.rgo, plan.go_r)
    out_core()

    def norm_back(i, e):
        n.gg[i : i + 1, :] = jnp.sum(e * n.XH[i], axis=0, keepdims=True)
        n.gg[3 + i : 4 + i, :] = jnp.sum(e, axis=0, keepdims=True)
        y = e * gain(i)
        xhat = n.XH[i]
        a = jnp.mean(y, axis=1, keepdims=True)
        b = jnp.mean(y * xhat, axis=1, keepdims=True)
        return (y - a - xhat * b) * n.RS[i]

    e = reduce_take(psE, n.rbE, n.rzE, plan.e_c, plan.e_z, ffn_z0, GZ)
    g2 = ogf[rows_of(mem, TB), :].astype(F32) + norm_back(2, e)
    n.GR[...] = g2
    dco = n.wide
    drain(plan.a_cq)
    dco[...] = dot_nt(g2.astype(BF), mat(2)).astype(BF)
    DC = n.DC
    to_heads(dco, DC, plan.b_cr)
    mat_grad_2()

    def ones_rows(count):
        spot = lax.broadcasted_iota(jnp.int32, (count, HP), 1) % HD
        return jnp.where((spot >= 4) & (spot < 7), 1.0, 0.0)

    def prepare_cross_back(rows):
        CVA[0, rows, :], CVA[1, rows, :] = split_pair(CV[rows, :], ones_rows(CH))
        CKT[:, rows] = jnp.transpose(CK[rows, :].astype(F32)).astype(BF)

    def with_delta(grad, full):
        front = first_half(grad.shape)
        wide = grad.astype(F32)
        prod = wide * full
        d0 = jnp.sum(jnp.where(front, prod, 0.0), axis=1, keepdims=True)
        d1 = jnp.sum(jnp.where(front, 0.0, prod), axis=1, keepdims=True)
        zero = jnp.zeros_like(wide)
        return (
            with_norm(jnp.where(front, wide, zero), 0, d0),
            with_norm(jnp.where(front, zero, wide), 1, d1),
        )

    each(T, CH, prepare_cross_back)
    DCK, DCV, DQ, dqo = n.DCK, n.DCV, n.out, n.dqo
    drain(plan.a_cr)

    def heads_join(a, b, axis):
        spot = lax.broadcasted_iota(jnp.int32, a.shape, axis)
        return jnp.where(spot < HD, a, b)

    def cross_back_rows(k, rows):
        grad = DC[rows, :]
        ga = with_delta(grad, CF[rows, :])
        q2 = CQ[rows, :]
        dv, dk, dq = [], [], []
        for h in range(2):
            prob = jnp.exp(dot_nt(CKA[h], CQB[h, rows, :]))
            ds = (prob * dot_nt(CVA[h], ga[h])).astype(BF)
            dv.append(dot(prob.astype(BF), grad))
            dk.append(dot(ds, q2))
            dq.append(dot(CKT[...], ds))
        dvj, dkj = heads_join(dv[0], dv[1], 1), heads_join(dk[0], dk[1], 1)
        if k:
            DCV[...] += dvj
            DCK[...] += dkj
        else:
            DCV[...] = dvj
            DCK[...] = dkj
        DQ[rows, :] = (jnp.transpose(heads_join(dq[0], dq[1], 0)) * scale).astype(BF)

    def cross_back_part(k):
        rows = heads_take(DC, plan.b_cr, k)

        def cross_back_block():
            cross_back_rows(k, rows)

        cross_back_block()
        to_tokens(DQ, dqo, plan.b_cq, k)

    cross_back_part(0)
    gin_pass()
    out_z()
    cross_back_part(1)
    cross_back_part(2)
    mat_grad_r(2)
    cross_back_part(3)

    DKV[:, :HP] = DCK[...].astype(BF)
    DKV[:, HP:] = DCV[...].astype(BF)
    for j in range(NZ):
        rows = pl.ds(j * CH, CH)

        def text_back():
            psT[rows, :] = dot_nt(DKV[rows, :], Wkv[...]).astype(BF)

        text_back()
        reduce_core(psT, n.rbT, plan.t_c, j)
    text_send()

    for p in seq_peers:
        arrive(dqo.at[:, rows_of(p, HP)], plan.b_cq, p)
    e = dot_nt(dqo[...], mat(1))
    g1 = n.GR[...] + norm_back(1, e)
    n.GR[...] = g1
    dao = n.wide
    drain(plan.b_cr)
    dao[...] = dot_nt(g1.astype(BF), mat(0)).astype(BF)
    DA = n.DA
    to_heads(dao, DA, plan.b_at)
    gout_pass()
    gkv_start()
    gin_send()
    mat_grad_1()
    mat_grad_0()
    gout_send()

    VA, KT, DOA = CVA, CKT, CQB
    DQT, DQKV = n.DQT, n.DQKV

    def prepare_self_back(rows):
        VA[0, rows, :], VA[1, rows, :] = split_pair(V[rows, :], ones_rows(CH))
        KT[:, rows] = jnp.transpose(K[rows, :].astype(F32)).astype(BF)

    each(T, CH, prepare_self_back)
    for k in range(NZ):
        rows = heads_take(DA, plan.b_at, k)
        DOA[0, rows, :], DOA[1, rows, :] = with_delta(DA[rows, :], AF[rows, :])
    mat_grad_p(2)
    mat_grad_r(0)
    text_relay()
    out_take()
    drain(plan.e_c, plan.e_z, plan.o_c, plan.o_z)

    def self_back_rows(j, low, high):
        grad, q2 = DA[low:, :], Q[low:, :]
        dv, dk, dq = [], [], []
        for h in range(2):
            sc = dot_nt(KA[h, low:high, :], QB[h, low:, :])
            head = jnp.where(qpos <= kpos, sc[:, :CH], NEG)
            sc = jnp.concatenate([head, sc[:, CH:]], axis=1) if j < NZ - 1 else head
            prob = jnp.exp(sc)
            ds = (prob * dot_nt(VA[h, low:high, :], DOA[h, low:, :])).astype(BF)
            dv.append(dot(prob.astype(BF), grad))
            dk.append(dot(ds, q2))
            dq.append(dot(KT[:, low:high], ds))
        if j:
            DQT[:, low:] += heads_join(dq[0], dq[1], 0)
        else:
            DQT[...] = heads_join(dq[0], dq[1], 0)
        DQKV[low:high, :HP] = (jnp.transpose(DQT[:, low:high]) * scale).astype(BF)
        DQKV[low:high, HP : 2 * HP] = heads_join(dk[0], dk[1], 1).astype(BF)
        DQKV[low:high, 2 * HP :] = heads_join(dv[0], dv[1], 1).astype(BF)
        ps0[low:high, :] = dot_nt(DQKV[low:high, :], Wq[...]).astype(BF)

    def self_back_part(j):
        def self_back_block():
            self_back_rows(j, j * CH, (j + 1) * CH)

        self_back_block()
        reduce_core(ps0, n.rb0, plan.s_c, j)
        if j:
            chain_send(core_sum(ps0, n.rb0, plan.s_c, j - 1), n.rz0, plan.s_z, j - 1)

    self_back_part(0)
    self_back_part(1)
    gkv_pass()
    self_back_part(2)
    self_back_part(3)
    mat_grad_r(1)
    mat_grad_p(1)
    chain_send(core_sum(ps0, n.rb0, plan.s_c, NZ - 1), n.rz0, plan.s_z, NZ - 1)
    mat_grad_p(0)
    mat_grad_z(2)
    sum_relay()
    gq_start()
    mat_grad_z(0)
    mat_grad_f(2)
    mat_grad_z(1)

    e = chain_total(rows_at(ps0), n.rz0, plan.s_z)
    back = norm_back(0, e)
    gg, rgg, gg2, rgg2 = n.gg, n.rgg, n.gg2, n.rgg2
    GW = D // R
    for k, p in enumerate(row_peers, 1):
        push(gg.at[:, rows_of(p, GW)], rgg.at[R - 1 - k], plan.gg_r, p, r, (p, s))
    emit(n.s_ig, n.o_ig, n.GR[...] + back)
    mat_grad_f(0)
    mat_grad_f(1)
    gq_pass()
    total = gg[:, rows_of(r, GW)]
    for k, p in enumerate(row_peers):
        arrive(rgg.at[k], plan.gg_r, p)
        total = total + rgg[k]
    gg2[...] = total
    for p in seq_peers:
        push(gg2.at[:, rows_of(p // per, 128)], rgg2.at[s], plan.gg_s, p, s, (r, p))
    gkv_send()
    gq_send()
    mat_grad_take(2, n.s_co, n.o_co)
    mat_grad_take(1, n.s_cq, n.o_cq)
    mat_grad_take(0, n.s_so, n.o_so)
    emit(n.s_tg, n.o_tg, chain_total(rows_at(psT), n.rzT, plan.t_z))
    total = Wout[out_rows, :].astype(F32)
    for j in range(1, E):
        g2i = (grp + j) % E
        arrive(rgo2.at[g2i], plan.go_g, (s + j * G) % S)
        total = total + rgo2[g2i].astype(F32)
    emit(n.s_ow, n.o_ow, total)
    for p in seq_peers:
        arrive(rgi2.at[p], plan.gi_s, p)
    for m in range(G):
        total = rgi2[m].astype(F32)
        for g in range(1, E):
            total = total + rgi2[g * G + m].astype(F32)
        for rr in range(R):
            for j in range(E):
                b = rr * S + j * G + m
                at = (rr * E + j) * UB
                n.s_in[:, b * UB : (b + 1) * UB] = total[:, at : at + UB]
    finals.append(local(n.s_in, n.o_in, 16 + len(finals)))
    for p in seq_peers:
        arrive(GC.at[:, rows_of(p, HP)], plan.gk_s, p)
    emit(n.s_ckv, n.o_ckv, GC[...].astype(F32))
    total = gg2[:, rows_of(s // per, 128)]
    for p in seq_peers:
        arrive(rgg2.at[p], plan.gg_s, p)
        total = total + rgg2[p]
    emit(n.s_gb, n.o_gb, total)
    for p in seq_peers:
        arrive(GQ.at[:, :, rows_of(p, HP)], plan.gq_s, p)
    emit(n.s_qkv, n.o_qkv, GQ[...].astype(F32))
    drain(*list(pending))
    for cp in finals:
        cp.wait()


def copy_kernel(count, *refs):
    stages, into, out_of = refs[2 * count : 3 * count], refs[3 * count], refs[3 * count + 1]
    loads = [pltpu.make_async_copy(refs[i], stages[i], into.at[i]) for i in range(count)]
    stores = [
        pltpu.make_async_copy(stages[i], refs[count + i], out_of.at[i]) for i in range(count)
    ]
    for cp in loads:
        cp.start()
    for load, store in zip(loads, stores):
        load.wait()
        store.start()
    for cp in stores:
        cp.wait()


def settle(arrays):
    anywhere = pl.BlockSpec(memory_space=pl.ANY)
    return pl.pallas_call(
        functools.partial(copy_kernel, len(arrays)),
        out_shape=[jax.ShapeDtypeStruct(a.shape, a.dtype) for a in arrays],
        in_specs=[anywhere] * len(arrays),
        out_specs=[anywhere] * len(arrays),
        scratch_shapes=[pltpu.VMEM(a.shape, a.dtype) for a in arrays]
        + [pltpu.SemaphoreType.DMA((len(arrays),))] * 2,
    )(*arrays)


def fused_shards(
    hidden_in, clip_lengths, text_lengths, text_states, norm_gain, norm_bias, self_qkv,
    self_out, cross_query, cross_kv, cross_out, ffn_in, ffn_out, out_grad,
):
    R, S = lax.axis_size("rows"), lax.axis_size("seq")
    TB, D = hidden_in.shape[1:]
    TW = text_states.shape[2]
    T, HP, DB = TB * S, D // S, D // (R * S)
    FF = ffn_in.shape[1]
    G = GROUP
    E, U, UB, NT, NZ = S // G, FF // G, FF // (R * S), G * TB, S // 2
    GZ = G // 2
    KB = 2 * cross_kv.shape[1]
    index = lax.axis_index("rows") * S + lax.axis_index("seq")
    per = 128 // DB
    both = jnp.concatenate([norm_gain, norm_bias], axis=0)
    both = jnp.pad(both, ((0, 10), (0, 0)))
    spot = jnp.arange(128, dtype=jnp.int32)[None, :] // DB
    gb = jnp.where(spot == index % per, jnp.tile(both, (1, per)), jnp.zeros((), both.dtype))
    ins = dict(
        cl=clip_lengths, tl=text_lengths, x=hidden_in.reshape(TB, D), og=out_grad.reshape(TB, D),
        text=text_states.reshape(T, TW), gb=gb, wqkv=self_qkv, wo=self_out, wcq=cross_query,
        wco=cross_out, wckv=cross_kv.reshape(KB, D), win=ffn_in, wout=ffn_out,
    )
    outs = dict(
        o_out=((TB, D), BF), o_ig=((TB, D), F32), o_tg=((TB, TW), F32), o_gb=((8, 128), F32),
        o_qkv=(self_qkv.shape, F32), o_so=(self_out.shape, F32), o_cq=(cross_query.shape, F32),
        o_ckv=((KB, D), F32), o_co=(cross_out.shape, F32), o_in=(ffn_in.shape, F32),
        o_ow=(ffn_out.shape, F32),
    )
    plan, count = semaphore_plan(GZ)
    hp = (T, HP)
    pair = (2, T, HP)
    scratch = dict(
        textv=((T, TW), BF),
        gbt=((R, S, 16, 128), BF), gbf=((16, D), F32), Wq3=((3, D, HP), BF), Wq=((D, 3 * HP), BF),
        Wkv3=((R * S * KB, HP), BF), Wkv=((TW, 2 * HP), BF),
        Wm0=((R * NZ, 2, DB, D), BF), Wm1=((R * NZ, 2, DB, D), BF), Wm2=((R * NZ, 2, DB, D), BF),
        Win=((D, U), BF), Wout=((U, D), BF), winp=((DB, FF), BF),
        XH=((3, TB, D), F32), RS=((3, TB, 1), F32), H=((TB, D), F32), GR=((TB, D), F32),
        n1f=((T, D), BF), n3f=((NT, D), BF), ogf=((NT, D), BF), n2=((TB, D), BF),
        oh=(hp, BF), kbs=(hp, BF), kbc=(hp, BF),
        Q=(hp, BF), K=(hp, BF), V=(hp, BF), CK=(hp, BF), CV=(hp, BF), CQ=(hp, BF),
        KA=(pair, BF), QB=(pair, BF),
        CKA=(pair, BF), CVA=(pair, BF), CQB=(pair, BF), CKT=((HP, T), BF),
        AF=(hp, F32), CF=(hp, F32), out=(hp, BF), DC=(hp, BF), DA=(hp, BF),
        ao=((TB, D), BF), wide=((TB, D), BF), co=((TB, D), BF), dqo=((TB, D), BF),
        DCK=(hp, F32), DCV=(hp, F32), DKV=((T, 2 * HP), BF),
        DQT=((HP, T), F32), DQKV=((T, 3 * HP), BF),
        AD=((2 * NT, U), BF),
        ps0=((max(T, 2 * NT), D), BF),
        rbE=((GZ, TB, D), BF), rzE=((GZ - 1, TB, D), BF), rbO=((GZ, TB, D), BF), rzO=((GZ - 1, TB, D), BF),
        rbT=((NZ, TB, TW), BF), rzT=((NZ, TB, TW), BF), rb0=((NZ, TB, D), BF), rz0=((NZ, TB, D), BF),
        rgo=((6, E * UB // 2, D), BF), rgo2=((E, UB, D), BF), rgi=((6, S * DB // 2, U), BF), rgi2=((S, DB, U), BF),
        rgk=((6, S * KB // 2, HP), BF), GC=((KB, D), BF), rgq=((6, 3, S * DB // 2, HP), BF), GQ=((3, DB, D), BF),
        gg=((8, D), F32), rgg=((R - 1, 8, D // R), F32), gg2=((8, D // R), F32), rgg2=((S, 8, 128), F32),
        rmc=((3, R * NZ, DB, D), BF), rmr=((3, 6, NZ // 2, DB, D), BF), rmz=((3, NZ, DB, D), BF),
    )
    for name, spec in outs.items():
        scratch[name.replace("o_", "s_")] = spec
    names = list(ins) + list(outs) + list(scratch) + ["ss", "rs", "ls"]
    anywhere = pl.BlockSpec(memory_space=pl.ANY)
    smem = pl.BlockSpec(memory_space=pltpu.SMEM)
    got = pl.pallas_call(
        functools.partial(layer_kernel, plan, names),
        out_shape=[jax.ShapeDtypeStruct(*v) for v in outs.values()],
        in_specs=[smem, smem] + [anywhere] * (len(ins) - 2),
        out_specs=[anywhere] * len(outs),
        scratch_shapes=[pltpu.VMEM(*v) for v in scratch.values()]
        + [pltpu.SemaphoreType.DMA((k,)) for k in (count, count, 32)],
        compiler_params=pltpu.CompilerParams(
            collective_id=0, has_side_effects=True, vmem_limit_bytes=63 << 20
        ),
    )(*ins.values())
    got = list(got)
    got = list(settle(got[:3] + got[4:])) + [got[3]]
    o = types.SimpleNamespace(**dict(zip([k for k in outs if k != "o_gb"] + ["o_gb"], got)))
    mine = lax.dynamic_slice(o.o_gb, (0, (index % per) * DB), (8, DB))
    return (
        o.o_out.reshape(hidden_in.shape), o.o_ig.reshape(hidden_in.shape),
        o.o_tg.reshape(1, TB, TW), mine[:3], mine[3:6], o.o_qkv, o.o_so, o.o_cq,
        o.o_ckv.reshape(cross_kv.shape), o.o_co, o.o_in, o.o_ow,
    )


def fits(mesh):
    return dict(mesh.shape) == {"rows": 4, "seq": 8}


def solution(mesh):
    placed = (
        P("rows", "seq", None),
        P("rows", None),
        P("rows", None),
        P("rows", None, None),
        P(None, ("rows", "seq")),
        P(None, ("rows", "seq")),
        P(None, ("rows", "seq"), None),
        P(("rows", "seq"), None),
        P(("rows", "seq"), None),
        P(None, ("rows", "seq"), None),
        P(("rows", "seq"), None),
        P(("rows", "seq"), None),
        P(("rows", "seq"), None),
        P("rows", "seq", None),
    )
    return jax.shard_map(
        fused_shards if fits(mesh) else shards,
        mesh=mesh,
        in_specs=placed,
        out_specs=(
            P("rows", "seq", None),
            P("rows", "seq", None),
            P("rows", "seq", None),
            P(None, ("rows", "seq")),
            P(None, ("rows", "seq")),
            P(None, ("rows", "seq"), None),
            P(("rows", "seq"), None),
            P(("rows", "seq"), None),
            P(None, ("rows", "seq"), None),
            P(("rows", "seq"), None),
            P(("rows", "seq"), None),
            P(("rows", "seq"), None),
        ),
        check_vma=False,
    )
```

```python
import functools
import types

import jax
import jax.numpy as jnp
from jax import lax
from jax.experimental import pallas as pl
from jax.experimental.pallas import tpu as pltpu
from jax.sharding import PartitionSpec as P

HD = 64


epsilon = 1e-05
masked_score = -1e30
group_heads = 4
highest = lax.Precision.HIGHEST


def layer_norm(values, gains, biases):
    average = jnp.mean(values, axis=-1, keepdims=True)
    centred = values - average
    variance = jnp.mean(centred * centred, axis=-1, keepdims=True)
    return centred * lax.rsqrt(variance + epsilon) * gains + biases


def gelu_exact(values):
    return jax.nn.gelu(values, approximate=False)


def project(left, weight):
    return jnp.einsum("rtd,de->rte", left, weight, preferred_element_type=jnp.float32)


def weight_term(left, right):
    return jnp.einsum("rtd,rte->de", left, right, preferred_element_type=jnp.float32)


def back_project(gradient, weight):
    return jnp.einsum("rte,de->rtd", gradient, weight, preferred_element_type=jnp.float32)


def exact_weight_term(left, right):
    return jnp.einsum(
        "rtd,rte->de", left, right, precision=highest, preferred_element_type=jnp.float32
    )


def exact_back_project(gradient, weight):
    return jnp.einsum(
        "rte,de->rtd", gradient, weight, precision=highest, preferred_element_type=jnp.float32
    )


def split_heads(values):
    return values.reshape(values.shape[0], values.shape[1], values.shape[2] // HD, HD)


def clip_of(positions, clip_ends):
    return jnp.sum((positions[None, :, None] >= clip_ends[:, None, :]).astype(jnp.int32), axis=2)


def pair_mask(query_pos, query_clip, key_pos, key_clip):
    causal = query_pos[None, :, None] >= key_pos[None, None, :]
    return (causal & (query_clip[:, :, None] == key_clip[:, None, :]))[:, None]


def blocks_of(arrived, frame_span):
    block_count = arrived.shape[1] // frame_span
    shaped = arrived.reshape((arrived.shape[0], block_count, frame_span) + arrived.shape[2:])
    return jnp.moveaxis(shaped, 1, 0)


def block_fold(visit_block, frame_span, carried, arrived):
    block_count = arrived.shape[1] // frame_span
    starts = frame_span * jnp.arange(block_count, dtype=jnp.int32)

    def scan_step(state, block_pair):
        return (visit_block(state, block_pair[0], block_pair[1]), None)

    carried, unused = lax.scan(scan_step, carried, (blocks_of(arrived, frame_span), starts))
    return carried


def head_dot(gradient, output):
    summed = jnp.sum(split_heads(gradient).astype(jnp.float32) * split_heads(output), axis=3)
    return jnp.swapaxes(summed, 1, 2)


def text_project(texts, w_text):
    return jnp.concatenate([project(texts, w_text[0]), project(texts, w_text[1])], axis=2).astype(
        jnp.bfloat16
    )


def self_forward(queries, key_value, clip_ends, clip_ids, frames):
    row_count, frame_span, model_width = queries.shape
    head_count = model_width // HD
    score_scale = HD ** (-0.5)
    query_heads = split_heads(queries)
    last_frame = frames[frame_span - 1]

    def visit_block(state, key_block, first_key):
        key_pos = first_key + jnp.arange(frame_span, dtype=jnp.int32)

        def accumulate(carried):
            running_max, running_sum, output_sum = carried
            key_heads = split_heads(key_block[:, :, :model_width])
            value_heads = split_heads(key_block[:, :, model_width:])
            allowed = pair_mask(frames, clip_ids, key_pos, clip_of(key_pos, clip_ends))
            scores = (
                jnp.einsum(
                    "rqhd,rkhd->rhqk", query_heads, key_heads, preferred_element_type=jnp.float32
                )
                * score_scale
            )
            scores = jnp.where(allowed, scores, masked_score)
            new_max = jnp.maximum(running_max, jnp.max(scores, axis=3))
            weights = jnp.where(allowed, jnp.exp(scores - new_max[..., None]), 0.0)
            shrink = jnp.exp(running_max - new_max)
            running_sum = running_sum * shrink + jnp.sum(weights, axis=3)
            output_sum = output_sum * shrink[..., None] + jnp.einsum(
                "rhqk,rkhd->rhqd",
                weights.astype(jnp.bfloat16),
                value_heads,
                preferred_element_type=jnp.float32,
            )
            return (new_max, running_sum, output_sum)

        return lax.cond(first_key > last_frame, lambda carried: carried, accumulate, state)

    initial = (
        jnp.full((row_count, head_count, frame_span), masked_score, jnp.float32),
        jnp.zeros((row_count, head_count, frame_span), jnp.float32),
        jnp.zeros((row_count, head_count, frame_span, HD), jnp.float32),
    )
    running_max, running_sum, output_sum = block_fold(
        visit_block, frame_span, initial, lax.all_gather(key_value, "seq", axis=1, tiled=True)
    )
    attended = output_sum / running_sum[..., None]
    return (
        jnp.swapaxes(attended, 1, 2).reshape(row_count, frame_span, model_width),
        running_max + jnp.log(running_sum),
    )


def self_query_grad(queries, key_value, clip_ends, clip_ids, frames, log_norm, delta_sum, d_attn):
    row_count, frame_span, model_width = queries.shape
    head_count = model_width // HD
    score_scale = HD ** (-0.5)
    query_heads = split_heads(queries)
    grad_heads = split_heads(d_attn)
    last_frame = frames[frame_span - 1]

    def visit_block(state, key_block, first_key):
        key_pos = first_key + jnp.arange(frame_span, dtype=jnp.int32)

        def accumulate(carried):
            key_heads = split_heads(key_block[:, :, :model_width])
            value_heads = split_heads(key_block[:, :, model_width:])
            allowed = pair_mask(frames, clip_ids, key_pos, clip_of(key_pos, clip_ends))
            scores = (
                jnp.einsum(
                    "rqhd,rkhd->rhqk", query_heads, key_heads, preferred_element_type=jnp.float32
                )
                * score_scale
            )
            probability = jnp.where(allowed, jnp.exp(scores - log_norm[..., None]), 0.0)
            d_prob = jnp.einsum(
                "rqhd,rkhd->rhqk", grad_heads, value_heads, preferred_element_type=jnp.float32
            )
            d_score = (probability * (d_prob - delta_sum[..., None])).astype(jnp.bfloat16)
            return carried + jnp.einsum(
                "rhqk,rkhd->rhqd", d_score, key_heads, preferred_element_type=jnp.float32
            )

        return lax.cond(first_key > last_frame, lambda carried: carried, accumulate, state)

    initial = jnp.zeros((row_count, head_count, frame_span, HD), jnp.float32)
    d_query = block_fold(
        visit_block, frame_span, initial, lax.all_gather(key_value, "seq", axis=1, tiled=True)
    )
    d_query = jnp.swapaxes(d_query, 1, 2).reshape(row_count, frame_span, model_width) * score_scale
    return d_query.astype(jnp.bfloat16)


def self_key_grad(query_grad, key_value, clip_ends, clip_ids, frames, gathered_stats):
    row_count, frame_span, double_width = key_value.shape
    model_width = double_width // 2
    head_count = model_width // HD
    score_scale = HD ** (-0.5)
    key_heads = split_heads(key_value[:, :, :model_width])
    value_heads = split_heads(key_value[:, :, model_width:])
    all_norm, all_delta = gathered_stats
    first_own = frames[0]

    def visit_block(state, query_block, first_query):
        query_pos = first_query + jnp.arange(frame_span, dtype=jnp.int32)

        def accumulate(carried):
            d_key, d_value = carried
            query_heads = split_heads(query_block[:, :, :model_width])
            grad_heads = split_heads(query_block[:, :, model_width:])
            log_norm = jnp.swapaxes(
                lax.dynamic_slice_in_dim(all_norm, first_query, frame_span, 1), 1, 2
            )
            delta_sum = jnp.swapaxes(
                lax.dynamic_slice_in_dim(all_delta, first_query, frame_span, 1), 1, 2
            )
            allowed = pair_mask(query_pos, clip_of(query_pos, clip_ends), frames, clip_ids)
            scores = (
                jnp.einsum(
                    "rqhd,rkhd->rhqk", query_heads, key_heads, preferred_element_type=jnp.float32
                )
                * score_scale
            )
            probability = jnp.where(allowed, jnp.exp(scores - log_norm[..., None]), 0.0)
            d_value = d_value + jnp.einsum(
                "rhqk,rqhd->rhkd",
                probability.astype(jnp.bfloat16),
                grad_heads,
                preferred_element_type=jnp.float32,
            )
            d_prob = jnp.einsum(
                "rqhd,rkhd->rhqk", grad_heads, value_heads, preferred_element_type=jnp.float32
            )
            d_score = (probability * (d_prob - delta_sum[..., None])).astype(jnp.bfloat16)
            d_key = d_key + jnp.einsum(
                "rhqk,rqhd->rhkd", d_score, query_heads, preferred_element_type=jnp.float32
            )
            return (d_key, d_value)

        return lax.cond(
            first_query + frame_span - 1 < first_own, lambda carried: carried, accumulate, state
        )

    zeros_heads = jnp.zeros((row_count, head_count, frame_span, HD), jnp.float32)
    d_key, d_value = block_fold(
        visit_block,
        frame_span,
        (zeros_heads, zeros_heads),
        lax.all_gather(query_grad, "seq", axis=1, tiled=True),
    )
    d_key = jnp.swapaxes(d_key, 1, 2).reshape(row_count, frame_span, model_width) * score_scale
    d_value = jnp.swapaxes(d_value, 1, 2).reshape(row_count, frame_span, model_width)
    return (d_key.astype(jnp.bfloat16), d_value.astype(jnp.bfloat16))


def cross_forward(queries, text_kv, readable):
    row_count, frame_span, model_width = queries.shape
    group_width = group_heads * HD
    score_scale = HD ** (-0.5)
    outputs = []
    log_norms = []
    for group_index in range(model_width // group_width):
        lower_edge = group_index * group_width
        query_heads = split_heads(queries[:, :, lower_edge : lower_edge + group_width])
        key_heads = split_heads(text_kv[:, :, lower_edge : lower_edge + group_width])
        value_heads = split_heads(
            text_kv[:, :, model_width + lower_edge : model_width + lower_edge + group_width]
        )
        scores = (
            jnp.einsum(
                "rqhd,rkhd->rhqk", query_heads, key_heads, preferred_element_type=jnp.float32
            )
            * score_scale
        )
        scores = jnp.where(readable, scores, masked_score)
        largest = jnp.max(scores, axis=3)
        weights = jnp.where(readable, jnp.exp(scores - largest[..., None]), 0.0)
        totals = jnp.sum(weights, axis=3)
        probability = (weights / totals[..., None]).astype(jnp.bfloat16)
        attended = jnp.einsum(
            "rhqk,rkhd->rqhd", probability, value_heads, preferred_element_type=jnp.float32
        )
        outputs.append(attended.reshape(row_count, frame_span, group_width))
        log_norms.append(largest + jnp.log(totals))
    return (jnp.concatenate(outputs, axis=2), jnp.concatenate(log_norms, axis=1))


def cross_backward(queries, text_kv, readable, log_norm, d_cross, delta_sum):
    row_count, frame_span, model_width = queries.shape
    slot_count = text_kv.shape[1]
    group_width = group_heads * HD
    score_scale = HD ** (-0.5)
    d_queries = []
    d_keys = []
    d_values = []
    for group_index in range(model_width // group_width):
        lower_edge = group_index * group_width
        head_edge = group_index * group_heads
        query_heads = split_heads(queries[:, :, lower_edge : lower_edge + group_width])
        grad_heads = split_heads(d_cross[:, :, lower_edge : lower_edge + group_width])
        key_heads = split_heads(text_kv[:, :, lower_edge : lower_edge + group_width])
        value_heads = split_heads(
            text_kv[:, :, model_width + lower_edge : model_width + lower_edge + group_width]
        )
        group_norm = log_norm[:, head_edge : head_edge + group_heads]
        group_delta = delta_sum[:, head_edge : head_edge + group_heads]
        scores = (
            jnp.einsum(
                "rqhd,rkhd->rhqk", query_heads, key_heads, preferred_element_type=jnp.float32
            )
            * score_scale
        )
        probability = jnp.where(readable, jnp.exp(scores - group_norm[..., None]), 0.0)
        d_value = jnp.einsum(
            "rhqk,rqhd->rkhd",
            probability.astype(jnp.bfloat16),
            grad_heads,
            preferred_element_type=jnp.float32,
        )
        d_values.append(d_value.reshape(row_count, slot_count, group_width))
        d_prob = jnp.einsum(
            "rqhd,rkhd->rhqk", grad_heads, value_heads, preferred_element_type=jnp.float32
        )
        d_score = (probability * (d_prob - group_delta[..., None])).astype(jnp.bfloat16)
        d_query = jnp.einsum(
            "rhqk,rkhd->rqhd", d_score, key_heads, preferred_element_type=jnp.float32
        )
        d_queries.append(d_query.reshape(row_count, frame_span, group_width) * score_scale)
        d_key = jnp.einsum(
            "rhqk,rqhd->rkhd", d_score, query_heads, preferred_element_type=jnp.float32
        )
        d_keys.append(d_key.reshape(row_count, slot_count, group_width) * score_scale)
    return (jnp.concatenate(d_queries, axis=2), jnp.concatenate(d_keys + d_values, axis=2))


def shards(
    hidden_in,
    clip_lengths,
    text_lengths,
    text_states,
    norm_gain,
    norm_bias,
    self_qkv,
    self_out,
    cross_query,
    cross_kv,
    cross_out,
    ffn_in,
    ffn_out,
    out_grad,
):
    gathered = (
        lax.all_gather(norm_gain, ("rows", "seq"), axis=1, tiled=True),
        lax.all_gather(norm_bias, ("rows", "seq"), axis=1, tiled=True),
        lax.all_gather(self_qkv, ("rows", "seq"), axis=1, tiled=True),
        lax.all_gather(self_out, ("rows", "seq"), axis=0, tiled=True),
        lax.all_gather(cross_query, ("rows", "seq"), axis=0, tiled=True),
        lax.all_gather(cross_kv, ("rows", "seq"), axis=1, tiled=True),
        lax.all_gather(cross_out, ("rows", "seq"), axis=0, tiled=True),
        lax.all_gather(ffn_in, ("rows", "seq"), axis=0, tiled=True),
        lax.all_gather(ffn_out, ("rows", "seq"), axis=0, tiled=True),
    )
    gains_all, biases_all, w_qkv, w_self, w_query, w_text, w_cross, w_up, w_down = gathered
    gains = gains_all.astype(jnp.float32)
    biases = biases_all.astype(jnp.float32)
    row_count, frame_span, model_width = hidden_in.shape
    seq_index = lax.axis_index("seq")
    frames = seq_index * frame_span + jnp.arange(frame_span, dtype=jnp.int32)
    clip_ends = jnp.cumsum(clip_lengths, axis=1)
    clip_ids = clip_of(frames, clip_ends)
    text_ends = jnp.cumsum(text_lengths, axis=1)
    text_starts = text_ends - text_lengths
    chosen = (
        clip_ids[:, :, None] == jnp.arange(clip_lengths.shape[1], dtype=jnp.int32)[None, None, :]
    )
    slot_low = jnp.sum(jnp.where(chosen, text_starts[:, None, :], 0), axis=2)
    slot_high = jnp.sum(jnp.where(chosen, text_ends[:, None, :], 0), axis=2)
    slot_index = jnp.arange(text_states.shape[1], dtype=jnp.int32)
    readable = (
        (slot_index[None, None, :] >= slot_low[:, :, None])
        & (slot_index[None, None, :] < slot_high[:, :, None])
    )[:, None]
    slot_share = text_states.shape[1] // lax.axis_size("seq")
    own_text = lax.dynamic_slice_in_dim(text_states, seq_index * slot_share, slot_share, 1)
    resid = hidden_in.astype(jnp.float32)
    normed_full, pull_first = jax.vjp(layer_norm, resid, gains[0], biases[0])
    normed = normed_full.astype(jnp.bfloat16)
    queries = project(normed, w_qkv[0]).astype(jnp.bfloat16)
    keys_low = project(normed, w_qkv[1]).astype(jnp.bfloat16)
    values_low = project(normed, w_qkv[2]).astype(jnp.bfloat16)
    key_value = jnp.concatenate([keys_low, values_low], axis=2)
    self_full, self_norm = self_forward(queries, key_value, clip_ends, clip_ids, frames)
    attended = self_full.astype(jnp.bfloat16)
    after_self = resid + project(attended, w_self)
    normed_full, pull_second = jax.vjp(layer_norm, after_self, gains[1], biases[1])
    normed_two = normed_full.astype(jnp.bfloat16)
    cross_queries = project(normed_two, w_query).astype(jnp.bfloat16)
    text_kv = lax.all_gather(text_project(own_text, w_text), "seq", axis=1, tiled=True)
    cross_full, cross_norm = cross_forward(cross_queries, text_kv, readable)
    crossed = cross_full.astype(jnp.bfloat16)
    after_cross = after_self + project(crossed, w_cross)
    normed_full, pull_third = jax.vjp(layer_norm, after_cross, gains[2], biases[2])
    normed_three = normed_full.astype(jnp.bfloat16)
    hidden_up = project(normed_three, w_up)
    activated_full, pull_gelu = jax.vjp(gelu_exact, hidden_up)
    activated = activated_full.astype(jnp.bfloat16)
    block_out = (after_cross + project(activated, w_down)).astype(jnp.bfloat16)
    gradient = out_grad.astype(jnp.float32)
    g_down = weight_term(activated, out_grad)
    d_up = pull_gelu(back_project(out_grad, w_down))[0].astype(jnp.bfloat16)
    g_up = weight_term(normed_three, d_up)
    d_third, g_gain_three, g_bias_three = pull_third(back_project(d_up, w_up))
    gradient = gradient + d_third
    grad_low = gradient.astype(jnp.bfloat16)
    g_cross = weight_term(crossed, grad_low)
    d_cross = back_project(grad_low, w_cross).astype(jnp.bfloat16)
    cross_delta = head_dot(d_cross, cross_full)
    d_cross_query, d_text_kv = cross_backward(
        cross_queries, text_kv, readable, cross_norm, d_cross, cross_delta
    )
    key_weight = w_text[0].astype(jnp.float32)
    value_weight = w_text[1].astype(jnp.float32)
    own_grad = lax.psum_scatter(
        d_text_kv.astype(jnp.bfloat16), "seq", scatter_dimension=1, tiled=True
    ).astype(jnp.float32)
    grad_text_key = own_grad[:, :, :model_width]
    grad_text_value = own_grad[:, :, model_width:]
    own_exact = own_text.astype(jnp.float32)
    g_text = jnp.stack(
        [exact_weight_term(own_exact, grad_text_key), exact_weight_term(own_exact, grad_text_value)]
    )
    text_grad = exact_back_project(grad_text_key, key_weight) + exact_back_project(
        grad_text_value, value_weight
    )
    d_cross_query = d_cross_query.astype(jnp.bfloat16)
    g_query = weight_term(normed_two, d_cross_query)
    d_second, g_gain_two, g_bias_two = pull_second(back_project(d_cross_query, w_query))
    gradient = gradient + d_second
    grad_low = gradient.astype(jnp.bfloat16)
    g_self = weight_term(attended, grad_low)
    d_attn = back_project(grad_low, w_self).astype(jnp.bfloat16)
    self_delta = head_dot(d_attn, self_full)
    d_query = self_query_grad(
        queries, key_value, clip_ends, clip_ids, frames, self_norm, self_delta, d_attn
    )
    gathered_stats = (
        lax.all_gather(jnp.swapaxes(self_norm, 1, 2), "seq", axis=1, tiled=True),
        lax.all_gather(jnp.swapaxes(self_delta, 1, 2), "seq", axis=1, tiled=True),
    )
    query_grad = jnp.concatenate([queries, d_attn], axis=2)
    d_key, d_value = self_key_grad(
        query_grad, key_value, clip_ends, clip_ids, frames, gathered_stats
    )
    g_qkv = jnp.stack(
        [weight_term(normed, d_query), weight_term(normed, d_key), weight_term(normed, d_value)]
    )
    d_normed = (
        back_project(d_query, w_qkv[0])
        + back_project(d_key, w_qkv[1])
        + back_project(d_value, w_qkv[2])
    )
    d_first, g_gain_one, g_bias_one = pull_first(d_normed)
    input_grad = gradient + d_first
    g_gain = jnp.stack([g_gain_one, g_gain_two, g_gain_three])
    g_bias = jnp.stack([g_bias_one, g_bias_two, g_bias_three])
    reduced = (
        lax.psum_scatter(g_gain, ("rows", "seq"), scatter_dimension=1, tiled=True),
        lax.psum_scatter(g_bias, ("rows", "seq"), scatter_dimension=1, tiled=True),
        lax.psum_scatter(g_qkv, ("rows", "seq"), scatter_dimension=1, tiled=True),
        lax.psum_scatter(g_self, ("rows", "seq"), scatter_dimension=0, tiled=True),
        lax.psum_scatter(g_query, ("rows", "seq"), scatter_dimension=0, tiled=True),
        lax.psum_scatter(g_text, ("rows", "seq"), scatter_dimension=1, tiled=True),
        lax.psum_scatter(g_cross, ("rows", "seq"), scatter_dimension=0, tiled=True),
        lax.psum_scatter(g_up, ("rows", "seq"), scatter_dimension=0, tiled=True),
        lax.psum_scatter(g_down, ("rows", "seq"), scatter_dimension=0, tiled=True),
    )
    return (
        block_out,
        input_grad,
        text_grad,
        reduced[0],
        reduced[1],
        reduced[2],
        reduced[3],
        reduced[4],
        reduced[5],
        reduced[6],
        reduced[7],
        reduced[8],
    )


MESH = pl.DeviceIdType.MESH
BF = jnp.bfloat16
F32 = jnp.float32
GROUP = 4
NEG = -1e30


def dot(a, b):
    return lax.dot_general(a, b, (((1,), (0,)), ((), ())), preferred_element_type=F32)


def dot_nt(a, b):
    return lax.dot_general(a, b, (((1,), (1,)), ((), ())), preferred_element_type=F32)


def dot_tn(a, b):
    return lax.dot_general(a, b, (((0,), (0,)), ((), ())), preferred_element_type=F32)


def mult(index, step):
    return pl.multiple_of(index * step, step)


def rows_of(index, step):
    return pl.ds(mult(index, step), step)


def each(count, step, body):
    def turn(i, carry):
        body(pl.ds(pl.multiple_of(i * step, step), step))
        return carry

    lax.fori_loop(0, count // step, turn, 0)


def three_parts(value):
    first = value.astype(BF).astype(F32)
    rest = value - first
    second = rest.astype(BF).astype(F32)
    return first, second, (rest - second).astype(BF).astype(F32)


def normalise(values):
    average = jnp.mean(values, axis=-1, keepdims=True)
    centred = values - average
    rstd = lax.rsqrt(jnp.mean(centred * centred, axis=-1, keepdims=True) + epsilon)
    return centred * rstd, rstd


def semaphore_plan(group_chips):
    sizes = dict(
        gb_s=8, gb_r=4, q_s=8, q_r=4, kv_s=8, kv_r=4, in_s=8, in_r=4, ow_g=8, ow_r=4, ow_x=4 * 8,
        n1=48, og=16, n3=16, a_at=8, a_cq=8, a_cr=8, b_cr=8, b_cq=8, b_at=8,
        e_c=4, e_z=4, o_c=4, o_z=4, t_c=4, t_z=8, s_c=4, s_z=8,
        gq_r=8, gq_s=8, gi_r=8, gi_s=8, go_r=8, go_g=8, gk_r=8, gk_s=8, gg_r=4, gg_s=8,
        m_z=12, m_r=12, m_c=6, h_c=6, h_r=24, h_z=24,
    )
    base, plan = 0, {}
    for name, size in sizes.items():
        plan[name] = base
        base += size
    return types.SimpleNamespace(**plan), base


def layer_kernel(plan, names, *refs):
    n = types.SimpleNamespace(**dict(zip(names, refs)))
    R, S, NZ, D = 4, 8, 4, n.x.shape[1]
    TB = n.x.shape[0]
    CH = 2 * TB
    T = S * TB
    HP = D // S
    FF = n.win.shape[1]
    G = GROUP
    GZ = G // 2
    E = S // G
    U = FF // G
    UB = FF // (R * S)
    DB = D // (R * S)
    TW = n.text.shape[1]
    KB = n.wckv.shape[0]
    r, s = lax.axis_index("rows"), lax.axis_index("seq")
    z, c = s // 2, s % 2
    sib = s + 1 - 2 * c
    ffn_z0 = (z // GZ) * GZ
    grp, mem = s // G, s % G
    ss, rs = n.ss, n.rs
    pending = {}
    gbt, Wq3, Wkv3, Win, Wout, winp, ogf = n.gbt, n.Wq3, n.Wkv3, n.Win, n.Wout, n.winp, n.ogf
    mats = [n.Wm0, n.Wm1, n.Wm2]

    def push(src, dst, name, to, origin, dev, send_shift=0, when=None):
        cp = pltpu.make_async_remote_copy(
            src_ref=src, dst_ref=dst,
            send_sem=ss.at[name + send_shift + to],
            recv_sem=rs.at[name + origin],
            device_id=dev, device_id_type=MESH,
        )
        pending.setdefault(name, []).append((cp, when))
        if when is None:
            cp.start()
        else:
            pl.when(when)(cp.start)

    def drain(*which):
        for name in which:
            for cp, when in pending.pop(name, []):
                if when is None:
                    cp.wait_send()
                else:
                    pl.when(when)(cp.wait_send)

    def arrive(landing, name, origin, when=None):
        cp = pltpu.make_async_remote_copy(
            src_ref=landing, dst_ref=landing, send_sem=ss.at[name],
            recv_sem=rs.at[name + origin], device_id=(r, sib), device_id_type=MESH,
        )
        if when is None:
            cp.wait_recv()
        else:
            pl.when(when)(cp.wait_recv)

    side = z // 2
    inner, outer = (z + 1) % NZ // 2 == 1, (z + 1) % NZ // 2 == 0
    beside = z + 1 - 2 * (z % 2)
    far_inner, far_outer = 2 - side, 3 - 3 * side
    legs = (((far_inner, None), (beside, outer)), ((far_outer, None), (beside, inner)))

    def spread(leg, send):
        for zl, when in legs[leg]:
            for core in range(2):
                send(2 * zl + core, when)

    across_x, across_y = r + 1 - 2 * (r % 2), (r + 2) % R
    corner = (across_x + 2) % R

    def plane_start(block, name):
        push(block(r), block(r), name, 0, 0, (across_x, s))
        push(block(r), block(r), name, 1, 1, (across_y, s))

    def plane_pass(block, half, name):
        arrive(block(across_x), name, 0)
        push(half(across_x, 0), half(across_x, 0), name, 2, 2, (across_y, s))
        arrive(block(across_y), name, 1)
        push(half(across_y, 1), half(across_y, 1), name, 3, 3, (across_x, s))

    def plane_take(half, name):
        arrive(half(corner, 0), name, 2)
        arrive(half(corner, 1), name, 3)

    def fold_start(half, landed, name):
        push(half(corner, 0), landed.at[1], name, 1, 1, (across_x, s))
        push(half(corner, 1), landed.at[3], name, 3, 3, (across_y, s))
        push(half(across_x, 0), landed.at[0], name, 0, 0, (across_x, s))
        push(half(across_y, 1), landed.at[2], name, 2, 2, (across_y, s))

    def fold_pass(half, landed, name):
        for k, (near, to) in enumerate(((across_y, across_y), (across_x, across_x))):
            arrive(landed.at[1 + 2 * k], name, 1 + 2 * k)
            mine = half(near, k)
            mine[...] = (mine[...].astype(F32) + landed[1 + 2 * k].astype(F32)).astype(BF)
            push(mine, landed.at[4 + k], name, 4 + k, 4 + k, (to, s))

    def fold_take(half, landed, name):
        for k in range(2):
            arrive(landed.at[2 * k], name, 2 * k)
            arrive(landed.at[4 + k], name, 4 + k)
            mine = half(r, k)
            total = mine[...].astype(F32) + landed[2 * k].astype(F32) + landed[4 + k].astype(F32)
            mine[...] = total.astype(BF)

    def rows_view(ref, step):
        def block(p):
            return ref.at[rows_of(p, step), :]

        def half(p, k):
            return ref.at[rows_of(2 * p + k, step // 2), :]

        return block, half

    def mid_view(ref, step):
        def block(p):
            return ref.at[:, rows_of(p, step), :]

        def half(p, k):
            return ref.at[:, rows_of(2 * p + k, step // 2), :]

        return block, half

    def mat_view(i):
        def block(p):
            return mats[i].at[pl.ds(p * NZ, NZ), c]

        def half(p, k):
            return mats[i].at[pl.ds(p * NZ + 2 * k, 2), c]

        return block, half

    def out_view(j):
        def block(p):
            return Wout.at[rows_of(p * E + (grp + j) % E, UB), :]

        def half(p, k):
            return Wout.at[rows_of(2 * (p * E + (grp + j) % E) + k, UB // 2), :]

        return block, half

    seq_peers = [(s + k) % S for k in range(1, S)]
    row_peers = [(r + k) % R for k in range(1, R)]
    z_peers = [(z + k) % NZ for k in range(1, NZ)]

    barrier = pltpu.get_barrier_semaphore()
    for p in seq_peers:
        pl.semaphore_signal(barrier, inc=1, device_id=(r, p), device_id_type=MESH)
    for p in row_peers:
        pl.semaphore_signal(barrier, inc=1, device_id=(p, s), device_id_type=MESH)
    finals = []

    def local(src, dst, i):
        cp = pltpu.make_async_copy(src, dst, n.ls.at[i])
        cp.start()
        return cp

    def emit(stage, out, value):
        stage[...] = value
        finals.append(local(stage, out, 16 + len(finals)))

    own_mats = [n.wo, n.wcq, n.wco]
    own_rows = rows_of(r * S + s, DB)
    kv_rows = rows_of(r * S + s, KB)
    out_rows = rows_of(r * E + grp, UB)
    xs, own_tokens = n.ps0, rows_of(s, TB)
    got_x = local(n.x, xs.at[own_tokens, :], 0)
    got_gb = local(n.gb, gbt.at[r, s], 1)
    got_q = local(n.wqkv.at[:, :, rows_of(s, HP)], Wq3.at[:, own_rows, :], 2)
    got_kv = local(n.wckv.at[:, rows_of(s, HP)], Wkv3.at[kv_rows, :], 3)
    got_mats = [local(own_mats[i], mats[i].at[r * NZ + z, c], 4 + i) for i in range(3)]
    for m in range(G):
        for rr in range(R):
            for j in range(E):
                b = rr * S + j * G + m
                at = m * U + (rr * E + j) * UB
                local(n.win.at[:, b * UB : (b + 1) * UB], winp.at[:, at : at + UB], 7)
    got_ow = local(n.wout, Wout.at[out_rows, :], 8)
    got_og = local(n.og, ogf.at[rows_of(mem, TB), :], 9)
    got_text = local(n.text, n.textv, 10)

    lane = lax.broadcasted_iota(jnp.int32, (T, HP), 1)
    row = lax.broadcasted_iota(jnp.int32, (T, HP), 0)
    slot = lane % HD
    cl, tl = n.cl, n.tl

    def inside(lengths):
        low, found = jnp.int32(0), jnp.zeros((T, HP), jnp.bool_)
        for k in range(4):
            high = low + lengths[0, k]
            found = found | ((slot == k) & (row >= low) & (row < high))
            low = high
        return found

    ones_tail = jnp.where((slot >= 4) & (slot < 7), 1.0, 0.0)

    def mask_block():
        in_clip = inside(cl)
        n.oh[...] = jnp.where(in_clip, 1.0, 0.0).astype(BF)
        n.kbs[...] = jnp.where(slot < 4, jnp.where(in_clip, 0.0, NEG), ones_tail).astype(BF)
        n.kbc[...] = jnp.where(slot < 4, jnp.where(inside(tl), 0.0, NEG), ones_tail).astype(BF)

    mask_block()

    pl.semaphore_wait(barrier, S + R - 2)

    q_block, q_half = mid_view(Wq3, S * DB)
    kv_block, kv_half = rows_view(Wkv3, S * KB)
    in_block, in_half = rows_view(Win, S * DB)
    ow_block, ow_half = out_view(0)

    def mat_z(i, leg):
        for p, when in legs[leg]:
            dst = mats[i].at[r * NZ + z, c]
            push(own_mats[i], dst, plan.m_z + 4 * i, p, z, (r, 2 * p + c), when=when)

    def mat_r(i):
        for p in z_peers:
            arrive(mats[i].at[r * NZ + p, c], plan.m_z + 4 * i, p)
        got_mats[i].wait()
        plane_start(mat_view(i)[0], plan.m_r + 4 * i)

    def mat_p(i):
        plane_pass(*mat_view(i), plan.m_r + 4 * i)

    def mat_c(i):
        plane_take(mat_view(i)[1], plan.m_r + 4 * i)
        block = mats[i].at[:, c]
        push(block, block, plan.m_c + 2 * i, 0, 0, (r, sib))

    def mat_take(i):
        arrive(mats[i].at[:, 1 - c], plan.m_c + 2 * i, 0)

    def mat(i):
        return mats[i][...].reshape(D, D)

    def kv_send(p, when):
        src = n.wckv.at[:, rows_of(p, HP)]
        push(src, Wkv3.at[kv_rows, :], plan.kv_s, p, s, (r, p), when=when)

    def kv_first():
        kv_send(sib, None)
        spread(0, kv_send)

    def kv_plane():
        for p in seq_peers:
            arrive(Wkv3.at[rows_of(r * S + p, KB), :], plan.kv_s, p)
        got_kv.wait()
        plane_start(kv_block, plan.kv_r)

    def kv_pass():
        plane_pass(kv_block, kv_half, plan.kv_r)

    def in_send(p, when):
        src = winp.at[:, rows_of(p % G, U)]
        push(src, Win.at[own_rows, :], plan.in_s, p, s, (r, p), when=when)

    def in_first():
        in_send(sib, None)
        spread(0, in_send)

    def in_plane():
        for p in seq_peers:
            arrive(Win.at[rows_of(r * S + p, DB), :], plan.in_s, p)
        plane_start(in_block, plan.in_r)

    def in_pass():
        plane_pass(in_block, in_half, plan.in_r)

    def ow_send(when):
        for j in range(1, E):
            p = (s + j * G) % S
            push(n.wout, Wout.at[out_rows, :], plan.ow_g, p, s, (r, p), when=when)

    def ow_first():
        push(n.wout, ow_block(r), plan.ow_r, 0, 0, (across_x, s))
        push(n.wout, ow_block(r), plan.ow_r, 1, 1, (across_y, s))

    def ow_pass():
        plane_pass(ow_block, ow_half, plan.ow_r)

    def ow_second():
        for j in range(1, E):
            arrive(out_view(j)[0](r), plan.ow_g, (s + j * G) % S)
            plane_start(out_view(j)[0], plan.ow_x + 4 * j)

    def ow_second_pass():
        for j in range(1, E):
            plane_pass(*out_view(j), plan.ow_x + 4 * j)

    def gather_start(buf, name, z0, nz):
        m = s - 2 * z0
        block = buf.at[rows_of(m, TB), :]
        for k in range(1, nz):
            zl = (z - z0 + k) % nz
            push(block, block, name, 2 * zl + c, m, (r, 2 * (z0 + zl) + c))
        push(block, block, name, sib - 2 * z0, m, (r, sib))

    def og_start():
        got_og.wait()
        gather_start(ogf, plan.og, ffn_z0, GZ)

    for p in seq_peers:
        push(n.gb, gbt.at[r, s], plan.gb_s, p, s, (r, p))
    for p in seq_peers:
        push(n.wqkv.at[:, :, rows_of(p, HP)], Wq3.at[:, own_rows, :], plan.q_s, p, s, (r, p))

    mat_z(1, 1)
    mat_z(1, 0)
    spread(1, kv_send)
    TH = TB // 2
    for q in range(2):
        src, dst = n.x.at[q * TH : (q + 1) * TH, :], xs.at[rows_of(2 * s + q, TH), :]
        for zl in (far_inner, beside):
            push(src, dst, plan.n1 + 24 * q, 2 * zl + c, s, (r, 2 * zl + c))
        push(src, dst, plan.n1 + 24 * q, sib, s, (r, sib))

    for p in seq_peers:
        arrive(gbt.at[r, p], plan.gb_s, p)
    got_gb.wait()
    for p in row_peers:
        push(gbt.at[r], gbt.at[r], plan.gb_r, p, r, (p, s))
    pltpu.make_async_copy(n.win, winp, n.ls.at[7]).wait()
    Win[own_rows, :] = winp[:, rows_of(mem, U)]
    ow_first()
    mat_z(0, 1)
    for p in seq_peers:
        arrive(Wq3.at[:, rows_of(r * S + p, DB), :], plan.q_s, p)
    got_q.wait()
    plane_start(q_block, plan.q_r)
    mat_z(0, 0)

    for p in row_peers:
        arrive(gbt.at[p], plan.gb_r, p)
    per = 128 // DB
    gbf = n.gbf
    for g in range(D // 128):
        total = None
        for k in range(per):
            rr, sx = divmod(g * per + k, S)
            tile = gbt[rr, sx].astype(F32)
            total = tile if total is None else total + tile
        gbf[:, g * 128 : (g + 1) * 128] = total

    def gain(i):
        return gbf[i : i + 1, :]

    def bias(i):
        return gbf[3 + i : 4 + i, :]

    def first_half(shape):
        return lax.broadcasted_iota(jnp.int32, shape, 1) < HD

    def split_pair(value, other):
        front = first_half(value.shape)
        v, o = value.astype(F32), other.astype(F32)
        return jnp.where(front, v, o).astype(BF), jnp.where(front, o, v).astype(BF)

    def gather_pass(buf, name, z0, nz, k):
        zl = (z - z0 + k) % nz
        if k:
            block = buf.at[rows_of(2 * zl + c, TB), :]
            arrive(block, name, 2 * zl + c)
            push(block, block, name, 2 * zl + c, 2 * zl + c, (r, sib), send_shift=8)

    def gather_take(buf, name, z0, nz, k):
        zl = (z - z0 + k) % nz
        arrive(buf.at[rows_of(2 * zl + 1 - c, TB), :], name, 2 * zl + 1 - c)
        return rows_of(zl, CH)

    def chain_pass(zl, q):
        origin, name = 2 * zl + c, plan.n1 + 24 * q
        block = xs.at[rows_of(2 * origin + q, TH), :]
        arrive(block, name, origin)
        push(block, block, name, 16 + origin, origin, (r, 2 * beside + c), when=inner & (zl // 2 != side))
        push(block, block, name, 8 + origin, origin, (r, sib))

    def chain_take(zl):
        origin = 2 * zl + 1 - c
        for q in range(2):
            arrive(xs.at[rows_of(2 * origin + q, TH), :], plan.n1 + 24 * q, origin)
        return rows_of(zl, CH)

    n1f, Wq = n.n1f, n.Wq
    Q, K, V = n.Q, n.K, n.V
    KA = n.KA
    scale = HD ** (-0.5)

    def norm_rows(rows):
        xh = normalise(xs[rows, :].astype(F32))[0]
        n1f[rows, :] = (xh * gain(0) + bias(0)).astype(BF)

    def qkv_chunk(rows):
        def block():
            qkv_block(rows)

        block()

    def qkv_block(rows):
        got = dot(n1f[rows, :], Wq[...])
        Q[rows, :] = (got[:, :HP].astype(BF).astype(F32) * scale).astype(BF)
        K[rows, :] = got[:, HP : 2 * HP].astype(BF)
        V[rows, :] = got[:, 2 * HP :].astype(BF)
        KA[0, rows, :], KA[1, rows, :] = split_pair(K[rows, :], n.kbs[rows, :])

    got_x.wait()
    rows = chain_take(z)
    norm_rows(rows)
    kv_first()
    chain_pass(far_inner, 0)
    chain_pass(far_outer, 0)
    in_first()
    mat_r(1)
    mat_z(2, 0)
    plane_pass(q_block, q_half, plan.q_r)
    chain_pass(far_inner, 1)
    chain_pass(far_outer, 1)
    mat_r(0)
    mat_z(2, 1)
    rows_1 = chain_take(far_inner)
    norm_rows(rows_1)
    og_start()
    rows_2 = chain_take(far_outer)
    norm_rows(rows_2)
    ow_pass()
    kv_plane()
    mat_p(1)
    plane_take(q_half, plan.q_r)
    for i in range(3):
        Wq[:, i * HP : (i + 1) * HP] = Wq3[i]
    qkv_chunk(rows)
    qkv_chunk(rows_1)
    qkv_chunk(rows_2)
    chain_pass(beside, 0)
    chain_pass(beside, 1)
    rows = chain_take(beside)
    norm_rows(rows)
    qkv_chunk(rows)
    spread(1, in_send)
    CK, CV = n.CK, n.CV
    half = KB // 2
    Wkv = n.Wkv

    def text_rows(rows):
        got = dot(n.textv[rows, :], Wkv[...]).astype(BF)
        CK[rows, :] = got[:, :HP]
        CV[rows, :] = got[:, HP:]

    def text_block():
        each(T, CH, text_rows)

    def text_all():
        plane_take(kv_half, plan.kv_r)
        wide = Wkv3[...].astype(F32).reshape(R * S, KB, HP)
        Wkv[:, :HP] = wide[:, :half, :].reshape(TW, HP).astype(BF)
        Wkv[:, HP:] = wide[:, half:, :].reshape(TW, HP).astype(BF)
        got_text.wait()
        text_block()

    AF, QB = n.AF, n.QB
    oh = n.oh
    AB = n.out
    ao = n.ao

    def finish(o0, o1, l0, l1):
        return jnp.where(first_half(o0.shape), o0 / l0, o1 / l1)

    def with_norm(q_aug, head, norm):
        spot = lax.broadcasted_iota(jnp.int32, q_aug.shape, 1)
        base = (1 - head) * HD
        a, b, d = three_parts(-norm)
        w = q_aug.astype(F32)
        w = jnp.where(spot == base + 4, a, w)
        w = jnp.where(spot == base + 5, b, w)
        return jnp.where(spot == base + 6, d, w).astype(BF)

    kpos = lax.broadcasted_iota(jnp.int32, (CH, CH), 1)
    qpos = lax.broadcasted_iota(jnp.int32, (CH, CH), 0)
    def self_rows(i, low, high):
        qa = split_pair(Q[low:high, :], oh[low:high, :])
        outs, sums = [], []
        for h in range(2):
            diag = jnp.where(kpos <= qpos, dot_nt(qa[h], KA[h, low:high, :]), NEG)
            top = jnp.max(diag, axis=1, keepdims=True)
            if i:
                left = dot_nt(qa[h], KA[h, :low, :])
                top = jnp.maximum(top, jnp.max(left, axis=1, keepdims=True))
            diag = jnp.exp(diag - top)
            total = jnp.sum(diag, axis=1, keepdims=True)
            got = dot(diag.astype(BF), V[low:high, :])
            if i:
                left = jnp.exp(left - top)
                total = total + jnp.sum(left, axis=1, keepdims=True)
                got = got + dot(left.astype(BF), V[:low, :])
            outs.append(got)
            sums.append(total)
            QB[h, low:high, :] = with_norm(qa[h], h, top + jnp.log(total))
        full = finish(outs[0], outs[1], sums[0], sums[1])
        AF[low:high, :] = full
        AB[low:high, :] = full.astype(BF)

    def self_part(i):
        def self_block():
            self_rows(i, i * CH, (i + 1) * CH)

        self_block()
        for p in (2 * i, 2 * i + 1):
            src, dst = AB.at[p * TB : (p + 1) * TB, :], ao.at[:, rows_of(s, HP)]
            push(src, dst, plan.a_at, p, s, (r, p), when=s != p)

    self_part(0)
    mat_p(0)
    self_part(1)
    mat_r(2)
    self_part(2)
    self_part(3)
    ao[:, rows_of(s, HP)] = AB[rows_of(s, TB), :]

    ow_send(outer)
    mat_c(0)
    kv_pass()
    mat_p(2)
    xh, rstd = normalise(xs[own_tokens, :].astype(F32))
    n.XH[0] = xh
    n.RS[0] = rstd
    mat_take(0)
    for p in seq_peers:
        arrive(ao.at[:, rows_of(p, HP)], plan.a_at, p)
    h1 = xs[own_tokens, :].astype(F32) + dot(ao[...], mat(0))
    n.H[...] = h1
    xh, rstd = normalise(h1)
    n.XH[1] = xh
    n.RS[1] = rstd
    n2 = (xh * gain(1) + bias(1)).astype(BF)
    n.n2[...] = n2
    ow_send(inner)
    mat_c(1)
    in_plane()
    mat_take(1)
    cqo = n.wide
    cqo[...] = dot(n2, mat(1)).astype(BF)
    CQ = n.CQ

    def to_heads(src, dst, name):
        for k in range(1, S):
            p = (s + k) % S
            push(src.at[:, rows_of(p, HP)], dst.at[own_tokens, :], name, p, s, (r, p))
        dst[own_tokens, :] = src[:, rows_of(s, HP)]

    def heads_take(dst, name, k):
        zl = (z + k) % NZ
        if k:
            arrive(dst.at[rows_of(2 * zl + c, TB), :], name, 2 * zl + c)
        arrive(dst.at[rows_of(2 * zl + 1 - c, TB), :], name, 2 * zl + 1 - c)
        return rows_of(zl, CH)

    def to_tokens(src, dst, name, k):
        zl = (z + k) % NZ
        for p in ([2 * zl + c] if k else []) + [2 * zl + 1 - c]:
            push(src.at[rows_of(p, TB), :], dst.at[:, rows_of(s, HP)], name, p, s, (r, p))
        if not k:
            dst[:, rows_of(s, HP)] = src[own_tokens, :]

    to_heads(cqo, CQ, plan.a_cq)
    text_all()
    ow_second()

    CKA, CVA, CKT, CQB = n.CKA, n.CVA, n.CKT, n.CQB
    CF, CB, co = n.CF, n.out, n.co
    drain(plan.a_at)

    def prepare_cross(rows):
        CKA[0, rows, :], CKA[1, rows, :] = split_pair(CK[rows, :], n.kbc[rows, :])

    each(T, CH, prepare_cross)
    def cross_rows(rows):
        scaled = (CQ[rows, :].astype(F32) * scale).astype(BF)
        CQ[rows, :] = scaled
        qa = split_pair(scaled, oh[rows, :])
        outs, sums = [], []
        for h in range(2):
            got = dot_nt(qa[h], CKA[h])
            top = jnp.max(got, axis=1, keepdims=True)
            got = jnp.exp(got - top)
            total = jnp.sum(got, axis=1, keepdims=True)
            outs.append(dot(got.astype(BF), CV[...]))
            sums.append(total)
            CQB[h, rows, :] = with_norm(qa[h], h, top + jnp.log(total))
        full = finish(outs[0], outs[1], sums[0], sums[1])
        CF[rows, :] = full
        CB[rows, :] = full.astype(BF)

    def cross_part(k):
        rows = heads_take(CQ, plan.a_cq, k)

        def cross_block():
            cross_rows(rows)

        cross_block()
        to_tokens(CB, co, plan.a_cr, k)

    cross_part(0)
    mat_c(2)
    cross_part(1)
    cross_part(2)
    in_pass()
    cross_part(3)
    mat_take(2)
    for p in seq_peers:
        arrive(co.at[:, rows_of(p, HP)], plan.a_cr, p)
    h2 = n.H[...] + dot(co[...], mat(2))
    n.H[...] = h2
    xh, rstd = normalise(h2)
    n.XH[2] = xh
    n.RS[2] = rstd
    n3f = n.n3f
    n3f[rows_of(mem, TB), :] = (xh * gain(2) + bias(2)).astype(BF)
    gather_start(n3f, plan.n3, ffn_z0, GZ)

    got_ow.wait()
    ow_second_pass()
    plane_take(in_half, plan.in_r)
    plane_take(ow_half, plan.ow_r)
    for j in range(1, E):
        plane_take(out_view(j)[1], plan.ow_x + 4 * j)
    AD = n.AD
    ACT, DUP = AD.at[: G * TB], AD.at[G * TB :]
    UT = 512

    def reduce_core(ps, rb, name, zl):
        push(ps.at[rows_of(2 * zl + 1 - c, TB), :], rb.at[zl], name, zl, zl, (r, sib))

    def reduce_z(ps, rb, rz, cname, zname, z0, nz, zl, when=None):
        arrive(rb.at[zl], cname, zl)
        mine = rows_of(2 * zl + c, TB)
        ps[mine, :] = (ps[mine, :].astype(F32) + rb[zl].astype(F32)).astype(BF)
        push(ps.at[mine, :], rz.at[(z - z0 - zl + nz - 1) % nz], zname, zl, z - z0, (r, 2 * (z0 + zl) + c), when=when)

    def reduce_take(ps, rb, rz, cname, zname, z0, nz, summed=False):
        own = z - z0
        mine = rows_of(2 * own + c, TB)
        total = ps[mine, :].astype(F32)
        if not summed:
            arrive(rb.at[own], cname, own)
            total = total + rb[own].astype(F32)
        for k in range(1, nz):
            zl = (own + k) % nz
            arrive(rz.at[k - 1], zname, zl)
            total = total + rz[k - 1].astype(F32)
        return total

    def chain_send(mine, land, name, j):
        push(mine, land.at[0], name, 0, 0, (r, 2 * beside + c), when=beside == j)
        push(mine, land.at[1 + j % 2], name, 1 + j % 2, 1 + j % 2, (r, 2 * beside + c), when=outer & (j // 2 != side))

    def chain_relay(at, land, name):
        for k in range(2):
            to = 2 - 2 * side + k
            mine = at(to)

            def add():
                arrive(land.at[1 + k], name, 1 + k)
                mine[...] = (mine[...].astype(F32) + land[1 + k].astype(F32)).astype(BF)

            pl.when(inner)(add)
            push(mine, land.at[3], name, 3 + k, 3, (r, 2 * to + c), when=inner)

    def chain_total(at, land, name):
        arrive(land.at[0], name, 0)
        arrive(land.at[3], name, 3)
        return at(z)[...].astype(F32) + land[0].astype(F32) + land[3].astype(F32)

    def core_sum(ps, rb, cname, j):
        arrive(rb.at[j], cname, j)
        mine = ps.at[rows_of(2 * j + c, TB), :]
        mine[...] = (mine[...].astype(F32) + rb[j].astype(F32)).astype(BF)
        return mine

    def rows_at(ps):
        def at(j):
            return ps.at[rows_of(2 * j + c, TB), :]

        return at

    ps0 = n.ps0
    drain(plan.n1, plan.n1 + 24)
    NT = G * TB
    psE = ps0.at[:NT]
    psO = ps0.at[NT:]
    for k in range(GZ):
        gather_pass(ogf, plan.og, ffn_z0, GZ, k)
        gather_take(ogf, plan.og, ffn_z0, GZ, k)
        gather_pass(n3f, plan.n3, ffn_z0, GZ, k)
        rows = gather_take(n3f, plan.n3, ffn_z0, GZ, k)

        def hidden(cols):
            up = dot(n3f[rows, :], Win[:, cols])
            d_act = dot_nt(ogf[rows, :], Wout[cols, :])
            cdf = 0.5 * (1.0 + lax.erf(up * (0.5**0.5)))
            pdf = jnp.exp(-0.5 * up * up) * 0.3989422804014327
            ACT[rows, cols] = (up * cdf).astype(BF)
            DUP[rows, cols] = (d_act * (cdf + up * pdf)).astype(BF)

        def hidden_block():
            each(U, UT, hidden)

        def back_block():
            psE[rows, :] = dot_nt(DUP[rows, :], Win[...]).astype(BF)

        hidden_block()
        back_block()
        zl = (z - ffn_z0 + k) % GZ
        reduce_core(psE, n.rbE, plan.e_c, zl)
    for k in range(1, GZ):
        reduce_z(psE, n.rbE, n.rzE, plan.e_c, plan.e_z, ffn_z0, GZ, (z - ffn_z0 + k) % GZ)
    drain(plan.ow_r, plan.ow_g, plan.in_r, plan.in_s, *[plan.ow_x + 4 * j for j in range(1, E)])

    def out_core():
        for k in range(GZ):
            reduce_core(psO, n.rbO, plan.o_c, (z - ffn_z0 + k) % GZ)

    def out_z():
        for k in range(1, GZ):
            zl = (z - ffn_z0 + k) % GZ
            reduce_z(psO, n.rbO, n.rzO, plan.o_c, plan.o_z, ffn_z0, GZ, zl)

    def out_take():
        total = n.H[...] + reduce_take(psO, n.rbO, n.rzO, plan.o_c, plan.o_z, ffn_z0, GZ)
        emit(n.s_out, n.o_out, total.astype(BF))

    def gin_rows(cols):
        Win[cols, :] = dot_tn(n3f[:, cols], DUP[...]).astype(BF)

    def gin_block():
        each(D, 256, gin_rows)

    def gin_start():
        gin_block()
        fold_start(in_half, n.rgi, plan.gi_r)

    def gin_pass():
        fold_pass(in_half, n.rgi, plan.gi_r)

    rgi2 = n.rgi2

    def gin_send():
        fold_take(in_half, n.rgi, plan.gi_r)
        for p in seq_peers:
            push(Win.at[rows_of(r * S + p, DB), :], rgi2.at[s], plan.gi_s, p, s, (r, p))
        rgi2[s] = Win[own_rows, :]

    go_half = rows_view(Wout, E * UB)[1]
    rgo2 = n.rgo2

    def gout_pass():
        fold_pass(go_half, n.rgo, plan.go_r)

    def gout_send():
        fold_take(go_half, n.rgo, plan.go_r)
        for j in range(1, E):
            src = Wout.at[rows_of(r * E + (grp + j) % E, UB), :]
            p = (s + j * G) % S
            push(src, rgo2.at[grp], plan.go_g, p, s, (r, p))

    def mat_grad(i, left, right):
        drain(plan.m_z + 4 * i, plan.m_r + 4 * i, plan.m_c + 2 * i)

        def mat_block():
            mats[i][...] = dot_tn(left, right).astype(BF).reshape(mats[i].shape)

        mat_block()
        push(mats[i].at[:, 1 - c], n.rmc.at[i], plan.h_c + 2 * i, 0, 0, (r, sib))

    def mat_grad_2():
        mat_grad(2, co[...], n.GR[...].astype(BF))

    def mat_grad_1():
        mat_grad(1, n.n2[...], n.dqo[...])

    def mat_grad_0():
        mat_grad(0, ao[...], n.GR[...].astype(BF))

    def mat_grad_r(i):
        arrive(n.rmc.at[i], plan.h_c + 2 * i, 0)
        mine = mats[i].at[:, c]
        mine[...] = (mine[...].astype(F32) + n.rmc[i].astype(F32)).astype(BF)
        fold_start(mat_view(i)[1], n.rmr.at[i], plan.h_r + 8 * i)

    def mat_grad_p(i):
        fold_pass(mat_view(i)[1], n.rmr.at[i], plan.h_r + 8 * i)

    def mat_at(i):
        def at(j):
            return mats[i].at[r * NZ + j, c]

        return at

    def mat_grad_z(i):
        fold_take(mat_view(i)[1], n.rmr.at[i], plan.h_r + 8 * i)
        for j in range(NZ):
            chain_send(mat_at(i)(j), n.rmz.at[i], plan.h_z + 8 * i, j)

    def mat_grad_f(i):
        chain_relay(mat_at(i), n.rmz.at[i], plan.h_z + 8 * i)

    def mat_grad_take(i, stage, out):
        emit(stage, out, chain_total(mat_at(i), n.rmz.at[i], plan.h_z + 8 * i))

    psT = AD.at[:T, :TW]
    DKV = n.DKV
    GC, GQ = n.GC, n.GQ

    def text_send():
        for j in range(NZ):
            chain_send(core_sum(psT, n.rbT, plan.t_c, j), n.rzT, plan.t_z, j)

    def text_relay():
        chain_relay(rows_at(psT), n.rzT, plan.t_z)

    def sum_relay():
        chain_relay(rows_at(ps0), n.rz0, plan.s_z)

    span = TW // 2

    def gkv_rows(i):
        got = dot_tn(n.textv[:, i * span : (i + 1) * span], DKV[...])
        both = [got[:, q * HP : (q + 1) * HP].reshape(span // half, half, HP) for q in range(2)]
        both = jnp.concatenate(both, axis=1).reshape(2 * span, HP)
        Wkv3[2 * i * span : 2 * (i + 1) * span, :] = both.astype(BF)

    def gkv_block():
        gkv_rows(0)
        gkv_rows(1)

    def gkv_start():
        drain(plan.kv_s, plan.kv_r)
        gkv_block()
        fold_start(kv_half, n.rgk, plan.gk_r)

    def gkv_pass():
        fold_pass(kv_half, n.rgk, plan.gk_r)

    def gkv_send():
        fold_take(kv_half, n.rgk, plan.gk_r)
        for p in seq_peers:
            src = Wkv3.at[rows_of(r * S + p, KB), :]
            push(src, GC.at[:, rows_of(s, HP)], plan.gk_s, p, s, (r, p))
        GC[:, rows_of(s, HP)] = Wkv3[kv_rows, :]

    def gq_rows(cols):
        got = dot_tn(n1f[:, cols], n.DQKV[...]).astype(BF)
        for i in range(3):
            Wq3[i, cols, :] = got[:, i * HP : (i + 1) * HP]

    def gq_block():
        each(D, 256, gq_rows)

    def gq_start():
        drain(plan.q_s, plan.q_r)
        gq_block()
        fold_start(q_half, n.rgq, plan.gq_r)

    def gq_pass():
        fold_pass(q_half, n.rgq, plan.gq_r)

    def gq_send():
        fold_take(q_half, n.rgq, plan.gq_r)
        for p in seq_peers:
            src = Wq3.at[:, rows_of(r * S + p, DB), :]
            push(src, GQ.at[:, :, rows_of(s, HP)], plan.gq_s, p, s, (r, p))
        GQ[:, :, rows_of(s, HP)] = Wq3[:, own_rows, :]

    gin_start()
    for k in range(GZ):
        rows = rows_of((z - ffn_z0 + k) % GZ, CH)

        def out_block_rows():
            psO[rows, :] = dot(ACT[rows, :], Wout[...]).astype(BF)

        out_block_rows()

    def gout_rows(cols):
        Wout[cols, :] = dot_tn(ACT[:, cols], ogf[...]).astype(BF)

    def gout_block():
        each(U, 256, gout_rows)

    gout_block()
    fold_start(go_half, n.rgo, plan.go_r)
    out_core()

    def norm_back(i, e):
        n.gg[i : i + 1, :] = jnp.sum(e * n.XH[i], axis=0, keepdims=True)
        n.gg[3 + i : 4 + i, :] = jnp.sum(e, axis=0, keepdims=True)
        y = e * gain(i)
        xhat = n.XH[i]
        a = jnp.mean(y, axis=1, keepdims=True)
        b = jnp.mean(y * xhat, axis=1, keepdims=True)
        return (y - a - xhat * b) * n.RS[i]

    e = reduce_take(psE, n.rbE, n.rzE, plan.e_c, plan.e_z, ffn_z0, GZ)
    g2 = ogf[rows_of(mem, TB), :].astype(F32) + norm_back(2, e)
    n.GR[...] = g2
    dco = n.wide
    drain(plan.a_cq)
    dco[...] = dot_nt(g2.astype(BF), mat(2)).astype(BF)
    DC = n.DC
    to_heads(dco, DC, plan.b_cr)
    mat_grad_2()

    def ones_rows(count):
        spot = lax.broadcasted_iota(jnp.int32, (count, HP), 1) % HD
        return jnp.where((spot >= 4) & (spot < 7), 1.0, 0.0)

    def prepare_cross_back(rows):
        CVA[0, rows, :], CVA[1, rows, :] = split_pair(CV[rows, :], ones_rows(CH))
        CKT[:, rows] = jnp.transpose(CK[rows, :].astype(F32)).astype(BF)

    def with_delta(grad, full):
        front = first_half(grad.shape)
        wide = grad.astype(F32)
        prod = wide * full
        d0 = jnp.sum(jnp.where(front, prod, 0.0), axis=1, keepdims=True)
        d1 = jnp.sum(jnp.where(front, 0.0, prod), axis=1, keepdims=True)
        zero = jnp.zeros_like(wide)
        return (
            with_norm(jnp.where(front, wide, zero), 0, d0),
            with_norm(jnp.where(front, zero, wide), 1, d1),
        )

    each(T, CH, prepare_cross_back)
    DCK, DCV, DQ, dqo = n.DCK, n.DCV, n.out, n.dqo
    drain(plan.a_cr)

    def heads_join(a, b, axis):
        spot = lax.broadcasted_iota(jnp.int32, a.shape, axis)
        return jnp.where(spot < HD, a, b)

    def cross_back_rows(k, rows):
        grad = DC[rows, :]
        ga = with_delta(grad, CF[rows, :])
        q2 = CQ[rows, :]
        dv, dk, dq = [], [], []
        for h in range(2):
            prob = jnp.exp(dot_nt(CKA[h], CQB[h, rows, :]))
            ds = (prob * dot_nt(CVA[h], ga[h])).astype(BF)
            dv.append(dot(prob.astype(BF), grad))
            dk.append(dot(ds, q2))
            dq.append(dot(CKT[...], ds))
        dvj, dkj = heads_join(dv[0], dv[1], 1), heads_join(dk[0], dk[1], 1)
        if k:
            DCV[...] += dvj
            DCK[...] += dkj
        else:
            DCV[...] = dvj
            DCK[...] = dkj
        DQ[rows, :] = (jnp.transpose(heads_join(dq[0], dq[1], 0)) * scale).astype(BF)

    def cross_back_part(k):
        rows = heads_take(DC, plan.b_cr, k)

        def cross_back_block():
            cross_back_rows(k, rows)

        cross_back_block()
        to_tokens(DQ, dqo, plan.b_cq, k)

    cross_back_part(0)
    gin_pass()
    out_z()
    cross_back_part(1)
    cross_back_part(2)
    mat_grad_r(2)
    cross_back_part(3)

    DKV[:, :HP] = DCK[...].astype(BF)
    DKV[:, HP:] = DCV[...].astype(BF)
    for j in range(NZ):
        rows = pl.ds(j * CH, CH)

        def text_back():
            psT[rows, :] = dot_nt(DKV[rows, :], Wkv[...]).astype(BF)

        text_back()
        reduce_core(psT, n.rbT, plan.t_c, j)
    text_send()

    for p in seq_peers:
        arrive(dqo.at[:, rows_of(p, HP)], plan.b_cq, p)
    e = dot_nt(dqo[...], mat(1))
    g1 = n.GR[...] + norm_back(1, e)
    n.GR[...] = g1
    dao = n.wide
    drain(plan.b_cr)
    dao[...] = dot_nt(g1.astype(BF), mat(0)).astype(BF)
    DA = n.DA
    to_heads(dao, DA, plan.b_at)
    gout_pass()
    gkv_start()
    gin_send()
    mat_grad_1()
    mat_grad_0()
    gout_send()

    VA, KT, DOA = CVA, CKT, CQB
    DQT, DQKV = n.DQT, n.DQKV

    def prepare_self_back(rows):
        VA[0, rows, :], VA[1, rows, :] = split_pair(V[rows, :], ones_rows(CH))
        KT[:, rows] = jnp.transpose(K[rows, :].astype(F32)).astype(BF)

    each(T, CH, prepare_self_back)
    for k in range(NZ):
        rows = heads_take(DA, plan.b_at, k)
        DOA[0, rows, :], DOA[1, rows, :] = with_delta(DA[rows, :], AF[rows, :])
    mat_grad_p(2)
    mat_grad_r(0)
    text_relay()
    out_take()
    drain(plan.e_c, plan.e_z, plan.o_c, plan.o_z)

    def self_back_rows(j, low, high):
        grad, q2 = DA[low:, :], Q[low:, :]
        dv, dk, dq = [], [], []
        for h in range(2):
            sc = dot_nt(KA[h, low:high, :], QB[h, low:, :])
            head = jnp.where(qpos <= kpos, sc[:, :CH], NEG)
            sc = jnp.concatenate([head, sc[:, CH:]], axis=1) if j < NZ - 1 else head
            prob = jnp.exp(sc)
            ds = (prob * dot_nt(VA[h, low:high, :], DOA[h, low:, :])).astype(BF)
            dv.append(dot(prob.astype(BF), grad))
            dk.append(dot(ds, q2))
            dq.append(dot(KT[:, low:high], ds))
        if j:
            DQT[:, low:] += heads_join(dq[0], dq[1], 0)
        else:
            DQT[...] = heads_join(dq[0], dq[1], 0)
        DQKV[low:high, :HP] = (jnp.transpose(DQT[:, low:high]) * scale).astype(BF)
        DQKV[low:high, HP : 2 * HP] = heads_join(dk[0], dk[1], 1).astype(BF)
        DQKV[low:high, 2 * HP :] = heads_join(dv[0], dv[1], 1).astype(BF)
        ps0[low:high, :] = dot_nt(DQKV[low:high, :], Wq[...]).astype(BF)

    def self_back_part(j):
        def self_back_block():
            self_back_rows(j, j * CH, (j + 1) * CH)

        self_back_block()
        reduce_core(ps0, n.rb0, plan.s_c, j)
        if j:
            chain_send(core_sum(ps0, n.rb0, plan.s_c, j - 1), n.rz0, plan.s_z, j - 1)

    self_back_part(0)
    self_back_part(1)
    gkv_pass()
    self_back_part(2)
    self_back_part(3)
    mat_grad_r(1)
    mat_grad_p(1)
    chain_send(core_sum(ps0, n.rb0, plan.s_c, NZ - 1), n.rz0, plan.s_z, NZ - 1)
    mat_grad_p(0)
    mat_grad_z(2)
    sum_relay()
    gq_start()
    mat_grad_z(0)
    mat_grad_f(2)
    mat_grad_z(1)

    e = chain_total(rows_at(ps0), n.rz0, plan.s_z)
    back = norm_back(0, e)
    gg, rgg, gg2, rgg2 = n.gg, n.rgg, n.gg2, n.rgg2
    GW = D // R
    for k, p in enumerate(row_peers, 1):
        push(gg.at[:, rows_of(p, GW)], rgg.at[R - 1 - k], plan.gg_r, p, r, (p, s))
    emit(n.s_ig, n.o_ig, n.GR[...] + back)
    mat_grad_f(0)
    mat_grad_f(1)
    gq_pass()
    total = gg[:, rows_of(r, GW)]
    for k, p in enumerate(row_peers):
        arrive(rgg.at[k], plan.gg_r, p)
        total = total + rgg[k]
    gg2[...] = total
    for p in seq_peers:
        push(gg2.at[:, rows_of(p // per, 128)], rgg2.at[s], plan.gg_s, p, s, (r, p))
    gkv_send()
    gq_send()
    mat_grad_take(2, n.s_co, n.o_co)
    mat_grad_take(1, n.s_cq, n.o_cq)
    mat_grad_take(0, n.s_so, n.o_so)
    emit(n.s_tg, n.o_tg, chain_total(rows_at(psT), n.rzT, plan.t_z))
    total = Wout[out_rows, :].astype(F32)
    for j in range(1, E):
        g2i = (grp + j) % E
        arrive(rgo2.at[g2i], plan.go_g, (s + j * G) % S)
        total = total + rgo2[g2i].astype(F32)
    emit(n.s_ow, n.o_ow, total)
    for p in seq_peers:
        arrive(rgi2.at[p], plan.gi_s, p)
    for m in range(G):
        total = rgi2[m].astype(F32)
        for g in range(1, E):
            total = total + rgi2[g * G + m].astype(F32)
        for rr in range(R):
            for j in range(E):
                b = rr * S + j * G + m
                at = (rr * E + j) * UB
                n.s_in[:, b * UB : (b + 1) * UB] = total[:, at : at + UB]
    finals.append(local(n.s_in, n.o_in, 16 + len(finals)))
    for p in seq_peers:
        arrive(GC.at[:, rows_of(p, HP)], plan.gk_s, p)
    emit(n.s_ckv, n.o_ckv, GC[...].astype(F32))
    total = gg2[:, rows_of(s // per, 128)]
    for p in seq_peers:
        arrive(rgg2.at[p], plan.gg_s, p)
        total = total + rgg2[p]
    emit(n.s_gb, n.o_gb, total)
    for p in seq_peers:
        arrive(GQ.at[:, :, rows_of(p, HP)], plan.gq_s, p)
    emit(n.s_qkv, n.o_qkv, GQ[...].astype(F32))
    drain(*list(pending))
    for cp in finals:
        cp.wait()


def copy_kernel(count, *refs):
    stages, into, out_of = refs[2 * count : 3 * count], refs[3 * count], refs[3 * count + 1]
    loads = [pltpu.make_async_copy(refs[i], stages[i], into.at[i]) for i in range(count)]
    stores = [
        pltpu.make_async_copy(stages[i], refs[count + i], out_of.at[i]) for i in range(count)
    ]
    for cp in loads:
        cp.start()
    for load, store in zip(loads, stores):
        load.wait()
        store.start()
    for cp in stores:
        cp.wait()


def settle(arrays):
    anywhere = pl.BlockSpec(memory_space=pl.ANY)
    return pl.pallas_call(
        functools.partial(copy_kernel, len(arrays)),
        out_shape=[jax.ShapeDtypeStruct(a.shape, a.dtype) for a in arrays],
        in_specs=[anywhere] * len(arrays),
        out_specs=[anywhere] * len(arrays),
        scratch_shapes=[pltpu.VMEM(a.shape, a.dtype) for a in arrays]
        + [pltpu.SemaphoreType.DMA((len(arrays),))] * 2,
    )(*arrays)


def fused_shards(
    hidden_in, clip_lengths, text_lengths, text_states, norm_gain, norm_bias, self_qkv,
    self_out, cross_query, cross_kv, cross_out, ffn_in, ffn_out, out_grad,
):
    R, S = lax.axis_size("rows"), lax.axis_size("seq")
    TB, D = hidden_in.shape[1:]
    TW = text_states.shape[2]
    T, HP, DB = TB * S, D // S, D // (R * S)
    FF = ffn_in.shape[1]
    G = GROUP
    E, U, UB, NT, NZ = S // G, FF // G, FF // (R * S), G * TB, S // 2
    GZ = G // 2
    KB = 2 * cross_kv.shape[1]
    index = lax.axis_index("rows") * S + lax.axis_index("seq")
    per = 128 // DB
    both = jnp.concatenate([norm_gain, norm_bias], axis=0)
    both = jnp.pad(both, ((0, 10), (0, 0)))
    spot = jnp.arange(128, dtype=jnp.int32)[None, :] // DB
    gb = jnp.where(spot == index % per, jnp.tile(both, (1, per)), jnp.zeros((), both.dtype))
    ins = dict(
        cl=clip_lengths, tl=text_lengths, x=hidden_in.reshape(TB, D), og=out_grad.reshape(TB, D),
        text=text_states.reshape(T, TW), gb=gb, wqkv=self_qkv, wo=self_out, wcq=cross_query,
        wco=cross_out, wckv=cross_kv.reshape(KB, D), win=ffn_in, wout=ffn_out,
    )
    outs = dict(
        o_out=((TB, D), BF), o_ig=((TB, D), F32), o_tg=((TB, TW), F32), o_gb=((8, 128), F32),
        o_qkv=(self_qkv.shape, F32), o_so=(self_out.shape, F32), o_cq=(cross_query.shape, F32),
        o_ckv=((KB, D), F32), o_co=(cross_out.shape, F32), o_in=(ffn_in.shape, F32),
        o_ow=(ffn_out.shape, F32),
    )
    plan, count = semaphore_plan(GZ)
    hp = (T, HP)
    pair = (2, T, HP)
    scratch = dict(
        textv=((T, TW), BF),
        gbt=((R, S, 16, 128), BF), gbf=((16, D), F32), Wq3=((3, D, HP), BF), Wq=((D, 3 * HP), BF),
        Wkv3=((R * S * KB, HP), BF), Wkv=((TW, 2 * HP), BF),
        Wm0=((R * NZ, 2, DB, D), BF), Wm1=((R * NZ, 2, DB, D), BF), Wm2=((R * NZ, 2, DB, D), BF),
        Win=((D, U), BF), Wout=((U, D), BF), winp=((DB, FF), BF),
        XH=((3, TB, D), F32), RS=((3, TB, 1), F32), H=((TB, D), F32), GR=((TB, D), F32),
        n1f=((T, D), BF), n3f=((NT, D), BF), ogf=((NT, D), BF), n2=((TB, D), BF),
        oh=(hp, BF), kbs=(hp, BF), kbc=(hp, BF),
        Q=(hp, BF), K=(hp, BF), V=(hp, BF), CK=(hp, BF), CV=(hp, BF), CQ=(hp, BF),
        KA=(pair, BF), QB=(pair, BF),
        CKA=(pair, BF), CVA=(pair, BF), CQB=(pair, BF), CKT=((HP, T), BF),
        AF=(hp, F32), CF=(hp, F32), out=(hp, BF), DC=(hp, BF), DA=(hp, BF),
        ao=((TB, D), BF), wide=((TB, D), BF), co=((TB, D), BF), dqo=((TB, D), BF),
        DCK=(hp, F32), DCV=(hp, F32), DKV=((T, 2 * HP), BF),
        DQT=((HP, T), F32), DQKV=((T, 3 * HP), BF),
        AD=((2 * NT, U), BF),
        ps0=((max(T, 2 * NT), D), BF),
        rbE=((GZ, TB, D), BF), rzE=((GZ - 1, TB, D), BF), rbO=((GZ, TB, D), BF), rzO=((GZ - 1, TB, D), BF),
        rbT=((NZ, TB, TW), BF), rzT=((NZ, TB, TW), BF), rb0=((NZ, TB, D), BF), rz0=((NZ, TB, D), BF),
        rgo=((6, E * UB // 2, D), BF), rgo2=((E, UB, D), BF), rgi=((6, S * DB // 2, U), BF), rgi2=((S, DB, U), BF),
        rgk=((6, S * KB // 2, HP), BF), GC=((KB, D), BF), rgq=((6, 3, S * DB // 2, HP), BF), GQ=((3, DB, D), BF),
        gg=((8, D), F32), rgg=((R - 1, 8, D // R), F32), gg2=((8, D // R), F32), rgg2=((S, 8, 128), F32),
        rmc=((3, R * NZ, DB, D), BF), rmr=((3, 6, NZ // 2, DB, D), BF), rmz=((3, NZ, DB, D), BF),
    )
    for name, spec in outs.items():
        scratch[name.replace("o_", "s_")] = spec
    names = list(ins) + list(outs) + list(scratch) + ["ss", "rs", "ls"]
    anywhere = pl.BlockSpec(memory_space=pl.ANY)
    smem = pl.BlockSpec(memory_space=pltpu.SMEM)
    got = pl.pallas_call(
        functools.partial(layer_kernel, plan, names),
        out_shape=[jax.ShapeDtypeStruct(*v) for v in outs.values()],
        in_specs=[smem, smem] + [anywhere] * (len(ins) - 2),
        out_specs=[anywhere] * len(outs),
        scratch_shapes=[pltpu.VMEM(*v) for v in scratch.values()]
        + [pltpu.SemaphoreType.DMA((k,)) for k in (count, count, 32)],
        compiler_params=pltpu.CompilerParams(
            collective_id=0, has_side_effects=True, vmem_limit_bytes=63 << 20
        ),
    )(*ins.values())
    got = list(got)
    got = list(settle(got[:3] + got[4:])) + [got[3]]
    o = types.SimpleNamespace(**dict(zip([k for k in outs if k != "o_gb"] + ["o_gb"], got)))
    mine = lax.dynamic_slice(o.o_gb, (0, (index % per) * DB), (8, DB))
    return (
        o.o_out.reshape(hidden_in.shape), o.o_ig.reshape(hidden_in.shape),
        o.o_tg.reshape(1, TB, TW), mine[:3], mine[3:6], o.o_qkv, o.o_so, o.o_cq,
        o.o_ckv.reshape(cross_kv.shape), o.o_co, o.o_in, o.o_ow,
    )


def fits(mesh):
    return dict(mesh.shape) == {"rows": 4, "seq": 8}


def solution(mesh):
    placed = (
        P("rows", "seq", None),
        P("rows", None),
        P("rows", None),
        P("rows", None, None),
        P(None, ("rows", "seq")),
        P(None, ("rows", "seq")),
        P(None, ("rows", "seq"), None),
        P(("rows", "seq"), None),
        P(("rows", "seq"), None),
        P(None, ("rows", "seq"), None),
        P(("rows", "seq"), None),
        P(("rows", "seq"), None),
        P(("rows", "seq"), None),
        P("rows", "seq", None),
    )
    return jax.shard_map(
        fused_shards if fits(mesh) else shards,
        mesh=mesh,
        in_specs=placed,
        out_specs=(
            P("rows", "seq", None),
            P("rows", "seq", None),
            P("rows", "seq", None),
            P(None, ("rows", "seq")),
            P(None, ("rows", "seq")),
            P(None, ("rows", "seq"), None),
            P(("rows", "seq"), None),
            P(("rows", "seq"), None),
            P(None, ("rows", "seq"), None),
            P(("rows", "seq"), None),
            P(("rows", "seq"), None),
            P(("rows", "seq"), None),
        ),
        check_vma=False,
    )
```

```python
import functools
import types

import jax
import jax.numpy as jnp
from jax import lax
from jax.experimental import pallas as pl
from jax.experimental.pallas import tpu as pltpu
from jax.sharding import PartitionSpec as P

HD = 64


epsilon = 1e-05
masked_score = -1e30
group_heads = 4
highest = lax.Precision.HIGHEST


def layer_norm(values, gains, biases):
    average = jnp.mean(values, axis=-1, keepdims=True)
    centred = values - average
    variance = jnp.mean(centred * centred, axis=-1, keepdims=True)
    return centred * lax.rsqrt(variance + epsilon) * gains + biases


def gelu_exact(values):
    return jax.nn.gelu(values, approximate=False)


def project(left, weight):
    return jnp.einsum("rtd,de->rte", left, weight, preferred_element_type=jnp.float32)


def weight_term(left, right):
    return jnp.einsum("rtd,rte->de", left, right, preferred_element_type=jnp.float32)


def back_project(gradient, weight):
    return jnp.einsum("rte,de->rtd", gradient, weight, preferred_element_type=jnp.float32)


def exact_weight_term(left, right):
    return jnp.einsum(
        "rtd,rte->de", left, right, precision=highest, preferred_element_type=jnp.float32
    )


def exact_back_project(gradient, weight):
    return jnp.einsum(
        "rte,de->rtd", gradient, weight, precision=highest, preferred_element_type=jnp.float32
    )


def split_heads(values):
    return values.reshape(values.shape[0], values.shape[1], values.shape[2] // HD, HD)


def clip_of(positions, clip_ends):
    return jnp.sum((positions[None, :, None] >= clip_ends[:, None, :]).astype(jnp.int32), axis=2)


def pair_mask(query_pos, query_clip, key_pos, key_clip):
    causal = query_pos[None, :, None] >= key_pos[None, None, :]
    return (causal & (query_clip[:, :, None] == key_clip[:, None, :]))[:, None]


def blocks_of(arrived, frame_span):
    block_count = arrived.shape[1] // frame_span
    shaped = arrived.reshape((arrived.shape[0], block_count, frame_span) + arrived.shape[2:])
    return jnp.moveaxis(shaped, 1, 0)


def block_fold(visit_block, frame_span, carried, arrived):
    block_count = arrived.shape[1] // frame_span
    starts = frame_span * jnp.arange(block_count, dtype=jnp.int32)

    def scan_step(state, block_pair):
        return (visit_block(state, block_pair[0], block_pair[1]), None)

    carried, unused = lax.scan(scan_step, carried, (blocks_of(arrived, frame_span), starts))
    return carried


def head_dot(gradient, output):
    summed = jnp.sum(split_heads(gradient).astype(jnp.float32) * split_heads(output), axis=3)
    return jnp.swapaxes(summed, 1, 2)


def text_project(texts, w_text):
    return jnp.concatenate([project(texts, w_text[0]), project(texts, w_text[1])], axis=2).astype(
        jnp.bfloat16
    )


def self_forward(queries, key_value, clip_ends, clip_ids, frames):
    row_count, frame_span, model_width = queries.shape
    head_count = model_width // HD
    score_scale = HD ** (-0.5)
    query_heads = split_heads(queries)
    last_frame = frames[frame_span - 1]

    def visit_block(state, key_block, first_key):
        key_pos = first_key + jnp.arange(frame_span, dtype=jnp.int32)

        def accumulate(carried):
            running_max, running_sum, output_sum = carried
            key_heads = split_heads(key_block[:, :, :model_width])
            value_heads = split_heads(key_block[:, :, model_width:])
            allowed = pair_mask(frames, clip_ids, key_pos, clip_of(key_pos, clip_ends))
            scores = (
                jnp.einsum(
                    "rqhd,rkhd->rhqk", query_heads, key_heads, preferred_element_type=jnp.float32
                )
                * score_scale
            )
            scores = jnp.where(allowed, scores, masked_score)
            new_max = jnp.maximum(running_max, jnp.max(scores, axis=3))
            weights = jnp.where(allowed, jnp.exp(scores - new_max[..., None]), 0.0)
            shrink = jnp.exp(running_max - new_max)
            running_sum = running_sum * shrink + jnp.sum(weights, axis=3)
            output_sum = output_sum * shrink[..., None] + jnp.einsum(
                "rhqk,rkhd->rhqd",
                weights.astype(jnp.bfloat16),
                value_heads,
                preferred_element_type=jnp.float32,
            )
            return (new_max, running_sum, output_sum)

        return lax.cond(first_key > last_frame, lambda carried: carried, accumulate, state)

    initial = (
        jnp.full((row_count, head_count, frame_span), masked_score, jnp.float32),
        jnp.zeros((row_count, head_count, frame_span), jnp.float32),
        jnp.zeros((row_count, head_count, frame_span, HD), jnp.float32),
    )
    running_max, running_sum, output_sum = block_fold(
        visit_block, frame_span, initial, lax.all_gather(key_value, "seq", axis=1, tiled=True)
    )
    attended = output_sum / running_sum[..., None]
    return (
        jnp.swapaxes(attended, 1, 2).reshape(row_count, frame_span, model_width),
        running_max + jnp.log(running_sum),
    )


def self_query_grad(queries, key_value, clip_ends, clip_ids, frames, log_norm, delta_sum, d_attn):
    row_count, frame_span, model_width = queries.shape
    head_count = model_width // HD
    score_scale = HD ** (-0.5)
    query_heads = split_heads(queries)
    grad_heads = split_heads(d_attn)
    last_frame = frames[frame_span - 1]

    def visit_block(state, key_block, first_key):
        key_pos = first_key + jnp.arange(frame_span, dtype=jnp.int32)

        def accumulate(carried):
            key_heads = split_heads(key_block[:, :, :model_width])
            value_heads = split_heads(key_block[:, :, model_width:])
            allowed = pair_mask(frames, clip_ids, key_pos, clip_of(key_pos, clip_ends))
            scores = (
                jnp.einsum(
                    "rqhd,rkhd->rhqk", query_heads, key_heads, preferred_element_type=jnp.float32
                )
                * score_scale
            )
            probability = jnp.where(allowed, jnp.exp(scores - log_norm[..., None]), 0.0)
            d_prob = jnp.einsum(
                "rqhd,rkhd->rhqk", grad_heads, value_heads, preferred_element_type=jnp.float32
            )
            d_score = (probability * (d_prob - delta_sum[..., None])).astype(jnp.bfloat16)
            return carried + jnp.einsum(
                "rhqk,rkhd->rhqd", d_score, key_heads, preferred_element_type=jnp.float32
            )

        return lax.cond(first_key > last_frame, lambda carried: carried, accumulate, state)

    initial = jnp.zeros((row_count, head_count, frame_span, HD), jnp.float32)
    d_query = block_fold(
        visit_block, frame_span, initial, lax.all_gather(key_value, "seq", axis=1, tiled=True)
    )
    d_query = jnp.swapaxes(d_query, 1, 2).reshape(row_count, frame_span, model_width) * score_scale
    return d_query.astype(jnp.bfloat16)


def self_key_grad(query_grad, key_value, clip_ends, clip_ids, frames, gathered_stats):
    row_count, frame_span, double_width = key_value.shape
    model_width = double_width // 2
    head_count = model_width // HD
    score_scale = HD ** (-0.5)
    key_heads = split_heads(key_value[:, :, :model_width])
    value_heads = split_heads(key_value[:, :, model_width:])
    all_norm, all_delta = gathered_stats
    first_own = frames[0]

    def visit_block(state, query_block, first_query):
        query_pos = first_query + jnp.arange(frame_span, dtype=jnp.int32)

        def accumulate(carried):
            d_key, d_value = carried
            query_heads = split_heads(query_block[:, :, :model_width])
            grad_heads = split_heads(query_block[:, :, model_width:])
            log_norm = jnp.swapaxes(
                lax.dynamic_slice_in_dim(all_norm, first_query, frame_span, 1), 1, 2
            )
            delta_sum = jnp.swapaxes(
                lax.dynamic_slice_in_dim(all_delta, first_query, frame_span, 1), 1, 2
            )
            allowed = pair_mask(query_pos, clip_of(query_pos, clip_ends), frames, clip_ids)
            scores = (
                jnp.einsum(
                    "rqhd,rkhd->rhqk", query_heads, key_heads, preferred_element_type=jnp.float32
                )
                * score_scale
            )
            probability = jnp.where(allowed, jnp.exp(scores - log_norm[..., None]), 0.0)
            d_value = d_value + jnp.einsum(
                "rhqk,rqhd->rhkd",
                probability.astype(jnp.bfloat16),
                grad_heads,
                preferred_element_type=jnp.float32,
            )
            d_prob = jnp.einsum(
                "rqhd,rkhd->rhqk", grad_heads, value_heads, preferred_element_type=jnp.float32
            )
            d_score = (probability * (d_prob - delta_sum[..., None])).astype(jnp.bfloat16)
            d_key = d_key + jnp.einsum(
                "rhqk,rqhd->rhkd", d_score, query_heads, preferred_element_type=jnp.float32
            )
            return (d_key, d_value)

        return lax.cond(
            first_query + frame_span - 1 < first_own, lambda carried: carried, accumulate, state
        )

    zeros_heads = jnp.zeros((row_count, head_count, frame_span, HD), jnp.float32)
    d_key, d_value = block_fold(
        visit_block,
        frame_span,
        (zeros_heads, zeros_heads),
        lax.all_gather(query_grad, "seq", axis=1, tiled=True),
    )
    d_key = jnp.swapaxes(d_key, 1, 2).reshape(row_count, frame_span, model_width) * score_scale
    d_value = jnp.swapaxes(d_value, 1, 2).reshape(row_count, frame_span, model_width)
    return (d_key.astype(jnp.bfloat16), d_value.astype(jnp.bfloat16))


def cross_forward(queries, text_kv, readable):
    row_count, frame_span, model_width = queries.shape
    group_width = group_heads * HD
    score_scale = HD ** (-0.5)
    outputs = []
    log_norms = []
    for group_index in range(model_width // group_width):
        lower_edge = group_index * group_width
        query_heads = split_heads(queries[:, :, lower_edge : lower_edge + group_width])
        key_heads = split_heads(text_kv[:, :, lower_edge : lower_edge + group_width])
        value_heads = split_heads(
            text_kv[:, :, model_width + lower_edge : model_width + lower_edge + group_width]
        )
        scores = (
            jnp.einsum(
                "rqhd,rkhd->rhqk", query_heads, key_heads, preferred_element_type=jnp.float32
            )
            * score_scale
        )
        scores = jnp.where(readable, scores, masked_score)
        largest = jnp.max(scores, axis=3)
        weights = jnp.where(readable, jnp.exp(scores - largest[..., None]), 0.0)
        totals = jnp.sum(weights, axis=3)
        probability = (weights / totals[..., None]).astype(jnp.bfloat16)
        attended = jnp.einsum(
            "rhqk,rkhd->rqhd", probability, value_heads, preferred_element_type=jnp.float32
        )
        outputs.append(attended.reshape(row_count, frame_span, group_width))
        log_norms.append(largest + jnp.log(totals))
    return (jnp.concatenate(outputs, axis=2), jnp.concatenate(log_norms, axis=1))


def cross_backward(queries, text_kv, readable, log_norm, d_cross, delta_sum):
    row_count, frame_span, model_width = queries.shape
    slot_count = text_kv.shape[1]
    group_width = group_heads * HD
    score_scale = HD ** (-0.5)
    d_queries = []
    d_keys = []
    d_values = []
    for group_index in range(model_width // group_width):
        lower_edge = group_index * group_width
        head_edge = group_index * group_heads
        query_heads = split_heads(queries[:, :, lower_edge : lower_edge + group_width])
        grad_heads = split_heads(d_cross[:, :, lower_edge : lower_edge + group_width])
        key_heads = split_heads(text_kv[:, :, lower_edge : lower_edge + group_width])
        value_heads = split_heads(
            text_kv[:, :, model_width + lower_edge : model_width + lower_edge + group_width]
        )
        group_norm = log_norm[:, head_edge : head_edge + group_heads]
        group_delta = delta_sum[:, head_edge : head_edge + group_heads]
        scores = (
            jnp.einsum(
                "rqhd,rkhd->rhqk", query_heads, key_heads, preferred_element_type=jnp.float32
            )
            * score_scale
        )
        probability = jnp.where(readable, jnp.exp(scores - group_norm[..., None]), 0.0)
        d_value = jnp.einsum(
            "rhqk,rqhd->rkhd",
            probability.astype(jnp.bfloat16),
            grad_heads,
            preferred_element_type=jnp.float32,
        )
        d_values.append(d_value.reshape(row_count, slot_count, group_width))
        d_prob = jnp.einsum(
            "rqhd,rkhd->rhqk", grad_heads, value_heads, preferred_element_type=jnp.float32
        )
        d_score = (probability * (d_prob - group_delta[..., None])).astype(jnp.bfloat16)
        d_query = jnp.einsum(
            "rhqk,rkhd->rqhd", d_score, key_heads, preferred_element_type=jnp.float32
        )
        d_queries.append(d_query.reshape(row_count, frame_span, group_width) * score_scale)
        d_key = jnp.einsum(
            "rhqk,rqhd->rkhd", d_score, query_heads, preferred_element_type=jnp.float32
        )
        d_keys.append(d_key.reshape(row_count, slot_count, group_width) * score_scale)
    return (jnp.concatenate(d_queries, axis=2), jnp.concatenate(d_keys + d_values, axis=2))


def shards(
    hidden_in,
    clip_lengths,
    text_lengths,
    text_states,
    norm_gain,
    norm_bias,
    self_qkv,
    self_out,
    cross_query,
    cross_kv,
    cross_out,
    ffn_in,
    ffn_out,
    out_grad,
):
    gathered = (
        lax.all_gather(norm_gain, ("rows", "seq"), axis=1, tiled=True),
        lax.all_gather(norm_bias, ("rows", "seq"), axis=1, tiled=True),
        lax.all_gather(self_qkv, ("rows", "seq"), axis=1, tiled=True),
        lax.all_gather(self_out, ("rows", "seq"), axis=0, tiled=True),
        lax.all_gather(cross_query, ("rows", "seq"), axis=0, tiled=True),
        lax.all_gather(cross_kv, ("rows", "seq"), axis=1, tiled=True),
        lax.all_gather(cross_out, ("rows", "seq"), axis=0, tiled=True),
        lax.all_gather(ffn_in, ("rows", "seq"), axis=0, tiled=True),
        lax.all_gather(ffn_out, ("rows", "seq"), axis=0, tiled=True),
    )
    gains_all, biases_all, w_qkv, w_self, w_query, w_text, w_cross, w_up, w_down = gathered
    gains = gains_all.astype(jnp.float32)
    biases = biases_all.astype(jnp.float32)
    row_count, frame_span, model_width = hidden_in.shape
    seq_index = lax.axis_index("seq")
    frames = seq_index * frame_span + jnp.arange(frame_span, dtype=jnp.int32)
    clip_ends = jnp.cumsum(clip_lengths, axis=1)
    clip_ids = clip_of(frames, clip_ends)
    text_ends = jnp.cumsum(text_lengths, axis=1)
    text_starts = text_ends - text_lengths
    chosen = (
        clip_ids[:, :, None] == jnp.arange(clip_lengths.shape[1], dtype=jnp.int32)[None, None, :]
    )
    slot_low = jnp.sum(jnp.where(chosen, text_starts[:, None, :], 0), axis=2)
    slot_high = jnp.sum(jnp.where(chosen, text_ends[:, None, :], 0), axis=2)
    slot_index = jnp.arange(text_states.shape[1], dtype=jnp.int32)
    readable = (
        (slot_index[None, None, :] >= slot_low[:, :, None])
        & (slot_index[None, None, :] < slot_high[:, :, None])
    )[:, None]
    slot_share = text_states.shape[1] // lax.axis_size("seq")
    own_text = lax.dynamic_slice_in_dim(text_states, seq_index * slot_share, slot_share, 1)
    resid = hidden_in.astype(jnp.float32)
    normed_full, pull_first = jax.vjp(layer_norm, resid, gains[0], biases[0])
    normed = normed_full.astype(jnp.bfloat16)
    queries = project(normed, w_qkv[0]).astype(jnp.bfloat16)
    keys_low = project(normed, w_qkv[1]).astype(jnp.bfloat16)
    values_low = project(normed, w_qkv[2]).astype(jnp.bfloat16)
    key_value = jnp.concatenate([keys_low, values_low], axis=2)
    self_full, self_norm = self_forward(queries, key_value, clip_ends, clip_ids, frames)
    attended = self_full.astype(jnp.bfloat16)
    after_self = resid + project(attended, w_self)
    normed_full, pull_second = jax.vjp(layer_norm, after_self, gains[1], biases[1])
    normed_two = normed_full.astype(jnp.bfloat16)
    cross_queries = project(normed_two, w_query).astype(jnp.bfloat16)
    text_kv = lax.all_gather(text_project(own_text, w_text), "seq", axis=1, tiled=True)
    cross_full, cross_norm = cross_forward(cross_queries, text_kv, readable)
    crossed = cross_full.astype(jnp.bfloat16)
    after_cross = after_self + project(crossed, w_cross)
    normed_full, pull_third = jax.vjp(layer_norm, after_cross, gains[2], biases[2])
    normed_three = normed_full.astype(jnp.bfloat16)
    hidden_up = project(normed_three, w_up)
    activated_full, pull_gelu = jax.vjp(gelu_exact, hidden_up)
    activated = activated_full.astype(jnp.bfloat16)
    block_out = (after_cross + project(activated, w_down)).astype(jnp.bfloat16)
    gradient = out_grad.astype(jnp.float32)
    g_down = weight_term(activated, out_grad)
    d_up = pull_gelu(back_project(out_grad, w_down))[0].astype(jnp.bfloat16)
    g_up = weight_term(normed_three, d_up)
    d_third, g_gain_three, g_bias_three = pull_third(back_project(d_up, w_up))
    gradient = gradient + d_third
    grad_low = gradient.astype(jnp.bfloat16)
    g_cross = weight_term(crossed, grad_low)
    d_cross = back_project(grad_low, w_cross).astype(jnp.bfloat16)
    cross_delta = head_dot(d_cross, cross_full)
    d_cross_query, d_text_kv = cross_backward(
        cross_queries, text_kv, readable, cross_norm, d_cross, cross_delta
    )
    key_weight = w_text[0].astype(jnp.float32)
    value_weight = w_text[1].astype(jnp.float32)
    own_grad = lax.psum_scatter(
        d_text_kv.astype(jnp.bfloat16), "seq", scatter_dimension=1, tiled=True
    ).astype(jnp.float32)
    grad_text_key = own_grad[:, :, :model_width]
    grad_text_value = own_grad[:, :, model_width:]
    own_exact = own_text.astype(jnp.float32)
    g_text = jnp.stack(
        [exact_weight_term(own_exact, grad_text_key), exact_weight_term(own_exact, grad_text_value)]
    )
    text_grad = exact_back_project(grad_text_key, key_weight) + exact_back_project(
        grad_text_value, value_weight
    )
    d_cross_query = d_cross_query.astype(jnp.bfloat16)
    g_query = weight_term(normed_two, d_cross_query)
    d_second, g_gain_two, g_bias_two = pull_second(back_project(d_cross_query, w_query))
    gradient = gradient + d_second
    grad_low = gradient.astype(jnp.bfloat16)
    g_self = weight_term(attended, grad_low)
    d_attn = back_project(grad_low, w_self).astype(jnp.bfloat16)
    self_delta = head_dot(d_attn, self_full)
    d_query = self_query_grad(
        queries, key_value, clip_ends, clip_ids, frames, self_norm, self_delta, d_attn
    )
    gathered_stats = (
        lax.all_gather(jnp.swapaxes(self_norm, 1, 2), "seq", axis=1, tiled=True),
        lax.all_gather(jnp.swapaxes(self_delta, 1, 2), "seq", axis=1, tiled=True),
    )
    query_grad = jnp.concatenate([queries, d_attn], axis=2)
    d_key, d_value = self_key_grad(
        query_grad, key_value, clip_ends, clip_ids, frames, gathered_stats
    )
    g_qkv = jnp.stack(
        [weight_term(normed, d_query), weight_term(normed, d_key), weight_term(normed, d_value)]
    )
    d_normed = (
        back_project(d_query, w_qkv[0])
        + back_project(d_key, w_qkv[1])
        + back_project(d_value, w_qkv[2])
    )
    d_first, g_gain_one, g_bias_one = pull_first(d_normed)
    input_grad = gradient + d_first
    g_gain = jnp.stack([g_gain_one, g_gain_two, g_gain_three])
    g_bias = jnp.stack([g_bias_one, g_bias_two, g_bias_three])
    reduced = (
        lax.psum_scatter(g_gain, ("rows", "seq"), scatter_dimension=1, tiled=True),
        lax.psum_scatter(g_bias, ("rows", "seq"), scatter_dimension=1, tiled=True),
        lax.psum_scatter(g_qkv, ("rows", "seq"), scatter_dimension=1, tiled=True),
        lax.psum_scatter(g_self, ("rows", "seq"), scatter_dimension=0, tiled=True),
        lax.psum_scatter(g_query, ("rows", "seq"), scatter_dimension=0, tiled=True),
        lax.psum_scatter(g_text, ("rows", "seq"), scatter_dimension=1, tiled=True),
        lax.psum_scatter(g_cross, ("rows", "seq"), scatter_dimension=0, tiled=True),
        lax.psum_scatter(g_up, ("rows", "seq"), scatter_dimension=0, tiled=True),
        lax.psum_scatter(g_down, ("rows", "seq"), scatter_dimension=0, tiled=True),
    )
    return (
        block_out,
        input_grad,
        text_grad,
        reduced[0],
        reduced[1],
        reduced[2],
        reduced[3],
        reduced[4],
        reduced[5],
        reduced[6],
        reduced[7],
        reduced[8],
    )


MESH = pl.DeviceIdType.MESH
BF = jnp.bfloat16
F32 = jnp.float32
GROUP = 4
NEG = -1e30


def dot(a, b):
    return lax.dot_general(a, b, (((1,), (0,)), ((), ())), preferred_element_type=F32)


def dot_nt(a, b):
    return lax.dot_general(a, b, (((1,), (1,)), ((), ())), preferred_element_type=F32)


def dot_tn(a, b):
    return lax.dot_general(a, b, (((0,), (0,)), ((), ())), preferred_element_type=F32)


def mult(index, step):
    return pl.multiple_of(index * step, step)


def rows_of(index, step):
    return pl.ds(mult(index, step), step)


def each(count, step, body):
    def turn(i, carry):
        body(pl.ds(pl.multiple_of(i * step, step), step))
        return carry

    lax.fori_loop(0, count // step, turn, 0)


def three_parts(value):
    first = value.astype(BF).astype(F32)
    rest = value - first
    second = rest.astype(BF).astype(F32)
    return first, second, (rest - second).astype(BF).astype(F32)


def normalise(values):
    average = jnp.mean(values, axis=-1, keepdims=True)
    centred = values - average
    rstd = lax.rsqrt(jnp.mean(centred * centred, axis=-1, keepdims=True) + epsilon)
    return centred * rstd, rstd


def semaphore_plan(group_chips):
    sizes = dict(
        gb_s=8, gb_r=4, q_s=8, q_r=4, kv_s=8, kv_r=4, in_s=8, in_r=4, ow_g=8, ow_r=4, ow_x=4 * 8,
        n1=48, og=16, n3=16, a_at=8, a_cq=8, a_cr=8, b_cr=8, b_cq=8, b_at=8,
        e_c=4, e_z=4, o_c=4, o_z=4, t_c=4, t_z=8, s_c=4, s_z=8,
        gq_r=8, gq_s=8, gi_r=8, gi_s=8, go_r=8, go_g=8, gk_r=8, gk_s=8, gg_r=4, gg_s=8,
        m_z=12, m_r=12, m_c=6, h_c=6, h_r=24, h_z=24,
    )
    base, plan = 0, {}
    for name, size in sizes.items():
        plan[name] = base
        base += size
    return types.SimpleNamespace(**plan), base


def layer_kernel(plan, names, *refs):
    n = types.SimpleNamespace(**dict(zip(names, refs)))
    R, S, NZ, D = 4, 8, 4, n.x.shape[1]
    TB = n.x.shape[0]
    CH = 2 * TB
    T = S * TB
    HP = D // S
    FF = n.win.shape[1]
    G = GROUP
    GZ = G // 2
    E = S // G
    U = FF // G
    UB = FF // (R * S)
    DB = D // (R * S)
    TW = n.text.shape[1]
    KB = n.wckv.shape[0]
    r, s = lax.axis_index("rows"), lax.axis_index("seq")
    z, c = s // 2, s % 2
    sib = s + 1 - 2 * c
    ffn_z0 = (z // GZ) * GZ
    grp, mem = s // G, s % G
    ss, rs = n.ss, n.rs
    pending = {}
    gbt, Wq3, Wkv3, Win, Wout, winp, ogf = n.gbt, n.Wq3, n.Wkv3, n.Win, n.Wout, n.winp, n.ogf
    mats = [n.Wm0, n.Wm1, n.Wm2]

    def push(src, dst, name, to, origin, dev, send_shift=0, when=None):
        cp = pltpu.make_async_remote_copy(
            src_ref=src, dst_ref=dst,
            send_sem=ss.at[name + send_shift + to],
            recv_sem=rs.at[name + origin],
            device_id=dev, device_id_type=MESH,
        )
        pending.setdefault(name, []).append((cp, when))
        if when is None:
            cp.start()
        else:
            pl.when(when)(cp.start)

    def drain(*which):
        for name in which:
            for cp, when in pending.pop(name, []):
                if when is None:
                    cp.wait_send()
                else:
                    pl.when(when)(cp.wait_send)

    def arrive(landing, name, origin, when=None):
        cp = pltpu.make_async_remote_copy(
            src_ref=landing, dst_ref=landing, send_sem=ss.at[name],
            recv_sem=rs.at[name + origin], device_id=(r, sib), device_id_type=MESH,
        )
        if when is None:
            cp.wait_recv()
        else:
            pl.when(when)(cp.wait_recv)

    side = z // 2
    inner, outer = (z + 1) % NZ // 2 == 1, (z + 1) % NZ // 2 == 0
    beside = z + 1 - 2 * (z % 2)
    far_inner, far_outer = 2 - side, 3 - 3 * side
    legs = (((far_inner, None), (beside, outer)), ((far_outer, None), (beside, inner)))

    def spread(leg, send):
        for zl, when in legs[leg]:
            for core in range(2):
                send(2 * zl + core, when)

    across_x, across_y = r + 1 - 2 * (r % 2), (r + 2) % R
    corner = (across_x + 2) % R

    def plane_start(block, name):
        push(block(r), block(r), name, 0, 0, (across_x, s))
        push(block(r), block(r), name, 1, 1, (across_y, s))

    def plane_pass(block, half, name):
        arrive(block(across_x), name, 0)
        push(half(across_x, 0), half(across_x, 0), name, 2, 2, (across_y, s))
        arrive(block(across_y), name, 1)
        push(half(across_y, 1), half(across_y, 1), name, 3, 3, (across_x, s))

    def plane_take(half, name):
        arrive(half(corner, 0), name, 2)
        arrive(half(corner, 1), name, 3)

    def fold_start(half, landed, name):
        push(half(corner, 0), landed.at[1], name, 1, 1, (across_x, s))
        push(half(corner, 1), landed.at[3], name, 3, 3, (across_y, s))
        push(half(across_x, 0), landed.at[0], name, 0, 0, (across_x, s))
        push(half(across_y, 1), landed.at[2], name, 2, 2, (across_y, s))

    def fold_pass(half, landed, name):
        for k, (near, to) in enumerate(((across_y, across_y), (across_x, across_x))):
            arrive(landed.at[1 + 2 * k], name, 1 + 2 * k)
            mine = half(near, k)
            mine[...] = (mine[...].astype(F32) + landed[1 + 2 * k].astype(F32)).astype(BF)
            push(mine, landed.at[4 + k], name, 4 + k, 4 + k, (to, s))

    def fold_take(half, landed, name):
        for k in range(2):
            arrive(landed.at[2 * k], name, 2 * k)
            arrive(landed.at[4 + k], name, 4 + k)
            mine = half(r, k)
            total = mine[...].astype(F32) + landed[2 * k].astype(F32) + landed[4 + k].astype(F32)
            mine[...] = total.astype(BF)

    def rows_view(ref, step):
        def block(p):
            return ref.at[rows_of(p, step), :]

        def half(p, k):
            return ref.at[rows_of(2 * p + k, step // 2), :]

        return block, half

    def mid_view(ref, step):
        def block(p):
            return ref.at[:, rows_of(p, step), :]

        def half(p, k):
            return ref.at[:, rows_of(2 * p + k, step // 2), :]

        return block, half

    def mat_view(i):
        def block(p):
            return mats[i].at[pl.ds(p * NZ, NZ), c]

        def half(p, k):
            return mats[i].at[pl.ds(p * NZ + 2 * k, 2), c]

        return block, half

    def out_view(j):
        def block(p):
            return Wout.at[rows_of(p * E + (grp + j) % E, UB), :]

        def half(p, k):
            return Wout.at[rows_of(2 * (p * E + (grp + j) % E) + k, UB // 2), :]

        return block, half

    seq_peers = [(s + k) % S for k in range(1, S)]
    row_peers = [(r + k) % R for k in range(1, R)]
    z_peers = [(z + k) % NZ for k in range(1, NZ)]

    barrier = pltpu.get_barrier_semaphore()
    for p in seq_peers:
        pl.semaphore_signal(barrier, inc=1, device_id=(r, p), device_id_type=MESH)
    for p in row_peers:
        pl.semaphore_signal(barrier, inc=1, device_id=(p, s), device_id_type=MESH)
    finals = []

    def local(src, dst, i):
        cp = pltpu.make_async_copy(src, dst, n.ls.at[i])
        cp.start()
        return cp

    def emit(stage, out, value):
        stage[...] = value
        finals.append(local(stage, out, 16 + len(finals)))

    own_mats = [n.wo, n.wcq, n.wco]
    own_rows = rows_of(r * S + s, DB)
    kv_rows = rows_of(r * S + s, KB)
    out_rows = rows_of(r * E + grp, UB)
    xs, own_tokens = n.ps0, rows_of(s, TB)
    got_x = local(n.x, xs.at[own_tokens, :], 0)
    got_gb = local(n.gb, gbt.at[r, s], 1)
    got_q = local(n.wqkv.at[:, :, rows_of(s, HP)], Wq3.at[:, own_rows, :], 2)
    got_kv = local(n.wckv.at[:, rows_of(s, HP)], Wkv3.at[kv_rows, :], 3)
    got_mats = [local(own_mats[i], mats[i].at[r * NZ + z, c], 4 + i) for i in range(3)]
    for m in range(G):
        for rr in range(R):
            for j in range(E):
                b = rr * S + j * G + m
                at = m * U + (rr * E + j) * UB
                local(n.win.at[:, b * UB : (b + 1) * UB], winp.at[:, at : at + UB], 7)
    got_ow = local(n.wout, Wout.at[out_rows, :], 8)
    got_og = local(n.og, ogf.at[rows_of(mem, TB), :], 9)
    got_text = local(n.text, n.textv, 10)

    lane = lax.broadcasted_iota(jnp.int32, (T, HP), 1)
    row = lax.broadcasted_iota(jnp.int32, (T, HP), 0)
    slot = lane % HD
    cl, tl = n.cl, n.tl

    def inside(lengths):
        low, found = jnp.int32(0), jnp.zeros((T, HP), jnp.bool_)
        for k in range(4):
            high = low + lengths[0, k]
            found = found | ((slot == k) & (row >= low) & (row < high))
            low = high
        return found

    ones_tail = jnp.where((slot >= 4) & (slot < 7), 1.0, 0.0)

    def mask_block():
        in_clip = inside(cl)
        n.oh[...] = jnp.where(in_clip, 1.0, 0.0).astype(BF)
        n.kbs[...] = jnp.where(slot < 4, jnp.where(in_clip, 0.0, NEG), ones_tail).astype(BF)
        n.kbc[...] = jnp.where(slot < 4, jnp.where(inside(tl), 0.0, NEG), ones_tail).astype(BF)

    mask_block()

    pl.semaphore_wait(barrier, S + R - 2)

    q_block, q_half = mid_view(Wq3, S * DB)
    kv_block, kv_half = rows_view(Wkv3, S * KB)
    in_block, in_half = rows_view(Win, S * DB)
    ow_block, ow_half = out_view(0)

    def mat_z(i, leg):
        for p, when in legs[leg]:
            dst = mats[i].at[r * NZ + z, c]
            push(own_mats[i], dst, plan.m_z + 4 * i, p, z, (r, 2 * p + c), when=when)

    def mat_r(i):
        for p in z_peers:
            arrive(mats[i].at[r * NZ + p, c], plan.m_z + 4 * i, p)
        got_mats[i].wait()
        plane_start(mat_view(i)[0], plan.m_r + 4 * i)

    def mat_p(i):
        plane_pass(*mat_view(i), plan.m_r + 4 * i)

    def mat_c(i):
        plane_take(mat_view(i)[1], plan.m_r + 4 * i)
        block = mats[i].at[:, c]
        push(block, block, plan.m_c + 2 * i, 0, 0, (r, sib))

    def mat_take(i):
        arrive(mats[i].at[:, 1 - c], plan.m_c + 2 * i, 0)

    def mat(i):
        return mats[i][...].reshape(D, D)

    def kv_send(p, when):
        src = n.wckv.at[:, rows_of(p, HP)]
        push(src, Wkv3.at[kv_rows, :], plan.kv_s, p, s, (r, p), when=when)

    def kv_first():
        kv_send(sib, None)
        spread(0, kv_send)

    def kv_plane():
        for p in seq_peers:
            arrive(Wkv3.at[rows_of(r * S + p, KB), :], plan.kv_s, p)
        got_kv.wait()
        plane_start(kv_block, plan.kv_r)

    def kv_pass():
        plane_pass(kv_block, kv_half, plan.kv_r)

    def in_send(p, when):
        src = winp.at[:, rows_of(p % G, U)]
        push(src, Win.at[own_rows, :], plan.in_s, p, s, (r, p), when=when)

    def in_first():
        in_send(sib, None)
        spread(0, in_send)

    def in_plane():
        for p in seq_peers:
            arrive(Win.at[rows_of(r * S + p, DB), :], plan.in_s, p)
        plane_start(in_block, plan.in_r)

    def in_pass():
        plane_pass(in_block, in_half, plan.in_r)

    def ow_send(when):
        for j in range(1, E):
            p = (s + j * G) % S
            push(n.wout, Wout.at[out_rows, :], plan.ow_g, p, s, (r, p), when=when)

    def ow_first():
        push(n.wout, ow_block(r), plan.ow_r, 0, 0, (across_x, s))
        push(n.wout, ow_block(r), plan.ow_r, 1, 1, (across_y, s))

    def ow_pass():
        plane_pass(ow_block, ow_half, plan.ow_r)

    def ow_second():
        for j in range(1, E):
            arrive(out_view(j)[0](r), plan.ow_g, (s + j * G) % S)
            plane_start(out_view(j)[0], plan.ow_x + 4 * j)

    def ow_second_pass():
        for j in range(1, E):
            plane_pass(*out_view(j), plan.ow_x + 4 * j)

    def gather_start(buf, name, z0, nz):
        m = s - 2 * z0
        block = buf.at[rows_of(m, TB), :]
        for k in range(1, nz):
            zl = (z - z0 + k) % nz
            push(block, block, name, 2 * zl + c, m, (r, 2 * (z0 + zl) + c))
        push(block, block, name, sib - 2 * z0, m, (r, sib))

    def og_start():
        got_og.wait()
        gather_start(ogf, plan.og, ffn_z0, GZ)

    for p in seq_peers:
        push(n.gb, gbt.at[r, s], plan.gb_s, p, s, (r, p))
    for p in seq_peers:
        push(n.wqkv.at[:, :, rows_of(p, HP)], Wq3.at[:, own_rows, :], plan.q_s, p, s, (r, p))

    mat_z(1, 1)
    mat_z(1, 0)
    spread(1, kv_send)
    TH = TB // 2
    for q in range(2):
        src, dst = n.x.at[q * TH : (q + 1) * TH, :], xs.at[rows_of(2 * s + q, TH), :]
        for zl in (far_inner, beside):
            push(src, dst, plan.n1 + 24 * q, 2 * zl + c, s, (r, 2 * zl + c))
        push(src, dst, plan.n1 + 24 * q, sib, s, (r, sib))

    for p in seq_peers:
        arrive(gbt.at[r, p], plan.gb_s, p)
    got_gb.wait()
    for p in row_peers:
        push(gbt.at[r], gbt.at[r], plan.gb_r, p, r, (p, s))
    pltpu.make_async_copy(n.win, winp, n.ls.at[7]).wait()
    Win[own_rows, :] = winp[:, rows_of(mem, U)]
    ow_first()
    mat_z(0, 1)
    for p in seq_peers:
        arrive(Wq3.at[:, rows_of(r * S + p, DB), :], plan.q_s, p)
    got_q.wait()
    plane_start(q_block, plan.q_r)
    mat_z(0, 0)

    for p in row_peers:
        arrive(gbt.at[p], plan.gb_r, p)
    per = 128 // DB
    gbf = n.gbf
    for g in range(D // 128):
        total = None
        for k in range(per):
            rr, sx = divmod(g * per + k, S)
            tile = gbt[rr, sx].astype(F32)
            total = tile if total is None else total + tile
        gbf[:, g * 128 : (g + 1) * 128] = total

    def gain(i):
        return gbf[i : i + 1, :]

    def bias(i):
        return gbf[3 + i : 4 + i, :]

    def first_half(shape):
        return lax.broadcasted_iota(jnp.int32, shape, 1) < HD

    def split_pair(value, other):
        front = first_half(value.shape)
        v, o = value.astype(F32), other.astype(F32)
        return jnp.where(front, v, o).astype(BF), jnp.where(front, o, v).astype(BF)

    def gather_pass(buf, name, z0, nz, k):
        zl = (z - z0 + k) % nz
        if k:
            block = buf.at[rows_of(2 * zl + c, TB), :]
            arrive(block, name, 2 * zl + c)
            push(block, block, name, 2 * zl + c, 2 * zl + c, (r, sib), send_shift=8)

    def gather_take(buf, name, z0, nz, k):
        zl = (z - z0 + k) % nz
        arrive(buf.at[rows_of(2 * zl + 1 - c, TB), :], name, 2 * zl + 1 - c)
        return rows_of(zl, CH)

    def chain_pass(zl, q):
        origin, name = 2 * zl + c, plan.n1 + 24 * q
        block = xs.at[rows_of(2 * origin + q, TH), :]
        arrive(block, name, origin)
        push(block, block, name, 16 + origin, origin, (r, 2 * beside + c), when=inner & (zl // 2 != side))
        push(block, block, name, 8 + origin, origin, (r, sib))

    def chain_take(zl):
        origin = 2 * zl + 1 - c
        for q in range(2):
            arrive(xs.at[rows_of(2 * origin + q, TH), :], plan.n1 + 24 * q, origin)
        return rows_of(zl, CH)

    n1f, Wq = n.n1f, n.Wq
    Q, K, V = n.Q, n.K, n.V
    KA = n.KA
    scale = HD ** (-0.5)

    def norm_rows(rows):
        xh = normalise(xs[rows, :].astype(F32))[0]
        n1f[rows, :] = (xh * gain(0) + bias(0)).astype(BF)

    def qkv_chunk(rows):
        def block():
            qkv_block(rows)

        block()

    def qkv_block(rows):
        got = dot(n1f[rows, :], Wq[...])
        Q[rows, :] = (got[:, :HP].astype(BF).astype(F32) * scale).astype(BF)
        K[rows, :] = got[:, HP : 2 * HP].astype(BF)
        V[rows, :] = got[:, 2 * HP :].astype(BF)
        KA[0, rows, :], KA[1, rows, :] = split_pair(K[rows, :], n.kbs[rows, :])

    got_x.wait()
    rows = chain_take(z)
    norm_rows(rows)
    kv_first()
    chain_pass(far_inner, 0)
    chain_pass(far_outer, 0)
    in_first()
    mat_r(1)
    mat_z(2, 0)
    plane_pass(q_block, q_half, plan.q_r)
    chain_pass(far_inner, 1)
    chain_pass(far_outer, 1)
    mat_r(0)
    mat_z(2, 1)
    rows_1 = chain_take(far_inner)
    norm_rows(rows_1)
    og_start()
    rows_2 = chain_take(far_outer)
    norm_rows(rows_2)
    ow_pass()
    kv_plane()
    mat_p(1)
    plane_take(q_half, plan.q_r)
    for i in range(3):
        Wq[:, i * HP : (i + 1) * HP] = Wq3[i]
    qkv_chunk(rows)
    qkv_chunk(rows_1)
    qkv_chunk(rows_2)
    chain_pass(beside, 0)
    chain_pass(beside, 1)
    rows = chain_take(beside)
    norm_rows(rows)
    qkv_chunk(rows)
    spread(1, in_send)
    CK, CV = n.CK, n.CV
    half = KB // 2
    Wkv = n.Wkv

    def text_rows(rows):
        got = dot(n.textv[rows, :], Wkv[...]).astype(BF)
        CK[rows, :] = got[:, :HP]
        CV[rows, :] = got[:, HP:]

    def text_block():
        each(T, CH, text_rows)

    def text_all():
        plane_take(kv_half, plan.kv_r)
        wide = Wkv3[...].astype(F32).reshape(R * S, KB, HP)
        Wkv[:, :HP] = wide[:, :half, :].reshape(TW, HP).astype(BF)
        Wkv[:, HP:] = wide[:, half:, :].reshape(TW, HP).astype(BF)
        got_text.wait()
        text_block()

    AF, QB = n.AF, n.QB
    oh = n.oh
    AB = n.out
    ao = n.ao

    def finish(o0, o1, l0, l1):
        return jnp.where(first_half(o0.shape), o0 / l0, o1 / l1)

    def with_norm(q_aug, head, norm):
        spot = lax.broadcasted_iota(jnp.int32, q_aug.shape, 1)
        base = (1 - head) * HD
        a, b, d = three_parts(-norm)
        w = q_aug.astype(F32)
        w = jnp.where(spot == base + 4, a, w)
        w = jnp.where(spot == base + 5, b, w)
        return jnp.where(spot == base + 6, d, w).astype(BF)

    kpos = lax.broadcasted_iota(jnp.int32, (CH, CH), 1)
    qpos = lax.broadcasted_iota(jnp.int32, (CH, CH), 0)
    def self_rows(i, low, high):
        qa = split_pair(Q[low:high, :], oh[low:high, :])
        outs, sums = [], []
        for h in range(2):
            diag = jnp.where(kpos <= qpos, dot_nt(qa[h], KA[h, low:high, :]), NEG)
            top = jnp.max(diag, axis=1, keepdims=True)
            if i:
                left = dot_nt(qa[h], KA[h, :low, :])
                top = jnp.maximum(top, jnp.max(left, axis=1, keepdims=True))
            diag = jnp.exp(diag - top)
            total = jnp.sum(diag, axis=1, keepdims=True)
            got = dot(diag.astype(BF), V[low:high, :])
            if i:
                left = jnp.exp(left - top)
                total = total + jnp.sum(left, axis=1, keepdims=True)
                got = got + dot(left.astype(BF), V[:low, :])
            outs.append(got)
            sums.append(total)
            QB[h, low:high, :] = with_norm(qa[h], h, top + jnp.log(total))
        full = finish(outs[0], outs[1], sums[0], sums[1])
        AF[low:high, :] = full
        AB[low:high, :] = full.astype(BF)

    def self_part(i):
        def self_block():
            self_rows(i, i * CH, (i + 1) * CH)

        self_block()
        for p in (2 * i, 2 * i + 1):
            src, dst = AB.at[p * TB : (p + 1) * TB, :], ao.at[:, rows_of(s, HP)]
            push(src, dst, plan.a_at, p, s, (r, p), when=s != p)

    self_part(0)
    mat_p(0)
    self_part(1)
    mat_r(2)
    self_part(2)
    self_part(3)
    ao[:, rows_of(s, HP)] = AB[rows_of(s, TB), :]

    ow_send(outer)
    mat_c(0)
    kv_pass()
    mat_p(2)
    xh, rstd = normalise(xs[own_tokens, :].astype(F32))
    n.XH[0] = xh
    n.RS[0] = rstd
    mat_take(0)
    for p in seq_peers:
        arrive(ao.at[:, rows_of(p, HP)], plan.a_at, p)
    h1 = xs[own_tokens, :].astype(F32) + dot(ao[...], mat(0))
    n.H[...] = h1
    xh, rstd = normalise(h1)
    n.XH[1] = xh
    n.RS[1] = rstd
    n2 = (xh * gain(1) + bias(1)).astype(BF)
    n.n2[...] = n2
    ow_send(inner)
    mat_c(1)
    in_plane()
    mat_take(1)
    cqo = n.wide
    cqo[...] = dot(n2, mat(1)).astype(BF)
    CQ = n.CQ

    def to_heads(src, dst, name):
        for k in range(1, S):
            p = (s + k) % S
            push(src.at[:, rows_of(p, HP)], dst.at[own_tokens, :], name, p, s, (r, p))
        dst[own_tokens, :] = src[:, rows_of(s, HP)]

    def heads_take(dst, name, k):
        zl = (z + k) % NZ
        if k:
            arrive(dst.at[rows_of(2 * zl + c, TB), :], name, 2 * zl + c)
        arrive(dst.at[rows_of(2 * zl + 1 - c, TB), :], name, 2 * zl + 1 - c)
        return rows_of(zl, CH)

    def to_tokens(src, dst, name, k):
        zl = (z + k) % NZ
        for p in ([2 * zl + c] if k else []) + [2 * zl + 1 - c]:
            push(src.at[rows_of(p, TB), :], dst.at[:, rows_of(s, HP)], name, p, s, (r, p))
        if not k:
            dst[:, rows_of(s, HP)] = src[own_tokens, :]

    to_heads(cqo, CQ, plan.a_cq)
    text_all()
    ow_second()

    CKA, CVA, CKT, CQB = n.CKA, n.CVA, n.CKT, n.CQB
    CF, CB, co = n.CF, n.out, n.co
    drain(plan.a_at)

    def prepare_cross(rows):
        CKA[0, rows, :], CKA[1, rows, :] = split_pair(CK[rows, :], n.kbc[rows, :])

    each(T, CH, prepare_cross)
    def cross_rows(rows):
        scaled = (CQ[rows, :].astype(F32) * scale).astype(BF)
        CQ[rows, :] = scaled
        qa = split_pair(scaled, oh[rows, :])
        outs, sums = [], []
        for h in range(2):
            got = dot_nt(qa[h], CKA[h])
            top = jnp.max(got, axis=1, keepdims=True)
            got = jnp.exp(got - top)
            total = jnp.sum(got, axis=1, keepdims=True)
            outs.append(dot(got.astype(BF), CV[...]))
            sums.append(total)
            CQB[h, rows, :] = with_norm(qa[h], h, top + jnp.log(total))
        full = finish(outs[0], outs[1], sums[0], sums[1])
        CF[rows, :] = full
        CB[rows, :] = full.astype(BF)

    def cross_part(k):
        rows = heads_take(CQ, plan.a_cq, k)

        def cross_block():
            cross_rows(rows)

        cross_block()
        to_tokens(CB, co, plan.a_cr, k)

    cross_part(0)
    mat_c(2)
    cross_part(1)
    cross_part(2)
    in_pass()
    cross_part(3)
    mat_take(2)
    for p in seq_peers:
        arrive(co.at[:, rows_of(p, HP)], plan.a_cr, p)
    h2 = n.H[...] + dot(co[...], mat(2))
    n.H[...] = h2
    xh, rstd = normalise(h2)
    n.XH[2] = xh
    n.RS[2] = rstd
    n3f = n.n3f
    n3f[rows_of(mem, TB), :] = (xh * gain(2) + bias(2)).astype(BF)
    gather_start(n3f, plan.n3, ffn_z0, GZ)

    got_ow.wait()
    ow_second_pass()
    plane_take(in_half, plan.in_r)
    plane_take(ow_half, plan.ow_r)
    for j in range(1, E):
        plane_take(out_view(j)[1], plan.ow_x + 4 * j)
    AD = n.AD
    ACT, DUP = AD.at[: G * TB], AD.at[G * TB :]
    UT = 512

    def reduce_core(ps, rb, name, zl):
        push(ps.at[rows_of(2 * zl + 1 - c, TB), :], rb.at[zl], name, zl, zl, (r, sib))

    def reduce_z(ps, rb, rz, cname, zname, z0, nz, zl, when=None):
        arrive(rb.at[zl], cname, zl)
        mine = rows_of(2 * zl + c, TB)
        ps[mine, :] = (ps[mine, :].astype(F32) + rb[zl].astype(F32)).astype(BF)
        push(ps.at[mine, :], rz.at[(z - z0 - zl + nz - 1) % nz], zname, zl, z - z0, (r, 2 * (z0 + zl) + c), when=when)

    def reduce_take(ps, rb, rz, cname, zname, z0, nz, summed=False):
        own = z - z0
        mine = rows_of(2 * own + c, TB)
        total = ps[mine, :].astype(F32)
        if not summed:
            arrive(rb.at[own], cname, own)
            total = total + rb[own].astype(F32)
        for k in range(1, nz):
            zl = (own + k) % nz
            arrive(rz.at[k - 1], zname, zl)
            total = total + rz[k - 1].astype(F32)
        return total

    def chain_send(mine, land, name, j):
        push(mine, land.at[0], name, 0, 0, (r, 2 * beside + c), when=beside == j)
        push(mine, land.at[1 + j % 2], name, 1 + j % 2, 1 + j % 2, (r, 2 * beside + c), when=outer & (j // 2 != side))

    def chain_relay(at, land, name):
        for k in range(2):
            to = 2 - 2 * side + k
            mine = at(to)

            def add():
                arrive(land.at[1 + k], name, 1 + k)
                mine[...] = (mine[...].astype(F32) + land[1 + k].astype(F32)).astype(BF)

            pl.when(inner)(add)
            push(mine, land.at[3], name, 3 + k, 3, (r, 2 * to + c), when=inner)

    def chain_total(at, land, name):
        arrive(land.at[0], name, 0)
        arrive(land.at[3], name, 3)
        return at(z)[...].astype(F32) + land[0].astype(F32) + land[3].astype(F32)

    def core_sum(ps, rb, cname, j):
        arrive(rb.at[j], cname, j)
        mine = ps.at[rows_of(2 * j + c, TB), :]
        mine[...] = (mine[...].astype(F32) + rb[j].astype(F32)).astype(BF)
        return mine

    def rows_at(ps):
        def at(j):
            return ps.at[rows_of(2 * j + c, TB), :]

        return at

    ps0 = n.ps0
    drain(plan.n1, plan.n1 + 24)
    NT = G * TB
    psE = ps0.at[:NT]
    psO = ps0.at[NT:]
    for k in range(GZ):
        gather_pass(ogf, plan.og, ffn_z0, GZ, k)
        gather_take(ogf, plan.og, ffn_z0, GZ, k)
        gather_pass(n3f, plan.n3, ffn_z0, GZ, k)
        rows = gather_take(n3f, plan.n3, ffn_z0, GZ, k)

        def hidden(cols):
            up = dot(n3f[rows, :], Win[:, cols])
            d_act = dot_nt(ogf[rows, :], Wout[cols, :])
            cdf = 0.5 * (1.0 + lax.erf(up * (0.5**0.5)))
            pdf = jnp.exp(-0.5 * up * up) * 0.3989422804014327
            ACT[rows, cols] = (up * cdf).astype(BF)
            DUP[rows, cols] = (d_act * (cdf + up * pdf)).astype(BF)

        def hidden_block():
            each(U, UT, hidden)

        def back_block():
            psE[rows, :] = dot_nt(DUP[rows, :], Win[...]).astype(BF)

        hidden_block()
        back_block()
        zl = (z - ffn_z0 + k) % GZ
        reduce_core(psE, n.rbE, plan.e_c, zl)
    for k in range(1, GZ):
        reduce_z(psE, n.rbE, n.rzE, plan.e_c, plan.e_z, ffn_z0, GZ, (z - ffn_z0 + k) % GZ)
    drain(plan.ow_r, plan.ow_g, plan.in_r, plan.in_s, *[plan.ow_x + 4 * j for j in range(1, E)])

    def out_core():
        for k in range(GZ):
            reduce_core(psO, n.rbO, plan.o_c, (z - ffn_z0 + k) % GZ)

    def out_z():
        for k in range(1, GZ):
            zl = (z - ffn_z0 + k) % GZ
            reduce_z(psO, n.rbO, n.rzO, plan.o_c, plan.o_z, ffn_z0, GZ, zl)

    def out_take():
        total = n.H[...] + reduce_take(psO, n.rbO, n.rzO, plan.o_c, plan.o_z, ffn_z0, GZ)
        emit(n.s_out, n.o_out, total.astype(BF))

    def gin_rows(cols):
        Win[cols, :] = dot_tn(n3f[:, cols], DUP[...]).astype(BF)

    def gin_block():
        each(D, 256, gin_rows)

    def gin_start():
        gin_block()
        fold_start(in_half, n.rgi, plan.gi_r)

    def gin_pass():
        fold_pass(in_half, n.rgi, plan.gi_r)

    rgi2 = n.rgi2

    def gin_send():
        fold_take(in_half, n.rgi, plan.gi_r)
        for p in seq_peers:
            push(Win.at[rows_of(r * S + p, DB), :], rgi2.at[s], plan.gi_s, p, s, (r, p))
        rgi2[s] = Win[own_rows, :]

    go_half = rows_view(Wout, E * UB)[1]
    rgo2 = n.rgo2

    def gout_pass():
        fold_pass(go_half, n.rgo, plan.go_r)

    def gout_send():
        fold_take(go_half, n.rgo, plan.go_r)
        for j in range(1, E):
            src = Wout.at[rows_of(r * E + (grp + j) % E, UB), :]
            p = (s + j * G) % S
            push(src, rgo2.at[grp], plan.go_g, p, s, (r, p))

    def mat_grad(i, left, right):
        drain(plan.m_z + 4 * i, plan.m_r + 4 * i, plan.m_c + 2 * i)

        def mat_block():
            mats[i][...] = dot_tn(left, right).astype(BF).reshape(mats[i].shape)

        mat_block()
        push(mats[i].at[:, 1 - c], n.rmc.at[i], plan.h_c + 2 * i, 0, 0, (r, sib))

    def mat_grad_2():
        mat_grad(2, co[...], n.GR[...].astype(BF))

    def mat_grad_1():
        mat_grad(1, n.n2[...], n.dqo[...])

    def mat_grad_0():
        mat_grad(0, ao[...], n.GR[...].astype(BF))

    def mat_grad_r(i):
        arrive(n.rmc.at[i], plan.h_c + 2 * i, 0)
        mine = mats[i].at[:, c]
        mine[...] = (mine[...].astype(F32) + n.rmc[i].astype(F32)).astype(BF)
        fold_start(mat_view(i)[1], n.rmr.at[i], plan.h_r + 8 * i)

    def mat_grad_p(i):
        fold_pass(mat_view(i)[1], n.rmr.at[i], plan.h_r + 8 * i)

    def mat_at(i):
        def at(j):
            return mats[i].at[r * NZ + j, c]

        return at

    def mat_grad_z(i):
        fold_take(mat_view(i)[1], n.rmr.at[i], plan.h_r + 8 * i)
        for j in range(NZ):
            chain_send(mat_at(i)(j), n.rmz.at[i], plan.h_z + 8 * i, j)

    def mat_grad_f(i):
        chain_relay(mat_at(i), n.rmz.at[i], plan.h_z + 8 * i)

    def mat_grad_take(i, stage, out):
        emit(stage, out, chain_total(mat_at(i), n.rmz.at[i], plan.h_z + 8 * i))

    psT = AD.at[:T, :TW]
    DKV = n.DKV
    GC, GQ = n.GC, n.GQ

    def text_send():
        for j in range(NZ):
            chain_send(core_sum(psT, n.rbT, plan.t_c, j), n.rzT, plan.t_z, j)

    def text_relay():
        chain_relay(rows_at(psT), n.rzT, plan.t_z)

    def sum_relay():
        chain_relay(rows_at(ps0), n.rz0, plan.s_z)

    span = TW // 2

    def gkv_rows(i):
        got = dot_tn(n.textv[:, i * span : (i + 1) * span], DKV[...])
        both = [got[:, q * HP : (q + 1) * HP].reshape(span // half, half, HP) for q in range(2)]
        both = jnp.concatenate(both, axis=1).reshape(2 * span, HP)
        Wkv3[2 * i * span : 2 * (i + 1) * span, :] = both.astype(BF)

    def gkv_block():
        gkv_rows(0)
        gkv_rows(1)

    def gkv_start():
        drain(plan.kv_s, plan.kv_r)
        gkv_block()
        fold_start(kv_half, n.rgk, plan.gk_r)

    def gkv_pass():
        fold_pass(kv_half, n.rgk, plan.gk_r)

    def gkv_send():
        fold_take(kv_half, n.rgk, plan.gk_r)
        for p in seq_peers:
            src = Wkv3.at[rows_of(r * S + p, KB), :]
            push(src, GC.at[:, rows_of(s, HP)], plan.gk_s, p, s, (r, p))
        GC[:, rows_of(s, HP)] = Wkv3[kv_rows, :]

    def gq_rows(cols):
        got = dot_tn(n1f[:, cols], n.DQKV[...]).astype(BF)
        for i in range(3):
            Wq3[i, cols, :] = got[:, i * HP : (i + 1) * HP]

    def gq_block():
        each(D, 256, gq_rows)

    def gq_start():
        drain(plan.q_s, plan.q_r)
        gq_block()
        fold_start(q_half, n.rgq, plan.gq_r)

    def gq_pass():
        fold_pass(q_half, n.rgq, plan.gq_r)

    def gq_send():
        fold_take(q_half, n.rgq, plan.gq_r)
        for p in seq_peers:
            src = Wq3.at[:, rows_of(r * S + p, DB), :]
            push(src, GQ.at[:, :, rows_of(s, HP)], plan.gq_s, p, s, (r, p))
        GQ[:, :, rows_of(s, HP)] = Wq3[:, own_rows, :]

    gin_start()
    for k in range(GZ):
        rows = rows_of((z - ffn_z0 + k) % GZ, CH)

        def out_block_rows():
            psO[rows, :] = dot(ACT[rows, :], Wout[...]).astype(BF)

        out_block_rows()

    def gout_rows(cols):
        Wout[cols, :] = dot_tn(ACT[:, cols], ogf[...]).astype(BF)

    def gout_block():
        each(U, 256, gout_rows)

    gout_block()
    fold_start(go_half, n.rgo, plan.go_r)
    out_core()

    def norm_back(i, e):
        n.gg[i : i + 1, :] = jnp.sum(e * n.XH[i], axis=0, keepdims=True)
        n.gg[3 + i : 4 + i, :] = jnp.sum(e, axis=0, keepdims=True)
        y = e * gain(i)
        xhat = n.XH[i]
        a = jnp.mean(y, axis=1, keepdims=True)
        b = jnp.mean(y * xhat, axis=1, keepdims=True)
        return (y - a - xhat * b) * n.RS[i]

    e = reduce_take(psE, n.rbE, n.rzE, plan.e_c, plan.e_z, ffn_z0, GZ)
    g2 = ogf[rows_of(mem, TB), :].astype(F32) + norm_back(2, e)
    n.GR[...] = g2
    dco = n.wide
    drain(plan.a_cq)
    dco[...] = dot_nt(g2.astype(BF), mat(2)).astype(BF)
    DC = n.DC
    to_heads(dco, DC, plan.b_cr)
    mat_grad_2()

    def ones_rows(count):
        spot = lax.broadcasted_iota(jnp.int32, (count, HP), 1) % HD
        return jnp.where((spot >= 4) & (spot < 7), 1.0, 0.0)

    def prepare_cross_back(rows):
        CVA[0, rows, :], CVA[1, rows, :] = split_pair(CV[rows, :], ones_rows(CH))
        CKT[:, rows] = jnp.transpose(CK[rows, :].astype(F32)).astype(BF)

    def with_delta(grad, full):
        front = first_half(grad.shape)
        wide = grad.astype(F32)
        prod = wide * full
        d0 = jnp.sum(jnp.where(front, prod, 0.0), axis=1, keepdims=True)
        d1 = jnp.sum(jnp.where(front, 0.0, prod), axis=1, keepdims=True)
        zero = jnp.zeros_like(wide)
        return (
            with_norm(jnp.where(front, wide, zero), 0, d0),
            with_norm(jnp.where(front, zero, wide), 1, d1),
        )

    each(T, CH, prepare_cross_back)
    DCK, DCV, DQ, dqo = n.DCK, n.DCV, n.out, n.dqo
    drain(plan.a_cr)

    def heads_join(a, b, axis):
        spot = lax.broadcasted_iota(jnp.int32, a.shape, axis)
        return jnp.where(spot < HD, a, b)

    def cross_back_rows(k, rows):
        grad = DC[rows, :]
        ga = with_delta(grad, CF[rows, :])
        q2 = CQ[rows, :]
        dv, dk, dq = [], [], []
        for h in range(2):
            prob = jnp.exp(dot_nt(CKA[h], CQB[h, rows, :]))
            ds = (prob * dot_nt(CVA[h], ga[h])).astype(BF)
            dv.append(dot(prob.astype(BF), grad))
            dk.append(dot(ds, q2))
            dq.append(dot(CKT[...], ds))
        dvj, dkj = heads_join(dv[0], dv[1], 1), heads_join(dk[0], dk[1], 1)
        if k:
            DCV[...] += dvj
            DCK[...] += dkj
        else:
            DCV[...] = dvj
            DCK[...] = dkj
        DQ[rows, :] = (jnp.transpose(heads_join(dq[0], dq[1], 0)) * scale).astype(BF)

    def cross_back_part(k):
        rows = heads_take(DC, plan.b_cr, k)

        def cross_back_block():
            cross_back_rows(k, rows)

        cross_back_block()
        to_tokens(DQ, dqo, plan.b_cq, k)

    cross_back_part(0)
    gin_pass()
    out_z()
    cross_back_part(1)
    cross_back_part(2)
    mat_grad_r(2)
    cross_back_part(3)

    DKV[:, :HP] = DCK[...].astype(BF)
    DKV[:, HP:] = DCV[...].astype(BF)
    for j in range(NZ):
        rows = pl.ds(j * CH, CH)

        def text_back():
            psT[rows, :] = dot_nt(DKV[rows, :], Wkv[...]).astype(BF)

        text_back()
        reduce_core(psT, n.rbT, plan.t_c, j)
    text_send()

    for p in seq_peers:
        arrive(dqo.at[:, rows_of(p, HP)], plan.b_cq, p)
    e = dot_nt(dqo[...], mat(1))
    g1 = n.GR[...] + norm_back(1, e)
    n.GR[...] = g1
    dao = n.wide
    drain(plan.b_cr)
    dao[...] = dot_nt(g1.astype(BF), mat(0)).astype(BF)
    DA = n.DA
    to_heads(dao, DA, plan.b_at)
    gout_pass()
    gkv_start()
    gin_send()
    mat_grad_1()
    mat_grad_0()
    gout_send()

    VA, KT, DOA = CVA, CKT, CQB
    DQT, DQKV = n.DQT, n.DQKV

    def prepare_self_back(rows):
        VA[0, rows, :], VA[1, rows, :] = split_pair(V[rows, :], ones_rows(CH))
        KT[:, rows] = jnp.transpose(K[rows, :].astype(F32)).astype(BF)

    each(T, CH, prepare_self_back)
    for k in range(NZ):
        rows = heads_take(DA, plan.b_at, k)
        DOA[0, rows, :], DOA[1, rows, :] = with_delta(DA[rows, :], AF[rows, :])
    mat_grad_p(2)
    mat_grad_r(0)
    text_relay()
    out_take()
    drain(plan.e_c, plan.e_z, plan.o_c, plan.o_z)

    def self_back_rows(j, low, high):
        grad, q2 = DA[low:, :], Q[low:, :]
        dv, dk, dq = [], [], []
        for h in range(2):
            sc = dot_nt(KA[h, low:high, :], QB[h, low:, :])
            head = jnp.where(qpos <= kpos, sc[:, :CH], NEG)
            sc = jnp.concatenate([head, sc[:, CH:]], axis=1) if j < NZ - 1 else head
            prob = jnp.exp(sc)
            ds = (prob * dot_nt(VA[h, low:high, :], DOA[h, low:, :])).astype(BF)
            dv.append(dot(prob.astype(BF), grad))
            dk.append(dot(ds, q2))
            dq.append(dot(KT[:, low:high], ds))
        if j:
            DQT[:, low:] += heads_join(dq[0], dq[1], 0)
        else:
            DQT[...] = heads_join(dq[0], dq[1], 0)
        DQKV[low:high, :HP] = (jnp.transpose(DQT[:, low:high]) * scale).astype(BF)
        DQKV[low:high, HP : 2 * HP] = heads_join(dk[0], dk[1], 1).astype(BF)
        DQKV[low:high, 2 * HP :] = heads_join(dv[0], dv[1], 1).astype(BF)
        ps0[low:high, :] = dot_nt(DQKV[low:high, :], Wq[...]).astype(BF)

    def self_back_part(j):
        def self_back_block():
            self_back_rows(j, j * CH, (j + 1) * CH)

        self_back_block()
        reduce_core(ps0, n.rb0, plan.s_c, j)
        if j:
            chain_send(core_sum(ps0, n.rb0, plan.s_c, j - 1), n.rz0, plan.s_z, j - 1)

    self_back_part(0)
    self_back_part(1)
    gkv_pass()
    self_back_part(2)
    self_back_part(3)
    mat_grad_r(1)
    mat_grad_p(1)
    chain_send(core_sum(ps0, n.rb0, plan.s_c, NZ - 1), n.rz0, plan.s_z, NZ - 1)
    mat_grad_p(0)
    mat_grad_z(2)
    sum_relay()
    gq_start()
    mat_grad_z(0)
    mat_grad_f(2)
    mat_grad_z(1)

    e = chain_total(rows_at(ps0), n.rz0, plan.s_z)
    back = norm_back(0, e)
    gg, rgg, gg2, rgg2 = n.gg, n.rgg, n.gg2, n.rgg2
    GW = D // R
    for k, p in enumerate(row_peers, 1):
        push(gg.at[:, rows_of(p, GW)], rgg.at[R - 1 - k], plan.gg_r, p, r, (p, s))
    emit(n.s_ig, n.o_ig, n.GR[...] + back)
    mat_grad_f(0)
    mat_grad_f(1)
    gq_pass()
    total = Wout[out_rows, :].astype(F32)
    for j in range(1, E):
        g2i = (grp + j) % E
        arrive(rgo2.at[g2i], plan.go_g, (s + j * G) % S)
        total = total + rgo2[g2i].astype(F32)
    emit(n.s_ow, n.o_ow, total)
    for p in seq_peers:
        arrive(rgi2.at[p], plan.gi_s, p)
    for m in range(G):
        total = rgi2[m].astype(F32)
        for g in range(1, E):
            total = total + rgi2[g * G + m].astype(F32)
        for rr in range(R):
            for j in range(E):
                b = rr * S + j * G + m
                at = (rr * E + j) * UB
                n.s_in[:, b * UB : (b + 1) * UB] = total[:, at : at + UB]
    finals.append(local(n.s_in, n.o_in, 16 + len(finals)))
    total = gg[:, rows_of(r, GW)]
    for k, p in enumerate(row_peers):
        arrive(rgg.at[k], plan.gg_r, p)
        total = total + rgg[k]
    gg2[...] = total
    for p in seq_peers:
        push(gg2.at[:, rows_of(p // per, 128)], rgg2.at[s], plan.gg_s, p, s, (r, p))
    gkv_send()
    gq_send()
    mat_grad_take(2, n.s_co, n.o_co)
    mat_grad_take(1, n.s_cq, n.o_cq)
    mat_grad_take(0, n.s_so, n.o_so)
    emit(n.s_tg, n.o_tg, chain_total(rows_at(psT), n.rzT, plan.t_z))
    for p in seq_peers:
        arrive(GC.at[:, rows_of(p, HP)], plan.gk_s, p)
    emit(n.s_ckv, n.o_ckv, GC[...].astype(F32))
    total = gg2[:, rows_of(s // per, 128)]
    for p in seq_peers:
        arrive(rgg2.at[p], plan.gg_s, p)
        total = total + rgg2[p]
    emit(n.s_gb, n.o_gb, total)
    for p in seq_peers:
        arrive(GQ.at[:, :, rows_of(p, HP)], plan.gq_s, p)
    emit(n.s_qkv, n.o_qkv, GQ[...].astype(F32))
    drain(*list(pending))
    for cp in finals:
        cp.wait()


def copy_kernel(count, *refs):
    stages, into, out_of = refs[2 * count : 3 * count], refs[3 * count], refs[3 * count + 1]
    loads = [pltpu.make_async_copy(refs[i], stages[i], into.at[i]) for i in range(count)]
    stores = [
        pltpu.make_async_copy(stages[i], refs[count + i], out_of.at[i]) for i in range(count)
    ]
    for cp in loads:
        cp.start()
    for load, store in zip(loads, stores):
        load.wait()
        store.start()
    for cp in stores:
        cp.wait()


def settle(arrays):
    anywhere = pl.BlockSpec(memory_space=pl.ANY)
    return pl.pallas_call(
        functools.partial(copy_kernel, len(arrays)),
        out_shape=[jax.ShapeDtypeStruct(a.shape, a.dtype) for a in arrays],
        in_specs=[anywhere] * len(arrays),
        out_specs=[anywhere] * len(arrays),
        scratch_shapes=[pltpu.VMEM(a.shape, a.dtype) for a in arrays]
        + [pltpu.SemaphoreType.DMA((len(arrays),))] * 2,
    )(*arrays)


def fused_shards(
    hidden_in, clip_lengths, text_lengths, text_states, norm_gain, norm_bias, self_qkv,
    self_out, cross_query, cross_kv, cross_out, ffn_in, ffn_out, out_grad,
):
    R, S = lax.axis_size("rows"), lax.axis_size("seq")
    TB, D = hidden_in.shape[1:]
    TW = text_states.shape[2]
    T, HP, DB = TB * S, D // S, D // (R * S)
    FF = ffn_in.shape[1]
    G = GROUP
    E, U, UB, NT, NZ = S // G, FF // G, FF // (R * S), G * TB, S // 2
    GZ = G // 2
    KB = 2 * cross_kv.shape[1]
    index = lax.axis_index("rows") * S + lax.axis_index("seq")
    per = 128 // DB
    both = jnp.concatenate([norm_gain, norm_bias], axis=0)
    both = jnp.pad(both, ((0, 10), (0, 0)))
    spot = jnp.arange(128, dtype=jnp.int32)[None, :] // DB
    gb = jnp.where(spot == index % per, jnp.tile(both, (1, per)), jnp.zeros((), both.dtype))
    ins = dict(
        cl=clip_lengths, tl=text_lengths, x=hidden_in.reshape(TB, D), og=out_grad.reshape(TB, D),
        text=text_states.reshape(T, TW), gb=gb, wqkv=self_qkv, wo=self_out, wcq=cross_query,
        wco=cross_out, wckv=cross_kv.reshape(KB, D), win=ffn_in, wout=ffn_out,
    )
    outs = dict(
        o_out=((TB, D), BF), o_ig=((TB, D), F32), o_tg=((TB, TW), F32), o_gb=((8, 128), F32),
        o_qkv=(self_qkv.shape, F32), o_so=(self_out.shape, F32), o_cq=(cross_query.shape, F32),
        o_ckv=((KB, D), F32), o_co=(cross_out.shape, F32), o_in=(ffn_in.shape, F32),
        o_ow=(ffn_out.shape, F32),
    )
    plan, count = semaphore_plan(GZ)
    hp = (T, HP)
    pair = (2, T, HP)
    scratch = dict(
        textv=((T, TW), BF),
        gbt=((R, S, 16, 128), BF), gbf=((16, D), F32), Wq3=((3, D, HP), BF), Wq=((D, 3 * HP), BF),
        Wkv3=((R * S * KB, HP), BF), Wkv=((TW, 2 * HP), BF),
        Wm0=((R * NZ, 2, DB, D), BF), Wm1=((R * NZ, 2, DB, D), BF), Wm2=((R * NZ, 2, DB, D), BF),
        Win=((D, U), BF), Wout=((U, D), BF), winp=((DB, FF), BF),
        XH=((3, TB, D), F32), RS=((3, TB, 1), F32), H=((TB, D), F32), GR=((TB, D), F32),
        n1f=((T, D), BF), n3f=((NT, D), BF), ogf=((NT, D), BF), n2=((TB, D), BF),
        oh=(hp, BF), kbs=(hp, BF), kbc=(hp, BF),
        Q=(hp, BF), K=(hp, BF), V=(hp, BF), CK=(hp, BF), CV=(hp, BF), CQ=(hp, BF),
        KA=(pair, BF), QB=(pair, BF),
        CKA=(pair, BF), CVA=(pair, BF), CQB=(pair, BF), CKT=((HP, T), BF),
        AF=(hp, F32), CF=(hp, F32), out=(hp, BF), DC=(hp, BF), DA=(hp, BF),
        ao=((TB, D), BF), wide=((TB, D), BF), co=((TB, D), BF), dqo=((TB, D), BF),
        DCK=(hp, F32), DCV=(hp, F32), DKV=((T, 2 * HP), BF),
        DQT=((HP, T), F32), DQKV=((T, 3 * HP), BF),
        AD=((2 * NT, U), BF),
        ps0=((max(T, 2 * NT), D), BF),
        rbE=((GZ, TB, D), BF), rzE=((GZ - 1, TB, D), BF), rbO=((GZ, TB, D), BF), rzO=((GZ - 1, TB, D), BF),
        rbT=((NZ, TB, TW), BF), rzT=((NZ, TB, TW), BF), rb0=((NZ, TB, D), BF), rz0=((NZ, TB, D), BF),
        rgo=((6, E * UB // 2, D), BF), rgo2=((E, UB, D), BF), rgi=((6, S * DB // 2, U), BF), rgi2=((S, DB, U), BF),
        rgk=((6, S * KB // 2, HP), BF), GC=((KB, D), BF), rgq=((6, 3, S * DB // 2, HP), BF), GQ=((3, DB, D), BF),
        gg=((8, D), F32), rgg=((R - 1, 8, D // R), F32), gg2=((8, D // R), F32), rgg2=((S, 8, 128), F32),
        rmc=((3, R * NZ, DB, D), BF), rmr=((3, 6, NZ // 2, DB, D), BF), rmz=((3, NZ, DB, D), BF),
    )
    for name, spec in outs.items():
        scratch[name.replace("o_", "s_")] = spec
    names = list(ins) + list(outs) + list(scratch) + ["ss", "rs", "ls"]
    anywhere = pl.BlockSpec(memory_space=pl.ANY)
    smem = pl.BlockSpec(memory_space=pltpu.SMEM)
    got = pl.pallas_call(
        functools.partial(layer_kernel, plan, names),
        out_shape=[jax.ShapeDtypeStruct(*v) for v in outs.values()],
        in_specs=[smem, smem] + [anywhere] * (len(ins) - 2),
        out_specs=[anywhere] * len(outs),
        scratch_shapes=[pltpu.VMEM(*v) for v in scratch.values()]
        + [pltpu.SemaphoreType.DMA((k,)) for k in (count, count, 32)],
        compiler_params=pltpu.CompilerParams(
            collective_id=0, has_side_effects=True, vmem_limit_bytes=63 << 20
        ),
    )(*ins.values())
    got = list(got)
    got = list(settle(got[:3] + got[4:])) + [got[3]]
    o = types.SimpleNamespace(**dict(zip([k for k in outs if k != "o_gb"] + ["o_gb"], got)))
    mine = lax.dynamic_slice(o.o_gb, (0, (index % per) * DB), (8, DB))
    return (
        o.o_out.reshape(hidden_in.shape), o.o_ig.reshape(hidden_in.shape),
        o.o_tg.reshape(1, TB, TW), mine[:3], mine[3:6], o.o_qkv, o.o_so, o.o_cq,
        o.o_ckv.reshape(cross_kv.shape), o.o_co, o.o_in, o.o_ow,
    )


def fits(mesh):
    return dict(mesh.shape) == {"rows": 4, "seq": 8}


def solution(mesh):
    placed = (
        P("rows", "seq", None),
        P("rows", None),
        P("rows", None),
        P("rows", None, None),
        P(None, ("rows", "seq")),
        P(None, ("rows", "seq")),
        P(None, ("rows", "seq"), None),
        P(("rows", "seq"), None),
        P(("rows", "seq"), None),
        P(None, ("rows", "seq"), None),
        P(("rows", "seq"), None),
        P(("rows", "seq"), None),
        P(("rows", "seq"), None),
        P("rows", "seq", None),
    )
    return jax.shard_map(
        fused_shards if fits(mesh) else shards,
        mesh=mesh,
        in_specs=placed,
        out_specs=(
            P("rows", "seq", None),
            P("rows", "seq", None),
            P("rows", "seq", None),
            P(None, ("rows", "seq")),
            P(None, ("rows", "seq")),
            P(None, ("rows", "seq"), None),
            P(("rows", "seq"), None),
            P(("rows", "seq"), None),
            P(None, ("rows", "seq"), None),
            P(("rows", "seq"), None),
            P(("rows", "seq"), None),
            P(("rows", "seq"), None),
        ),
        check_vma=False,
    )
```
